256 devices in a mesh: wide: 32 (over x, z), pencil: 8 (over y, core).
Axes of the slice: x: 4, y: 4, z: 8, core: 2. Of those that a mesh axis runs over, the one named last changes fastest.
Arguments:
- force_adjoint: float32 [3, 8, 524288], P(None, 'pencil', 'wide'), may hold values from -4 to 4
- paint_index: int32 [8, 524288], P('pencil', 'wide'), may hold values from 0 to 511
- block_count: int32 [8, 1024], P('pencil', 'wide'), may hold values from 1 to 512, 314572 in all within a row
- block_owner: int32 [8, 1024, 1], P('pencil', 'wide'), may hold values from 0 to 31; in each aligned block of 32 rows (0 to 31, 32 to 63, ..., all dimensions but the last counted through in order) at most 2 rows name the same one
- block_tile: int32 [8, 1024], P('pencil', 'wide'), may hold values from 0 to 127
Outputs:
- mesh_grad: float32 [256, 256, 256], P('wide', 'pencil')
- mass_grad: float32 [8, 524288], P('pencil', 'wide')
The draws below stay inside these ranges and needn't reach their ends.
Inputs may be any that keep to these rules, and one draw needn't show every extreme that they name: `block_owner`: no device sends more than 2 of its blocks to one owner, and some device sends exactly 2. `block_count`: the live particles of a block are its first slots.
All inputs are finite; a program needn't handle non-finite values.
Results may differ from the reference program's by a relative error of at most 0.00011.
Values sent between devices are 32-bit elements; how exact they have to be, the bound alone decides.
A program may use at most 64 MiB of HBM per device.

```python
import math
import jax
import jax.numpy as jnp
import numpy as np

NG = 256
TE = 8
BP = 512
NB = 32
CAP = 2
BLOCKS = 1024
SLOTS = 524288
TILES = 128
N_WIDE = 32
N_PENCIL = 8


def set_ends(values, own_key, least, top_value):
    longest = values.shape.index(max(values.shape))
    spots = []
    for shift in (0, 1):
        where = [jax.random.randint(jax.random.fold_in(own_key, axis), (), 0, length) for axis, length in enumerate(values.shape)]
        where[longest] = (where[longest] + shift) % values.shape[longest]
        spots.append(tuple(where))
    return values.at[spots[0]].set(least).at[spots[1]].set(top_value)


def block_levels(key, shape, shards, least, top_value):
    def one(dim, blocks):
        steps = jax.random.uniform(jax.random.fold_in(jax.random.fold_in(key, 6), dim), (blocks,), jnp.float32, least / len(shards), top_value / len(shards))
        return jnp.repeat(jnp.exp(steps), shape[dim] // blocks).reshape((-1,) + (1,) * (len(shape) - dim - 1))

    gain = one(*shards[0])
    for cut in shards[1:]:
        gain = gain * one(*cut)
    return gain


def length_profile(amount, total, limit, skew):
    weights = [(1 << 20) // math.isqrt(rank ** skew) + 1 for rank in range(2, amount + 1)]
    spare, holding = total - limit - (amount - 1), [1] * (amount - 1)
    while spare > 0:
        candidates = [i for i in range(amount - 1) if holding[i] < limit]
        mass, remaining = sum([weights[i] for i in candidates]), spare
        for i in candidates:
            more = min(limit - holding[i], max(1, remaining * weights[i] // mass), spare)
            holding[i] = holding[i] + more
            spare = spare - more
    return np.array([limit] + holding)


def uneven_parts(rng, number_of, total, most, lean):
    if number_of == 2:
        one = jax.random.randint(rng, (), max(1, total - most), min(most, total - 1) + 1)
        return jnp.stack([one, total - one])
    sizes = jnp.asarray(length_profile(number_of, total, most, lean), jnp.int32)
    couples = (number_of - 1) // 2
    giver, taker = sizes[1:1 + 2 * couples:2], sizes[2:2 + 2 * couples:2]
    margin = jnp.minimum(giver - 1, most - taker)
    shifted = jax.random.randint(jax.random.fold_in(rng, 1), (couples,), 0, 1 << 20) % (margin + 1)
    sizes = sizes.at[1:1 + 2 * couples:2].set(giver - shifted).at[2:2 + 2 * couples:2].set(taker + shifted)
    return sizes[jax.random.permutation(jax.random.fold_in(rng, 2), number_of)]


def routed_block(rng, own, number, rows, number_of, top, most, skew):
    sequence = jax.random.permutation(rng, number_of)
    packed, ordinary = load_shares(number_of, rows * top, most, skew, True), load_shares(number_of, rows * top, most, skew, False)
    places = jnp.arange(number_of)

    def named(tallies, rotation):
        used = int((tallies > 0).sum())
        fixed = max(1, used // 4)
        shifted = fixed + (places - fixed + rotation * (used - fixed)) % max(1, number_of - fixed)
        return jnp.zeros((number_of,), jnp.int32).at[sequence[jnp.where(places < fixed, places, shifted)]].set(jnp.asarray(tallies, jnp.int32))

    tallies = jnp.where(number % 4 == 0, named(packed, number // 4), named(ordinary, number - number // 4 - 1))
    mixed = jax.random.permutation(jax.random.fold_in(own, 3), number_of)
    giver, receiver = mixed[0:number_of // 2 * 2:2], mixed[1:number_of // 2 * 2:2]
    margin = jnp.minimum(tallies[giver] - 1, most - tallies[receiver]) // 2
    margin = jnp.where((giver == sequence[0]) | (receiver == sequence[0]) | (tallies[receiver] == 0), 0, jnp.maximum(margin, 0))
    shifted = jax.random.randint(jax.random.fold_in(own, 4), (number_of // 2,), 0, 1 << 20) % (margin + 1)
    tallies = tallies.at[giver].add(-shifted).at[receiver].add(shifted)
    items = jnp.searchsorted(jnp.cumsum(tallies), jnp.arange(rows * top), side="right").astype(jnp.int32)
    table = items.reshape(top, rows).T
    table = table[jax.random.permutation(jax.random.fold_in(own, 1), rows)]
    rotation = jax.random.randint(jax.random.fold_in(own, 2), (rows, 1), 0, top)
    return jnp.take_along_axis(table, (jnp.arange(top)[None, :] + rotation) % top, axis=1)


def load_shares(amount, total, reach, skew, full):
    loads = [(1 << 20) // math.isqrt(standing ** skew) + 1 for standing in range(1, amount + 1)]
    largest = reach if full else min(reach, max(-(-total // amount), total * loads[0] // sum(loads)))
    least = 1 if total - largest >= amount - 1 else 0
    holding, spare = [largest] + [least] * (amount - 1), total - largest - least * (amount - 1)
    while spare > 0:
        movable = [i for i in range(1, amount) if holding[i] < largest] or [i for i in range(1, amount) if holding[i] < reach]
        whole, budget = sum([loads[i] for i in movable]), spare
        for i in movable:
            more = min(reach - holding[i], max(1, budget * loads[i] // whole), spare)
            holding[i] = holding[i] + more
            spare = spare - more
    return np.array(holding)


def scatter_about(own_key, dims, deviation, limit, shards=(), kind=jnp.bfloat16):
    loudness = block_levels(own_key, dims, shards, -0.22, 0.18) if shards else 1.0
    entries = jax.random.normal(own_key, dims, jnp.float32) * deviation * loudness
    return jnp.minimum(jnp.maximum(entries, -limit), limit).astype(kind)


def setup_inputs(seed: int = 0) -> dict:
    streams_of = jax.random.split(jax.random.key(seed), 6)
    force_adjoint = scatter_about(streams_of[0], (3, N_PENCIL, SLOTS), 0.5, 4.0, ((1, 8), (2, 32)), jnp.float32)
    paint_index = set_ends(jax.random.randint(streams_of[1], (N_PENCIL, SLOTS), 0, TE**3), jax.random.fold_in(streams_of[1], 1), 0, (TE**3) - 1).astype(jnp.int32)
    block_count = jax.vmap(lambda own: uneven_parts(own, BLOCKS, BLOCKS * BP * 3 // 5, BP, 1))(jax.random.split(streams_of[2], N_PENCIL)).reshape((N_PENCIL, BLOCKS)).astype(jnp.int32)
    block_owner_keys = jax.random.split(jax.random.fold_in(streams_of[3], 1), N_PENCIL * BLOCKS // NB)
    block_owner_turns = jax.random.permutation(jax.random.fold_in(streams_of[3], 3), N_PENCIL * BLOCKS // NB)
    block_owner = jax.vmap(lambda own, number: routed_block(jax.random.fold_in(streams_of[3], 2), own, number, NB, N_WIDE, 1, CAP, 2))(block_owner_keys, block_owner_turns).reshape((N_PENCIL, BLOCKS, 1))
    block_tile = set_ends(jax.random.randint(streams_of[4], (N_PENCIL, BLOCKS), 0, TILES), jax.random.fold_in(streams_of[4], 1), 0, TILES - 1).astype(jnp.int32)
    return {"force_adjoint": force_adjoint, "paint_index": paint_index, "block_count": block_count, "block_owner": block_owner, "block_tile": block_tile}


def reference(force_adjoint, paint_index, block_count, block_owner, block_tile):
    span_x = NG // N_WIDE
    span_y = NG // N_PENCIL
    tiles_y = span_y // TE
    tiles_z = NG // TE
    live_slot = (jnp.arange(BP, dtype=jnp.int32)[None, None, :] < block_count[:, :, None]).astype(jnp.float32)
    amounts = force_adjoint.reshape(3, N_PENCIL, BLOCKS, BP) * live_slot[None]
    cell_index = paint_index.reshape(N_PENCIL, BLOCKS, BP)
    owner_rank = block_owner[:, :, 0]
    tile_x = block_tile // (tiles_y * tiles_z)
    tile_y = (block_tile // tiles_z) % tiles_y
    tile_z = block_tile % tiles_z
    pencil_row = jnp.arange(N_PENCIL, dtype=jnp.int32)[:, None]
    corner_x = owner_rank * span_x + tile_x * TE
    corner_y = pencil_row * span_y + tile_y * TE
    corner_z = tile_z * TE
    global_x = corner_x[:, :, None] + cell_index // (TE * TE)
    global_y = corner_y[:, :, None] + (cell_index // TE) % TE
    global_z = corner_z[:, :, None] + cell_index % TE
    flat_cell = ((global_x * NG + global_y) * NG + global_z).reshape(-1).astype(jnp.int32)
    painted = jnp.stack([jax.ops.segment_sum(amounts[component].reshape(-1), flat_cell, num_segments=NG ** 3) for component in range(3)])
    spectrum = jnp.fft.fftn(painted.reshape(3, NG, NG, NG), axes=(1, 2, 3))
    positions = jnp.arange(NG, dtype=jnp.int32)
    signed = jnp.where(positions < NG // 2, positions, positions - NG).astype(jnp.float32)
    slopes = jnp.where(positions == NG // 2, jnp.float32(0.0), signed)
    squared = signed[:, None, None] ** 2 + signed[None, :, None] ** 2 + signed[None, None, :] ** 2
    combined = slopes[:, None, None] * spectrum[0] + slopes[None, :, None] * spectrum[1] + slopes[None, None, :] * spectrum[2]
    factor = NG / jnp.maximum(squared, 1.0)
    mesh_grad = jnp.real(jnp.fft.ifftn(1j * factor * combined)).astype(jnp.float32)
    picked = mesh_grad.reshape(-1)[flat_cell].reshape(N_PENCIL, BLOCKS, BP) * live_slot
    mass_grad = picked.reshape(N_PENCIL, BLOCKS * BP)
    return (mesh_grad, mass_grad)
```

```python
import functools
import math

import jax
import jax.numpy as jnp
import ml_dtypes
import numpy as np
from jax import lax
from jax.experimental import pallas as pl
from jax.experimental.pallas import tpu as pltpu
from jax.sharding import PartitionSpec as P

NG = 256
NW = 32
NP = 8
NB = 32
BP = 512
MESH = pl.DeviceIdType.MESH
f32 = jnp.float32
bf16 = jnp.bfloat16


def roll(x, shift, axis):
    return pltpu.roll(x, shift, axis)


def halves(table):
    table = np.asarray(table, np.float32)
    high = table.astype(ml_dtypes.bfloat16)
    low = (table - high.astype(np.float32)).astype(ml_dtypes.bfloat16)
    return np.stack([high, low])


def waves(first, second):
    phase = (np.asarray(first)[:, None] * np.asarray(second)[None, :]) % NG
    angle = phase * (2.0 * math.pi / NG)
    return np.cos(angle), np.sin(angle)


def ky_of_row():
    out = []
    for w in range(NW):
        for j in range(8):
            base = 4 * w + j % 4
            out.append(base if j < 4 else (128 if base == 0 else NG - base))
    return np.array(out)


def make_tables():
    line = np.arange(NG)
    half = np.arange(NG // 2)
    sign = np.where(line % 2 == 0, 1.0, -1.0)
    c, s = waves(line, half)
    s = -s
    s[:, 0] = sign
    z_fwd = np.concatenate([c, s], axis=1)
    c, s = waves(half, line)
    weight = np.where(half == 0, 1.0, 2.0)[:, None]
    c = c * weight
    s = -2.0 * s
    s[0] = sign
    z_inv = np.concatenate([c, s], axis=0)
    ky = ky_of_row()
    c, s = waves(ky, line)
    y_fwd = np.concatenate([c, s], axis=0)
    kyt = ky.reshape(NW, 8).T.reshape(-1)
    c, s = waves(line, kyt)
    y_inv = np.concatenate([c, s], axis=0)
    xt = line.reshape(NW, 8).T.reshape(-1)
    c, s = waves(line, xt)
    x_fwd = np.concatenate([c, s], axis=0)
    c, s = waves(line, line)
    x_inv = np.concatenate([c, s], axis=0)
    return dict(
        z_fwd=halves(z_fwd),
        z_inv=halves(z_inv),
        z_inv_t=halves(z_inv.T),
        y_fwd=halves(y_fwd),
        y_inv=halves(y_inv),
        x_fwd=halves(x_fwd),
        x_inv=halves(x_inv),
    )


def dot(a, b, dims=((1,), (0,))):
    return lax.dot_general(a, b, (dims, ((), ())), preferred_element_type=f32)


def split(x):
    high = x.astype(bf16)
    return high, (x - high.astype(f32)).astype(bf16)


def dot3(a, b, dims=((1,), (0,))):
    return dot(a[0], b[0], dims) + (dot(a[0], b[1], dims) + dot(a[1], b[0], dims))


def iota(shape, axis):
    return lax.broadcasted_iota(jnp.int32, shape, axis)


def exchange(arrays):
    chunk = iota(arrays[0].shape, 1) // 16
    for b in range(3):
        bit = (chunk >> b) & 1
        new = []
        for i in range(8):
            mine = (i >> b) & 1
            shift = 16 << b if mine == 0 else 128 - (16 << b)
            new.append(jnp.where(bit == mine, arrays[i], roll(arrays[i ^ (1 << b)], shift, 1)))
        arrays = new
    return arrays


def one_hot_rows(ids):
    spot = (ids & 31) * 8 + iota((NW, 8, 128), 1)
    spot = spot.reshape(NW * 8, 128)
    lane = iota((NW * 8, 128), 1)
    both = jnp.concatenate(
        [jnp.where(spot == lane, 1.0, 0.0), jnp.where(spot == lane + 128, 1.0, 0.0)], axis=1
    )
    return both.astype(bf16)


def tile_y(ids):
    return jnp.broadcast_to(ids >> 5, (NW, 8, 128)).reshape(NW * 8, 128)


def scatter_rows(field, ty0, ty1):
    upper = (iota((NW * 8, 128), 1) >= 64).astype(jnp.int32)
    turned = roll(field, 64, 1)
    first = jnp.where(upper == 0, field, turned)
    second = jnp.where(upper == 0, turned, field)
    rows = []
    for values, ty in ((first, ty0), (second, ty1)):
        rows.append(
            jnp.concatenate(
                [jnp.where(ty == upper, values, 0.0), jnp.where(ty == upper + 2, values, 0.0)],
                axis=1,
            )
        )
    return jnp.concatenate(rows, axis=0)


def pick_rows(v0, v1, ty0, ty1):
    lower = iota((NW * 8, 128), 1) < 64
    out = []
    for v, ty in ((v0, ty0), (v1, ty1)):
        half = jnp.where(ty >= 2, v[:, 128:], v[:, :128])
        out.append((half, roll(half, 64, 1)))
    first = jnp.where((ty0 & 1) == 1, out[0][1], out[0][0])
    second = jnp.where((ty1 & 1) == 1, out[1][0], out[1][1])
    return jnp.where(lower, first, second)


def y_slopes():
    row = iota((NG, 128), 0)
    base = (row >> 3) * 4 + (row & 3)
    return jnp.where((row & 4) == 0, base, -base).astype(f32)


def y_forward(table, real, imag):
    out = dot3(table, split(jnp.concatenate([real, imag], axis=1)))
    return out[:NG, :128] + out[NG:, 128:], out[:NG, 128:] - out[NG:, :128]


def back(table, real, imag):
    out = dot3(table, split(jnp.concatenate([real, imag], axis=1)))
    return out[:NG, :128] - out[NG:, 128:], out[:NG, 128:] + out[NG:, :128]


def solve_x(x_fwd, x_inv, first, second, w, p):
    a = dot3(x_fwd, split(first))
    b = dot3(x_fwd, split(second))
    cra, cia, sra, sia = a[:NG, :128], a[:NG, 128:], a[NG:, :128], a[NG:, 128:]
    crb, cib, srb, sib = b[:NG, :128], b[:NG, 128:], b[NG:, :128], b[NG:, 128:]
    row = iota((NG, 128), 0)
    lane = iota((NG, 128), 1)
    signed = jnp.where(row < 128, row, row - NG)
    slope = jnp.where(row == 128, 0, signed).astype(f32)
    p_re = slope * (cra + sia) + (crb + sib)
    p_im = slope * (cia - sra) + (cib - srb)
    q_re = (crb - sib) - slope * (cra - sia)
    q_im = slope * (cia + sra) - (cib + srb)
    alone = (w == 0) & ((lane & 63) < 16)
    r_re = jnp.where(alone, q_re, roll(q_re, 64, 1))
    r_im = jnp.where(alone, q_im, roll(q_im, 64, 1))
    j = lane >> 4
    base = 4 * w + (j & 3)
    ny = jnp.where((base == 0) & (j == 4), 128, base)
    kz = lane & 15
    nz = 16 * p + kz
    flat = signed * signed + ny * ny
    factor = (1.0 / NG**2) / jnp.maximum(flat + nz * nz, 1).astype(f32)
    top = (1.0 / NG**2) / (flat + (NG // 2) ** 2).astype(f32)
    shared = (nz == 0)
    alpha = jnp.where(shared, 0.5 * (factor + top), factor)
    beta = jnp.where(shared, 0.5 * (top - factor), 0.0)
    h_re = -(alpha * p_im + beta * r_im)
    h_im = alpha * p_re + beta * r_re
    return back(x_inv, h_re, h_im)


def block_key(cells_ref, b, slot):
    cells = cells_ref[0:1, pl.ds(pl.multiple_of(b * BP, BP), BP)]
    key = (cells >> 3) + 64 * slot
    spread = jnp.where(iota((128, BP), 0) == key, 1.0, 0.0).astype(bf16)
    return spread, cells & 7


def paint_kernel(count_ref, owner_ref, tile_ref, force_ref, cells_ref, msg_ref, ids_ref, seen):
    msg_ref[...] = jnp.zeros_like(msg_ref)
    ids_ref[...] = jnp.full(ids_ref.shape, -1, jnp.int32)
    for o in range(NW):
        seen[o] = 0

    def body(b, carry):
        owner = owner_ref[0, b]
        slot = seen[owner]
        seen[owner] = slot + 1
        ids_ref[owner, slot] = jnp.full((1, 128), tile_ref[0, b], jnp.int32)
        spread, cz = block_key(cells_ref, b, slot)
        live = iota((1, BP), 1) < count_ref[0, b]
        keep = (iota((8, BP), 0) == cz) & live
        high, low = [], []
        for f in range(3):
            amount = force_ref[f, 0:1, pl.ds(pl.multiple_of(b * BP, BP), BP)]
            top = amount.astype(bf16).astype(f32)
            high.append(jnp.where(keep, top, 0.0))
            low.append(jnp.where(keep, amount - top, 0.0))
        left = jnp.concatenate(high + low, axis=0).astype(bf16)
        out = dot(left, spread, ((1,), (1,)))
        msg_ref[owner] += (out[:24] + out[24:]).reshape(3, 8, 128)
        return carry

    lax.fori_loop(0, NB, body, 0, unroll=4)


def read_kernel(count_ref, owner_ref, cells_ref, ret_ref, mass_ref, seen):
    for o in range(NW):
        seen[o] = 0

    def body(b, carry):
        owner = owner_ref[0, b]
        slot = seen[owner]
        seen[owner] = slot + 1
        spread, cz = block_key(cells_ref, b, slot)
        live = iota((1, BP), 1) < count_ref[0, b]
        keep = (iota((8, BP), 0) == cz) & live
        tile = ret_ref[pl.ds(pl.multiple_of(owner * 8, 8), 8), :]
        top = tile.astype(bf16).astype(f32)
        left = jnp.concatenate([top, tile - top], axis=0).astype(bf16)
        out = dot(left, spread)
        value = jnp.sum(jnp.where(keep, out[:8] + out[8:], 0.0), axis=0, keepdims=True)
        mass_ref[0:1, pl.ds(pl.multiple_of(b * BP, BP), BP)] = value
        return carry

    lax.fori_loop(0, NB, body, 0, unroll=4)


def mesh_kernel(
    msg_ref, ids_ref, z_fwd, z_inv, z_inv_t, y_fwd, y_inv, x_fwd, x_inv,
    mesh_ref, ret_ref,
    ids_rx, msg_rx, snd2, rx2, snd3, rx3, snd4, rx4, snd5, rx5, snd6,
    wsend, wrecv, psend, precv, lsem,
):
    w = lax.axis_index("wide")
    p = lax.axis_index("pencil")

    barrier = pltpu.get_barrier_semaphore()

    def greet_wide(d, carry):
        pl.semaphore_signal(barrier, inc=1, device_id={"wide": (w + d) % NW}, device_id_type=MESH)
        return carry

    def greet_pencil(d, carry):
        pl.semaphore_signal(barrier, inc=1, device_id={"pencil": (p + d) % NP}, device_id_type=MESH)
        return carry

    lax.fori_loop(1, NW, greet_wide, 0)
    lax.fori_loop(1, NP, greet_pencil, 0)
    pl.semaphore_wait(barrier, NW - 1 + NP - 1)

    def wide_copy(phase, src, dst, other):
        return pltpu.make_async_remote_copy(
            src_ref=src, dst_ref=dst, send_sem=wsend.at[phase, other], recv_sem=wrecv.at[phase, w],
            device_id={"wide": other}, device_id_type=MESH,
        )

    def wide_send(phase, src, dst):
        def step(d, carry):
            other = (w + d) % NW
            wide_copy(phase, src(other), dst(w), other).start()
            return carry

        lax.fori_loop(1, NW, step, 0)

    def wide_wait(phase, src, dst):
        def step(d, carry):
            other = (w + d) % NW
            pltpu.make_async_remote_copy(
                src_ref=src(other), dst_ref=dst(other), send_sem=wsend.at[phase, other],
                recv_sem=wrecv.at[phase, other], device_id={"wide": other}, device_id_type=MESH,
            ).wait()
            return carry

        lax.fori_loop(1, NW, step, 0)

    def pencil_send(phase, src, dst):
        def step(d, carry):
            other = (p + d) % NP
            pltpu.make_async_remote_copy(
                src_ref=src(other), dst_ref=dst(p), send_sem=psend.at[phase, other],
                recv_sem=precv.at[phase, p], device_id={"pencil": other}, device_id_type=MESH,
            ).start()
            return carry

        lax.fori_loop(1, NP, step, 0)

    def pencil_wait(phase, src, dst):
        def step(d, carry):
            other = (p + d) % NP
            pltpu.make_async_remote_copy(
                src_ref=src(other), dst_ref=dst(other), send_sem=psend.at[phase, other],
                recv_sem=precv.at[phase, other], device_id={"pencil": other}, device_id_type=MESH,
            ).wait()
            return carry

        lax.fori_loop(1, NP, step, 0)

    def keep_own(src, dst):
        copy = pltpu.make_async_copy(src, dst, lsem)
        copy.start()
        copy.wait()

    def rows8(ref, i):
        return ref.at[:, pl.ds(pl.multiple_of(i * 8, 8), 8), :]

    def rows32(ref, i):
        return ref.at[:, pl.ds(pl.multiple_of(i * 32, 32), 32), :]

    id_src, id_dst = (lambda i: ids_ref.at[i]), (lambda i: ids_rx.at[i])
    msg_src, msg_dst = (lambda i: msg_ref.at[i]), (lambda i: msg_rx.at[i])
    wide_send(0, id_src, id_dst)
    wide_send(1, msg_src, msg_dst)
    keep_own(ids_ref.at[w], ids_rx.at[w])
    keep_own(msg_ref.at[w], msg_rx.at[w])
    wide_wait(0, id_src, id_dst)
    ids0, ids1 = ids_rx[:, 0], ids_rx[:, 1]
    chosen = jnp.concatenate([one_hot_rows(ids0), one_hot_rows(ids1)], axis=0)
    g_fwd = [dot(chosen, z_fwd[i]).astype(bf16) for i in range(2)]
    g_inv = [dot(chosen, z_inv_t[i]).astype(bf16) for i in range(2)]
    ty0, ty1 = tile_y(ids0), tile_y(ids1)
    wide_wait(1, msg_src, msg_dst)

    kz = (iota((NG, 256), 1) & 127).astype(f32)
    for f in range(3):
        field = msg_rx[:, f].reshape(NW * 8, 128)
        placed = split(scatter_rows(field, ty0, ty1))
        lines = dot3(placed, g_fwd, ((0,), (0,)))
        if f == 2:
            lines = lines * kz
        for c in range(2):
            part = lines[:, c * 128 : (c + 1) * 128]
            by_x = [
                jnp.concatenate(
                    [part[ty * 64 + cx * 8 : ty * 64 + cx * 8 + 8] for ty in range(4)], axis=0
                )
                for cx in range(8)
            ]
            for i, value in enumerate(exchange(by_x)):
                snd2[f, c, 32 * i : 32 * i + 32, :] = value
        s, r = snd2.at[f], rx2.at[f]
        pencil_send(f, functools.partial(rows32, s), functools.partial(rows32, r))
    for f in range(3):
        keep_own(rows32(snd2.at[f], p), rows32(rx2.at[f], p))

    slope = y_slopes()
    parts = []
    table = (y_fwd[0], y_fwd[1])
    for f in range(3):
        s, r = snd2.at[f], rx2.at[f]
        pencil_wait(f, functools.partial(rows32, s), functools.partial(rows32, r))
        real, imag = y_forward(table, rx2[f, 0], rx2[f, 1])
        if f == 0:
            snd3[0, 0], snd3[0, 1] = real, imag
            s, r = snd3.at[0], rx3.at[0]
            wide_send(2, functools.partial(rows8, s), functools.partial(rows8, r))
        elif f == 1:
            snd3[1, 0], snd3[1, 1] = slope * real, slope * imag
        else:
            snd3[1, 0] += real
            snd3[1, 1] += imag
            s, r = snd3.at[1], rx3.at[1]
            wide_send(3, functools.partial(rows8, s), functools.partial(rows8, r))
    for i in range(2):
        keep_own(rows8(snd3.at[i], w), rows8(rx3.at[i], w))

    both = []
    for i in range(2):
        s, r = snd3.at[i], rx3.at[i]
        wide_wait(2 + i, functools.partial(rows8, s), functools.partial(rows8, r))
        both.append(
            jnp.concatenate(
                [
                    jnp.concatenate(
                        exchange([rx3[i, c, pl.ds(j, NW, stride=8), :] for j in range(8)]), axis=0
                    )
                    for c in range(2)
                ],
                axis=1,
            )
        )
    real, imag = solve_x(
        (x_fwd[0], x_fwd[1]), (x_inv[0], x_inv[1]), both[0], both[1], w, p
    )
    snd4[0], snd4[1] = real, imag
    s4, d4 = functools.partial(rows8, snd4), functools.partial(rows8, rx4)
    wide_send(4, s4, d4)
    keep_own(rows8(snd4, w), rows8(rx4, w))
    wide_wait(4, s4, d4)

    parts = [
        jnp.concatenate(exchange([rx4[c, pl.ds(j, NW, stride=8), :] for j in range(8)]), axis=0)
        for c in range(2)
    ]
    real, imag = back((y_inv[0], y_inv[1]), parts[0], parts[1])
    snd5[0], snd5[1] = real, imag
    s5, d5 = functools.partial(rows32, snd5), functools.partial(rows32, rx5)
    pencil_send(3, s5, d5)
    keep_own(rows32(snd5, p), rows32(rx5, p))
    pencil_wait(3, s5, d5)

    halves_z = []
    for c in range(2):
        by_x = exchange([rx5[c, 32 * i : 32 * i + 32, :] for i in range(8)])
        halves_z.append(
            jnp.concatenate(
                [by_x[cx][ty * 8 : ty * 8 + 8] for ty in range(4) for cx in range(8)], axis=0
            )
        )
    lines = split(jnp.concatenate(halves_z, axis=1))
    values = dot3(g_inv, lines, ((1,), (1,)))
    snd6[...] = pick_rows(values[: NW * 8], values[NW * 8 :], ty0, ty1)

    def row8(ref, i):
        return ref.at[pl.ds(pl.multiple_of(i * 8, 8), 8), :]

    s6, d6 = functools.partial(row8, snd6), functools.partial(row8, ret_ref)
    wide_send(5, s6, d6)
    keep_own(row8(snd6, w), row8(ret_ref, w))
    mesh = dot3(lines, (z_inv[0], z_inv[1]))
    for ty in range(4):
        for cx in range(8):
            mesh_ref[cx, ty * 8 : ty * 8 + 8, :] = mesh[ty * 64 + cx * 8 : ty * 64 + cx * 8 + 8]
    wide_wait(5, s6, d6)


def on_device(force_adjoint, paint_index, block_count, block_owner, block_tile):
    owner = block_owner.reshape(1, NB)
    smem = pl.BlockSpec(memory_space=pltpu.SMEM)
    vmem = pl.BlockSpec(memory_space=pltpu.VMEM)
    msg, ids = pl.pallas_call(
        paint_kernel,
        out_shape=(
            jax.ShapeDtypeStruct((NW, 3, 8, 128), f32),
            jax.ShapeDtypeStruct((NW, 2, 1, 128), jnp.int32),
        ),
        in_specs=[smem] * 3 + [vmem] * 2,
        out_specs=(vmem, vmem),
        scratch_shapes=[pltpu.SMEM((NW,), jnp.int32)],
        compiler_params=pltpu.CompilerParams(vmem_limit_bytes=32 << 20),
        name="paint",
    )(block_count, owner, block_tile, force_adjoint, paint_index)

    tabs = make_tables()
    names = ["z_fwd", "z_inv", "z_inv_t", "y_fwd", "y_inv", "x_fwd", "x_inv"]
    mesh_grad, ret = pl.pallas_call(
        mesh_kernel,
        out_shape=(
            jax.ShapeDtypeStruct((8, 32, NG), f32),
            jax.ShapeDtypeStruct((NG, 128), f32),
        ),
        in_specs=[vmem] * (2 + len(names)),
        out_specs=(vmem, vmem),
        scratch_shapes=[
            pltpu.VMEM((NW, 2, 1, 128), jnp.int32),
            pltpu.VMEM((NW, 3, 8, 128), f32),
            pltpu.VMEM((3, 2, NG, 128), f32),
            pltpu.VMEM((3, 2, NG, 128), f32),
            pltpu.VMEM((2, 2, NG, 128), f32),
            pltpu.VMEM((2, 2, NG, 128), f32),
            pltpu.VMEM((2, NG, 128), f32),
            pltpu.VMEM((2, NG, 128), f32),
            pltpu.VMEM((2, NG, 128), f32),
            pltpu.VMEM((2, NG, 128), f32),
            pltpu.VMEM((NG, 128), f32),
            pltpu.SemaphoreType.DMA((6, NW)),
            pltpu.SemaphoreType.DMA((6, NW)),
            pltpu.SemaphoreType.DMA((4, NP)),
            pltpu.SemaphoreType.DMA((4, NP)),
            pltpu.SemaphoreType.DMA,
        ],
        compiler_params=pltpu.CompilerParams(
            collective_id=0, has_side_effects=True, vmem_limit_bytes=48 << 20
        ),
        name="mesh",
    )(msg, ids, *[jnp.asarray(tabs[n]) for n in names])

    mass_grad = pl.pallas_call(
        read_kernel,
        out_shape=jax.ShapeDtypeStruct((1, NB * BP), f32),
        in_specs=[smem] * 2 + [vmem] * 2,
        out_specs=vmem,
        scratch_shapes=[pltpu.SMEM((NW,), jnp.int32)],
        compiler_params=pltpu.CompilerParams(vmem_limit_bytes=32 << 20),
        name="read",
    )(block_count, owner, paint_index, ret)
    return mesh_grad, mass_grad


def solution(mesh):
    return jax.shard_map(
        on_device,
        mesh=mesh,
        in_specs=(
            P(None, "pencil", "wide"),
            P("pencil", "wide"),
            P("pencil", "wide"),
            P("pencil", "wide", None),
            P("pencil", "wide"),
        ),
        out_specs=(P("wide", "pencil", None), P("pencil", "wide")),
        check_vma=False,
    )
```

```python
import math

import jax
import jax.numpy as jnp
import ml_dtypes
import numpy as np
from jax import lax
from jax.experimental import pallas as pl
from jax.experimental.pallas import tpu as pltpu
from jax.sharding import PartitionSpec as P

NG = 256
NW = 32
NP = 8
NB = 32
BP = 512
MESH = pl.DeviceIdType.MESH
f32 = jnp.float32
bf16 = jnp.bfloat16


def roll(x, shift, axis):
    return pltpu.roll(x, shift, axis)


def halves(table):
    table = np.asarray(table, np.float32)
    high = table.astype(ml_dtypes.bfloat16)
    low = (table - high.astype(np.float32)).astype(ml_dtypes.bfloat16)
    return np.stack([high, low])


def waves(first, second):
    phase = (np.asarray(first)[:, None] * np.asarray(second)[None, :]) % NG
    angle = phase * (2.0 * math.pi / NG)
    return np.cos(angle), np.sin(angle)


def ky_of_row():
    out = []
    for w in range(NW):
        for j in range(8):
            base = 4 * w + j % 4
            out.append(base if j < 4 else (128 if base == 0 else NG - base))
    return np.array(out)


def make_tables():
    line = np.arange(NG)
    half = np.arange(NG // 2)
    sign = np.where(line % 2 == 0, 1.0, -1.0)
    c, s = waves(line, half)
    s = -s
    s[:, 0] = sign
    z_fwd = np.concatenate([c, s], axis=1)
    c, s = waves(half, line)
    weight = np.where(half == 0, 1.0, 2.0)[:, None]
    c = c * weight
    s = -2.0 * s
    s[0] = sign
    z_inv = np.concatenate([c, s], axis=0)
    ky = ky_of_row()
    c, s = waves(ky, line)
    y_fwd = np.concatenate([c, s], axis=0)
    kyt = ky.reshape(NW, 8).T.reshape(-1)
    c, s = waves(line, kyt)
    y_inv = np.concatenate([c, s], axis=0)
    xt = line.reshape(NW, 8).T.reshape(-1)
    c, s = waves(line, xt)
    x_fwd = np.concatenate([c, s], axis=0)
    c, s = waves(line, line)
    x_inv = np.concatenate([c, s], axis=0)
    return dict(
        z_fwd=halves(z_fwd),
        z_inv=halves(z_inv),
        z_inv_t=halves(z_inv.T),
        y_fwd=halves(y_fwd),
        y_inv=halves(y_inv),
        x_fwd=halves(x_fwd),
        x_inv=halves(x_inv),
    )


def dot(a, b, dims=((1,), (0,))):
    return lax.dot_general(a, b, (dims, ((), ())), preferred_element_type=f32)


def split(x):
    high = x.astype(bf16)
    return high, (x - high.astype(f32)).astype(bf16)


def dot3(a, b, dims=((1,), (0,))):
    return dot(a[0], b[0], dims) + (dot(a[0], b[1], dims) + dot(a[1], b[0], dims))


def iota(shape, axis):
    return lax.broadcasted_iota(jnp.int32, shape, axis)


def exchange(arrays):
    chunk = iota(arrays[0].shape, 1) // 16
    for b in range(3):
        bit = (chunk >> b) & 1
        new = []
        for i in range(8):
            mine = (i >> b) & 1
            shift = 16 << b if mine == 0 else 128 - (16 << b)
            new.append(jnp.where(bit == mine, arrays[i], roll(arrays[i ^ (1 << b)], shift, 1)))
        arrays = new
    return arrays


def one_hot_rows(ids):
    spot = (ids & 31) * 8 + iota((NW, 8, 128), 1)
    spot = spot.reshape(NW * 8, 128)
    lane = iota((NW * 8, 128), 1)
    both = jnp.concatenate(
        [jnp.where(spot == lane, 1.0, 0.0), jnp.where(spot == lane + 128, 1.0, 0.0)], axis=1
    )
    return both.astype(bf16)


def tile_y(ids):
    return jnp.broadcast_to(ids >> 5, (NW, 8, 128)).reshape(NW * 8, 128)


def scatter_rows(field, ty0, ty1):
    upper = (iota((NW * 8, 128), 1) >= 64).astype(jnp.int32)
    turned = roll(field, 64, 1)
    first = jnp.where(upper == 0, field, turned)
    second = jnp.where(upper == 0, turned, field)
    rows = []
    for values, ty in ((first, ty0), (second, ty1)):
        rows.append(
            jnp.concatenate(
                [jnp.where(ty == upper, values, 0.0), jnp.where(ty == upper + 2, values, 0.0)],
                axis=1,
            )
        )
    return jnp.concatenate(rows, axis=0)


def pick_rows(v0, v1, ty0, ty1):
    lower = iota((NW * 8, 128), 1) < 64
    out = []
    for v, ty in ((v0, ty0), (v1, ty1)):
        half = jnp.where(ty >= 2, v[:, 128:], v[:, :128])
        out.append((half, roll(half, 64, 1)))
    first = jnp.where((ty0 & 1) == 1, out[0][1], out[0][0])
    second = jnp.where((ty1 & 1) == 1, out[1][0], out[1][1])
    return jnp.where(lower, first, second)


def y_slopes():
    row = iota((NG, 128), 0)
    base = (row >> 3) * 4 + (row & 3)
    return jnp.where((row & 4) == 0, base, -base).astype(f32)


def y_forward(table, real, imag):
    out = dot3(table, split(jnp.concatenate([real, imag], axis=1)))
    return out[:NG, :128] + out[NG:, 128:], out[:NG, 128:] - out[NG:, :128]


def back(table, real, imag):
    out = dot3(table, split(jnp.concatenate([real, imag], axis=1)))
    return out[:NG, :128] - out[NG:, 128:], out[:NG, 128:] + out[NG:, :128]


def solve_x(x_inv, a, b, w, p):
    cra, cia, sra, sia = a[:NG, :128], a[:NG, 128:], a[NG:, :128], a[NG:, 128:]
    crb, cib, srb, sib = b[:NG, :128], b[:NG, 128:], b[NG:, :128], b[NG:, 128:]
    row = iota((NG, 128), 0)
    lane = iota((NG, 128), 1)
    signed = jnp.where(row < 128, row, row - NG)
    slope = jnp.where(row == 128, 0, signed).astype(f32)
    p_re = slope * (cra + sia) + (crb + sib)
    p_im = slope * (cia - sra) + (cib - srb)
    q_re = (crb - sib) - slope * (cra - sia)
    q_im = slope * (cia + sra) - (cib + srb)
    alone = (w == 0) & ((lane & 63) < 16)
    r_re = jnp.where(alone, q_re, roll(q_re, 64, 1))
    r_im = jnp.where(alone, q_im, roll(q_im, 64, 1))
    j = lane >> 4
    base = 4 * w + (j & 3)
    ny = jnp.where((base == 0) & (j == 4), 128, base)
    kz = lane & 15
    nz = 16 * p + kz
    flat = signed * signed + ny * ny
    factor = (1.0 / NG**2) / jnp.maximum(flat + nz * nz, 1).astype(f32)
    top = (1.0 / NG**2) / (flat + (NG // 2) ** 2).astype(f32)
    shared = (nz == 0)
    alpha = jnp.where(shared, 0.5 * (factor + top), factor)
    beta = jnp.where(shared, 0.5 * (top - factor), 0.0)
    h_re = -(alpha * p_im + beta * r_im)
    h_im = alpha * p_re + beta * r_re
    return back(x_inv, h_re, h_im)


def wide_peer(w, i):
    iz, ix = i // 4, i % 4
    dz = 4 + (iz + 1) // 2 * (1 - 2 * ((iz + 1) % 2))
    dx = 2 + (ix + 1) // 2 * (1 - 2 * ((ix + 1) % 2))
    return (w // 8 + dx) % 4 * 8 + (w + dz) % 8


def loop(count, step, unroll=1):
    def body(i, carry):
        step(i)
        return carry

    lax.fori_loop(0, count, body, 0, unroll=unroll)


def rows(ref, i, size):
    return ref.at[:, pl.ds(pl.multiple_of(i * size, 8), size), :]


def step_kernel(
    force_hbm, cells_hbm, count_hbm, owner_hbm, tile_hbm,
    z_fwd_hbm, z_inv_t_hbm, z_inv_hbm, y_fwd_hbm, y_inv_hbm, x_fwd_hbm, x_inv_hbm,
    mesh_ref, mass_ref,
    force, cells, count, owner, tile, owner_v,
    z_fwd, z_inv_t, z_inv, y_fwd, y_inv, x_fwd, x_inv,
    spread, tiles, pick_v, pick, ids, msg, ids_rx, msg_rx,
    snd2, rx2, snd3, rx3, snd4, rx4, snd5, rx5, snd6, rx6,
    arg_sem, table_sem, pick_sem, wide_out, wide_in, pencil_out, pencil_in,
):
    w = lax.axis_index("wide")
    p = lax.axis_index("pencil")

    arg_copies = [
        pltpu.make_async_copy(src, dst, arg_sem.at[i])
        for i, (src, dst) in enumerate(
            [
                (owner_hbm, owner_v), (owner_hbm, owner), (count_hbm, count), (tile_hbm, tile),
                (cells_hbm, cells), (force_hbm, force),
            ]
        )
    ]
    table_copies = [
        pltpu.make_async_copy(src, dst, table_sem.at[i])
        for i, (src, dst) in enumerate(
            [
                (z_fwd_hbm, z_fwd), (z_inv_t_hbm, z_inv_t), (y_fwd_hbm, y_fwd),
                (x_fwd_hbm, x_fwd), (x_inv_hbm, x_inv), (y_inv_hbm, y_inv), (z_inv_hbm, z_inv),
            ]
        )
    ]
    for copy in arg_copies:
        copy.start()
    barrier = pltpu.get_barrier_semaphore()
    loop(
        NW - 1,
        lambda i: pl.semaphore_signal(
            barrier, inc=1, device_id={"wide": wide_peer(w, i)}, device_id_type=MESH
        ),
    )
    loop(
        NP - 1,
        lambda i: pl.semaphore_signal(
            barrier, inc=1, device_id={"pencil": (p + 1 + i) % NP}, device_id_type=MESH
        ),
    )
    for copy in table_copies:
        copy.start()

    def wide_copy(phase, src, dst, other):
        return pltpu.make_async_remote_copy(
            src_ref=src, dst_ref=dst, send_sem=wide_out.at[phase], recv_sem=wide_in.at[phase],
            device_id={"wide": other}, device_id_type=MESH,
        )

    def pencil_copy(phase, src, dst, other):
        return pltpu.make_async_remote_copy(
            src_ref=src, dst_ref=dst, send_sem=pencil_out.at[phase], recv_sem=pencil_in.at[phase],
            device_id={"pencil": other}, device_id_type=MESH,
        )

    def wide_send(phase, src, dst):
        def step(i):
            other = wide_peer(w, i)
            wide_copy(phase, rows(src, other, 8), rows(dst, w, 8), other).start()

        loop(NW - 1, step)
        here = pl.ds(pl.multiple_of(w * 8, 8), 8)
        dst[:, here, :] = src[:, here, :]

    def wide_all(phase, src, dst):
        part = pl.ds(0, (NW - 1) * 8)
        return wide_copy(phase, src.at[:, part, :], dst.at[:, part, :], (w + 1) % NW)

    def pencil_send(phase, src, dst):
        def step(i):
            other = (p + 1 + i) % NP
            pencil_copy(phase, rows(src, other, 32), rows(dst, p, 32), other).start()

        loop(NP - 1, step)
        here = pl.ds(pl.multiple_of(p * 32, 32), 32)
        dst[:, here, :] = src[:, here, :]

    def pencil_all(phase, src, dst):
        part = pl.ds(0, (NP - 1) * 32)
        return pencil_copy(phase, src.at[:, part, :], dst.at[:, part, :], (p + 1) % NP)

    arg_copies[0].wait()
    block = iota((NW, NB), 1)
    match = owner_v[...] == iota((NW, NB), 0)
    first = jnp.min(jnp.where(match, block, NB), axis=1, keepdims=True)
    last = jnp.max(jnp.where(match, block, -1), axis=1, keepdims=True)
    second = jnp.where(last > first, last, NB)
    pick_v[...] = jnp.where(iota((NW, 128), 1) == 0, first, second)
    pick_copy = pltpu.make_async_copy(pick_v, pick, pick_sem)
    pick_copy.start()

    for copy in arg_copies[1:]:
        copy.wait()
    tiles[NB] = jnp.zeros((3, 8, 128), f32)

    def slots(b):
        return pl.ds(pl.multiple_of(b * BP, BP), BP)

    def kept(b):
        live = iota((1, BP), 1) < count[0, b]
        return (iota((8, BP), 0) == (cells[0:1, slots(b)] & 7)) & live

    def paint(b):
        key = cells[0:1, slots(b)] >> 3
        hot = jnp.where((iota((128, BP), 0) & 63) == key, 1.0, 0.0).astype(bf16)
        spread[b] = hot
        keep = kept(b)
        high, low = [], []
        for f in range(3):
            amount = force[f, 0:1, slots(b)]
            top = amount.astype(bf16).astype(f32)
            high.append(jnp.where(keep, top, 0.0))
            low.append(jnp.where(keep, amount - top, 0.0))
        out = dot(jnp.concatenate(high + low, axis=0).astype(bf16), hot, ((1,), (1,)))
        tiles[b] = (out[:24] + out[24:]).reshape(3, 8, 128)

    loop(NB, paint, unroll=4)
    pick_copy.wait()
    pl.semaphore_wait(barrier, NW - 1 + NP - 1)

    left = iota((8, 128), 1) < 64

    def assemble(f, o):
        msg[f, o] = jnp.where(left, tiles[pick[o, 0], f], tiles[pick[o, 1], f])

    def number(o):
        for s in range(2):
            b = pick[o, s]
            t = jnp.where(b < NB, tile[0, jnp.minimum(b, NB - 1)], -1)
            ids[o, s] = jnp.full((1, 128), t, jnp.int32)

    def send_first(i):
        other = wide_peer(w, i)
        number(other)
        wide_copy(0, ids.at[other], ids_rx.at[w], other).start()
        assemble(0, other)
        wide_copy(1, msg.at[0, other], msg_rx.at[0, w], other).start()

    loop(NW - 1, send_first)
    for f in (1, 2):

        def send_field(i, f=f):
            other = wide_peer(w, i)
            assemble(f, other)
            wide_copy(1 + f, msg.at[f, other], msg_rx.at[f, w], other).start()

        loop(NW - 1, send_field)
    number(w)
    ids_rx[w] = ids[w]
    for f in range(3):
        assemble(f, w)
        msg_rx[f, w] = msg[f, w]
    others = pl.ds(0, NW - 1)
    ids_all = wide_copy(0, ids.at[others], ids_rx.at[others], (w + 1) % NW)
    msg_all = [
        wide_copy(1 + f, msg.at[f, others], msg_rx.at[f, others], (w + 1) % NW) for f in range(3)
    ]
    ids_all.wait_recv()
    ids0, ids1 = ids_rx[:, 0], ids_rx[:, 1]
    chosen = jnp.concatenate([one_hot_rows(ids0), one_hot_rows(ids1)], axis=0)
    table_copies[0].wait()
    table_copies[1].wait()
    g_fwd = [dot(chosen, z_fwd[i]).astype(bf16) for i in range(2)]
    g_inv = [dot(chosen, z_inv_t[i]).astype(bf16) for i in range(2)]
    ty0, ty1 = tile_y(ids0), tile_y(ids1)

    kz = (iota((NG, 256), 1) & 127).astype(f32)
    for f in range(3):
        msg_all[f].wait_recv()
        field = msg_rx[f].reshape(NW * 8, 128)
        lines = dot3(split(scatter_rows(field, ty0, ty1)), g_fwd, ((0,), (0,)))
        if f == 2:
            lines = lines * kz
        for c in range(2):
            part = lines[:, c * 128 : (c + 1) * 128]
            by_x = [
                jnp.concatenate(
                    [part[ty * 64 + cx * 8 : ty * 64 + cx * 8 + 8] for ty in range(4)], axis=0
                )
                for cx in range(8)
            ]
            for i, value in enumerate(exchange(by_x)):
                snd2[f, c, 32 * i : 32 * i + 32, :] = value
        pencil_send(f, snd2.at[f], rx2.at[f])

    slope = y_slopes()
    table_copies[2].wait()
    for f in range(3):
        pencil_all(f, snd2.at[f], rx2.at[f]).wait_recv()
        real, imag = y_forward((y_fwd[0], y_fwd[1]), rx2[f, 0], rx2[f, 1])
        if f == 0:
            snd3[0, 0], snd3[0, 1] = real, imag
            wide_send(4, snd3.at[0], rx3.at[0])
        elif f == 1:
            snd3[1, 0], snd3[1, 1] = slope * real, slope * imag
        else:
            snd3[1, 0] += real
            snd3[1, 1] += imag
            wide_send(5, snd3.at[1], rx3.at[1])

    table_copies[3].wait()
    table_copies[4].wait()
    both = []
    for i in range(2):
        wide_all(4 + i, snd3.at[i], rx3.at[i]).wait_recv()
        parts = [
            jnp.concatenate(
                exchange([rx3[i, c, pl.ds(j, NW, stride=8), :] for j in range(8)]), axis=0
            )
            for c in range(2)
        ]
        both.append(dot3((x_fwd[0], x_fwd[1]), split(jnp.concatenate(parts, axis=1))))
    snd4[0], snd4[1] = solve_x((x_inv[0], x_inv[1]), both[0], both[1], w, p)
    wide_send(6, snd4, rx4)

    table_copies[5].wait()
    wide_all(6, snd4, rx4).wait_recv()
    parts = [
        jnp.concatenate(exchange([rx4[c, pl.ds(j, NW, stride=8), :] for j in range(8)]), axis=0)
        for c in range(2)
    ]
    snd5[0], snd5[1] = back((y_inv[0], y_inv[1]), parts[0], parts[1])
    pencil_send(3, snd5, rx5)

    table_copies[6].wait()
    pencil_all(3, snd5, rx5).wait_recv()
    halves_z = []
    for c in range(2):
        by_x = exchange([rx5[c, 32 * i : 32 * i + 32, :] for i in range(8)])
        halves_z.append(
            jnp.concatenate(
                [by_x[cx][ty * 8 : ty * 8 + 8] for ty in range(4) for cx in range(8)], axis=0
            )
        )
    lines = split(jnp.concatenate(halves_z, axis=1))
    values = dot3(g_inv, lines, ((1,), (1,)))
    snd6[...] = pick_rows(values[: NW * 8], values[NW * 8 :], ty0, ty1).reshape(NW, 8, 128)

    def send_back(i):
        other = wide_peer(w, i)
        wide_copy(7, snd6.at[other], rx6.at[w], other).start()

    loop(NW - 1, send_back)
    rx6[w] = snd6[w]
    mesh = dot3(lines, (z_inv[0], z_inv[1]))
    for ty in range(4):
        for cx in range(8):
            mesh_ref[cx, ty * 8 : ty * 8 + 8, :] = mesh[ty * 64 + cx * 8 : ty * 64 + cx * 8 + 8]
    ids_all.wait_send()
    for f in range(3):
        msg_all[f].wait_send()
        pencil_all(f, snd2.at[f], rx2.at[f]).wait_send()
    for i in range(2):
        wide_all(4 + i, snd3.at[i], rx3.at[i]).wait_send()
    wide_all(6, snd4, rx4).wait_send()
    pencil_all(3, snd5, rx5).wait_send()
    wide_copy(7, snd6.at[others], rx6.at[others], (w + 1) % NW).wait()

    lower = iota((8, 128), 1) < 64

    def read(b):
        o = owner[0, b]
        here = jnp.where(pick[o, 0] == b, 0, 1)
        tile_in = rx6[o]
        side = jnp.where(lower, 0, 1)
        tile_in = jnp.where(side == here, tile_in, 0.0)
        top = tile_in.astype(bf16).astype(f32)
        out = dot(jnp.concatenate([top, tile_in - top], axis=0).astype(bf16), spread[b])
        value = jnp.sum(jnp.where(kept(b), out[:8] + out[8:], 0.0), axis=0, keepdims=True)
        mass_ref[0:1, slots(b)] = value

    loop(NB, read, unroll=4)


def on_device(force_adjoint, paint_index, block_count, block_owner, block_tile):
    tabs = make_tables()
    names = ["z_fwd", "z_inv_t", "z_inv", "y_fwd", "y_inv", "x_fwd", "x_inv"]
    tables = [tabs[n] for n in names]
    vmem = pl.BlockSpec(memory_space=pltpu.VMEM)
    wave = pltpu.VMEM((2, NG, 128), f32)
    dma = pltpu.SemaphoreType.DMA
    mesh_grad, mass_grad = pl.pallas_call(
        step_kernel,
        out_shape=(
            jax.ShapeDtypeStruct((8, 32, NG), f32),
            jax.ShapeDtypeStruct((1, NB * BP), f32),
        ),
        in_specs=[pl.BlockSpec(memory_space=pl.ANY)] * (5 + len(names)),
        out_specs=(vmem, vmem),
        scratch_shapes=[
            pltpu.VMEM((3, 1, NB * BP), f32),
            pltpu.VMEM((1, NB * BP), jnp.int32),
            pltpu.SMEM((1, NB), jnp.int32),
            pltpu.SMEM((1, NB), jnp.int32),
            pltpu.SMEM((1, NB), jnp.int32),
            pltpu.VMEM((1, NB), jnp.int32),
            *[pltpu.VMEM(t.shape, bf16) for t in tables],
            pltpu.VMEM((NB, 128, BP), bf16),
            pltpu.VMEM((NB + 1, 3, 8, 128), f32),
            pltpu.VMEM((NW, 128), jnp.int32),
            pltpu.SMEM((NW, 128), jnp.int32),
            pltpu.VMEM((NW, 2, 1, 128), jnp.int32),
            pltpu.VMEM((3, NW, 8, 128), f32),
            pltpu.VMEM((NW, 2, 1, 128), jnp.int32),
            pltpu.VMEM((3, NW, 8, 128), f32),
            pltpu.VMEM((3, 2, NG, 128), f32),
            pltpu.VMEM((3, 2, NG, 128), f32),
            pltpu.VMEM((2, 2, NG, 128), f32),
            pltpu.VMEM((2, 2, NG, 128), f32),
            wave, wave, wave, wave,
            pltpu.VMEM((NW, 8, 128), f32),
            pltpu.VMEM((NW, 8, 128), f32),
            dma((6,)), dma((7,)), dma, dma((8,)), dma((8,)), dma((4,)), dma((4,)),
        ],
        compiler_params=pltpu.CompilerParams(
            collective_id=0, has_side_effects=True, vmem_limit_bytes=60 << 20
        ),
        name="step",
    )(
        force_adjoint, paint_index, block_count, block_owner.reshape(1, NB), block_tile,
        *[jnp.asarray(t) for t in tables],
    )
    return mesh_grad, mass_grad


def solution(mesh):
    return jax.shard_map(
        on_device,
        mesh=mesh,
        in_specs=(
            P(None, "pencil", "wide"),
            P("pencil", "wide"),
            P("pencil", "wide"),
            P("pencil", "wide", None),
            P("pencil", "wide"),
        ),
        out_specs=(P("wide", "pencil", None), P("pencil", "wide")),
        check_vma=False,
    )
```

```python
import math

import jax
import jax.numpy as jnp
import ml_dtypes
import numpy as np
from jax import lax
from jax.experimental import pallas as pl
from jax.experimental.pallas import tpu as pltpu
from jax.sharding import PartitionSpec as P

NG = 256
NW = 32
NP = 8
NB = 32
BP = 512
MESH = pl.DeviceIdType.MESH
f32 = jnp.float32
bf16 = jnp.bfloat16


def roll(x, shift, axis):
    return pltpu.roll(x, shift, axis)


def halves(table):
    table = np.asarray(table, np.float32)
    high = table.astype(ml_dtypes.bfloat16)
    low = (table - high.astype(np.float32)).astype(ml_dtypes.bfloat16)
    return np.stack([high, low])


def waves(first, second):
    phase = (np.asarray(first)[:, None] * np.asarray(second)[None, :]) % NG
    angle = phase * (2.0 * math.pi / NG)
    return np.cos(angle), np.sin(angle)


def ky_of_row():
    out = []
    for w in range(NW):
        for j in range(8):
            base = 4 * w + j % 4
            out.append(base if j < 4 else (128 if base == 0 else NG - base))
    return np.array(out)


def make_tables():
    line = np.arange(NG)
    half = np.arange(NG // 2)
    sign = np.where(line % 2 == 0, 1.0, -1.0)
    c, s = waves(line, half)
    s = -s
    s[:, 0] = sign
    z_fwd = np.concatenate([c, s], axis=1)
    c, s = waves(half, line)
    weight = np.where(half == 0, 1.0, 2.0)[:, None]
    c = c * weight
    s = -2.0 * s
    s[0] = sign
    z_inv = np.concatenate([c, s], axis=0)
    ky = ky_of_row()
    c, s = waves(ky, line)
    y_fwd = np.concatenate([c, s], axis=0)
    kyt = ky.reshape(NW, 8).T.reshape(-1)
    c, s = waves(line, kyt)
    y_inv = np.concatenate([c, s], axis=0)
    xt = line.reshape(NW, 8).T.reshape(-1)
    c, s = waves(line, xt)
    x_fwd = np.concatenate([c, s], axis=0)
    c, s = waves(line, line)
    full = np.stack([np.concatenate([c, -s], axis=1), np.concatenate([s, c], axis=1)])
    x_inv = full.reshape(2, NW, 2, 4, 2 * NG).transpose(2, 1, 0, 3, 4).reshape(2 * NG, 2 * NG)
    return dict(
        z_fwd=halves(z_fwd),
        z_inv=halves(z_inv),
        z_inv_t=halves(z_inv.T),
        y_fwd=halves(y_fwd),
        y_inv=halves(y_inv),
        x_fwd=halves(x_fwd),
        x_inv=halves(x_inv),
    )


def dot(a, b, dims=((1,), (0,))):
    return lax.dot_general(a, b, (dims, ((), ())), preferred_element_type=f32)


def split(x):
    high = x.astype(bf16)
    return high, (x - high.astype(f32)).astype(bf16)


def dot3(a, b, dims=((1,), (0,))):
    return dot(a[0], b[0], dims) + (dot(a[0], b[1], dims) + dot(a[1], b[0], dims))


def iota(shape, axis):
    return lax.broadcasted_iota(jnp.int32, shape, axis)


def exchange(arrays):
    chunk = iota(arrays[0].shape, 1) // 16
    for b in range(3):
        bit = (chunk >> b) & 1
        new = []
        for i in range(8):
            mine = (i >> b) & 1
            shift = 16 << b if mine == 0 else 128 - (16 << b)
            new.append(jnp.where(bit == mine, arrays[i], roll(arrays[i ^ (1 << b)], shift, 1)))
        arrays = new
    return arrays


def one_hot_rows(ids):
    spot = (ids & 31) * 8 + (iota((NW * 8, 128), 0) & 7)
    lane = iota((NW * 8, 128), 1)
    both = jnp.concatenate(
        [jnp.where(spot == lane, 1.0, 0.0), jnp.where(spot == lane + 128, 1.0, 0.0)], axis=1
    )
    return both.astype(bf16)


def scatter_rows(field, ty0, ty1):
    upper = (iota((NW * 8, 128), 1) >= 64).astype(jnp.int32)
    turned = roll(field, 64, 1)
    first = jnp.where(upper == 0, field, turned)
    second = jnp.where(upper == 0, turned, field)
    rows = []
    for values, ty in ((first, ty0), (second, ty1)):
        rows.append(
            jnp.concatenate(
                [jnp.where(ty == upper, values, 0.0), jnp.where(ty == upper + 2, values, 0.0)],
                axis=1,
            )
        )
    return jnp.concatenate(rows, axis=0)


def pick_rows(v0, v1, ty0, ty1):
    lower = iota((NW * 8, 128), 1) < 64
    out = []
    for v, ty in ((v0, ty0), (v1, ty1)):
        half = jnp.where(ty >= 2, v[:, 128:], v[:, :128])
        out.append((half, roll(half, 64, 1)))
    first = jnp.where((ty0 & 1) == 1, out[0][1], out[0][0])
    second = jnp.where((ty1 & 1) == 1, out[1][0], out[1][1])
    return jnp.where(lower, first, second)


def y_slopes():
    row = iota((NG, 128), 0)
    base = (row >> 3) * 4 + (row & 3)
    return jnp.where((row & 4) == 0, base, -base).astype(f32)


def combine(sums, sign):
    out = []
    for k in range(0, sums.shape[1], 128):
        turned = roll(sums[NG:, k : k + 128], 64, 1)
        real = iota((NG, 128), 1) < 64
        out.append(sums[:NG, k : k + 128] + jnp.where(real, -sign * turned, sign * turned))
    return out


def solve_x(a, b, w, p):
    cra, cia, sra, sia = a[:NG, :128], a[:NG, 128:], a[NG:, :128], a[NG:, 128:]
    crb, cib, srb, sib = b[:NG, :128], b[:NG, 128:], b[NG:, :128], b[NG:, 128:]
    row = iota((NG, 128), 0)
    lane = iota((NG, 128), 1)
    signed = jnp.where(row < 128, row, row - NG)
    slope = jnp.where(row == 128, 0, signed).astype(f32)
    p_re = slope * (cra + sia) + (crb + sib)
    p_im = slope * (cia - sra) + (cib - srb)
    q_re = (crb - sib) - slope * (cra - sia)
    q_im = slope * (cia + sra) - (cib + srb)
    alone = (w == 0) & ((lane & 63) < 16)
    r_re = jnp.where(alone, q_re, roll(q_re, 64, 1))
    r_im = jnp.where(alone, q_im, roll(q_im, 64, 1))
    j = lane >> 4
    base = 4 * w + (j & 3)
    ny = jnp.where((base == 0) & (j == 4), 128, base)
    kz = lane & 15
    nz = 16 * p + kz
    flat = signed * signed + ny * ny
    factor = (1.0 / NG**2) / jnp.maximum(flat + nz * nz, 1).astype(f32)
    top = (1.0 / NG**2) / (flat + (NG // 2) ** 2).astype(f32)
    shared = (nz == 0)
    alpha = jnp.where(shared, 0.5 * (factor + top), factor)
    beta = jnp.where(shared, 0.5 * (top - factor), 0.0)
    h_re = -(alpha * p_im + beta * r_im)
    h_im = alpha * p_re + beta * r_re
    return h_re, h_im


def wide_peer(w, i):
    iz, ix = i // 4, i % 4
    dz = 4 + (iz + 1) // 2 * (1 - 2 * ((iz + 1) % 2))
    dx = 2 + (ix + 1) // 2 * (1 - 2 * ((ix + 1) % 2))
    return (w // 8 + dx) % 4 * 8 + (w + dz) % 8


def pencil_peer(p, i):
    dy = 2 + (i // 2 + 1) // 2 * (1 - 2 * ((i // 2 + 1) % 2))
    return (p // 2 + dy) % 4 * 2 + (p + i + i // 6) % 2


def loop(count, step, unroll=1):
    def body(i, carry):
        step(i)
        return carry

    lax.fori_loop(0, count, body, 0, unroll=unroll)


def half(ref, h):
    return ref.at[pl.ds(h, 1)]


def rows(ref, i, size):
    return ref.at[:, pl.ds(pl.multiple_of(i * size, 8), size), :]


def step_kernel(
    force_hbm, cells_hbm, count_hbm, owner_hbm, tile_hbm,
    z_fwd_hbm, z_inv_t_hbm, z_inv_hbm, y_fwd_hbm, y_inv_hbm, x_fwd_hbm, x_inv_hbm,
    mesh_ref, mass_ref,
    force, cells, count, owner, tile, owner_v,
    z_fwd, z_inv_t, z_inv, y_fwd, y_inv, x_fwd, x_inv,
    spread, tiles, pick_v, pick, ids, msg, ids_rx, msg_rx,
    snd2, rx2, snd3, rx3, snd4, rx4, snd5, rx5, snd6, rx6, mesh_v,
    arg_sem, table_sem, pick_sem, wide_out, wide_in, pencil_out, pencil_in,
):
    w = lax.axis_index("wide")
    p = lax.axis_index("pencil")

    arg_copies = [
        pltpu.make_async_copy(src, dst, arg_sem.at[i])
        for i, (src, dst) in enumerate(
            [
                (owner_hbm, owner_v), (owner_hbm, owner), (count_hbm, count), (tile_hbm, tile),
                (cells_hbm, cells), (force_hbm, force),
            ]
        )
    ]
    table_copies = [
        pltpu.make_async_copy(src, dst, table_sem.at[i])
        for i, (src, dst) in enumerate(
            [
                (z_fwd_hbm, z_fwd), (z_inv_t_hbm, z_inv_t), (y_fwd_hbm, y_fwd),
                (x_fwd_hbm, x_fwd), (x_inv_hbm, x_inv), (y_inv_hbm, y_inv), (z_inv_hbm, z_inv),
            ]
        )
    ]
    for copy in arg_copies:
        copy.start()
    barrier = pltpu.get_barrier_semaphore()
    loop(
        NW - 1,
        lambda i: pl.semaphore_signal(
            barrier, inc=1, device_id={"wide": wide_peer(w, i)}, device_id_type=MESH
        ),
    )
    loop(
        NP - 1,
        lambda i: pl.semaphore_signal(
            barrier, inc=1, device_id={"pencil": pencil_peer(p, i)}, device_id_type=MESH
        ),
    )
    for copy in table_copies:
        copy.start()

    def wide_copy(phase, src, dst, other):
        return pltpu.make_async_remote_copy(
            src_ref=src, dst_ref=dst, send_sem=wide_out.at[phase], recv_sem=wide_in.at[phase],
            device_id={"wide": other}, device_id_type=MESH,
        )

    def pencil_copy(phase, src, dst, other):
        return pltpu.make_async_remote_copy(
            src_ref=src, dst_ref=dst, send_sem=pencil_out.at[phase], recv_sem=pencil_in.at[phase],
            device_id={"pencil": other}, device_id_type=MESH,
        )

    def wide_send(phase, src, dst):
        def step(i):
            other = wide_peer(w, i)
            wide_copy(phase, rows(src, other, 8), rows(dst, w, 8), other).start()

        loop(NW - 1, step)
        here = pl.ds(pl.multiple_of(w * 8, 8), 8)
        dst[:, here, :] = src[:, here, :]

    def wide_all(phase, src, dst):
        part = pl.ds(0, (NW - 1) * 8)
        return wide_copy(phase, src.at[:, part, :], dst.at[:, part, :], (w + 1) % NW)

    def pencil_send(phase, src, dst):
        def step(i):
            other = pencil_peer(p, i)
            pencil_copy(phase, rows(src, other, 32), rows(dst, p, 32), other).start()

        loop(NP - 1, step)
        here = pl.ds(pl.multiple_of(p * 32, 32), 32)
        dst[:, here, :] = src[:, here, :]

    def pencil_all(phase, src, dst):
        part = pl.ds(0, (NP - 1) * 32)
        return pencil_copy(phase, src.at[:, part, :], dst.at[:, part, :], (p + 1) % NP)

    arg_copies[0].wait()
    block = iota((NW, NB), 1)
    match = owner_v[...] == iota((NW, NB), 0)
    first = jnp.min(jnp.where(match, block, NB), axis=1, keepdims=True)
    last = jnp.max(jnp.where(match, block, -1), axis=1, keepdims=True)
    second = jnp.where(last > first, last, NB)
    pick_v[...] = jnp.where(iota((NW, 128), 1) == 0, first, second)
    pick_copy = pltpu.make_async_copy(pick_v, pick, pick_sem)
    pick_copy.start()

    for copy in arg_copies[1:]:
        copy.wait()
    tiles[NB] = jnp.zeros((3, 8, 128), f32)

    def slots(b):
        return pl.ds(pl.multiple_of(b * BP, BP), BP)

    def kept(b):
        live = iota((1, BP), 1) < count[0, b]
        return (iota((8, BP), 0) == (cells[0:1, slots(b)] & 7)) & live

    def paint(b):
        key = cells[0:1, slots(b)] >> 3
        hot = jnp.where(iota((64, BP), 0) == key, 1.0, 0.0).astype(bf16)
        spread[b] = hot
        keep = kept(b)
        high, low = [], []
        for f in range(3):
            amount = force[f, 0:1, slots(b)]
            top = amount.astype(bf16).astype(f32)
            high.append(jnp.where(keep, top, 0.0))
            low.append(jnp.where(keep, amount - top, 0.0))
        out = dot(jnp.concatenate(high + low, axis=0).astype(bf16), hot, ((1,), (1,)))
        out = out[:24] + out[24:]
        tiles[b] = jnp.concatenate([out, out], axis=1).reshape(3, 8, 128)

    loop(NB, paint, unroll=4)
    pick_copy.wait()
    pl.semaphore_wait(barrier, NW - 1 + NP - 1)

    left = iota((8, 128), 1) < 64

    def assemble(f, o):
        msg[f, o] = jnp.where(left, tiles[pick[o, 0], f], tiles[pick[o, 1], f])

    def number(o):
        name = []
        for s in range(2):
            b = pick[o, s]
            name.append(jnp.where(b < NB, tile[0, jnp.minimum(b, NB - 1)], -1))
        ids[o] = jnp.where(iota((1, 128), 1) < 64, name[0], name[1])

    def send_first(i):
        other = wide_peer(w, i)
        number(other)
        wide_copy(0, ids.at[other], ids_rx.at[w], other).start()
        assemble(0, other)
        wide_copy(1, msg.at[0, other], msg_rx.at[0, w], other).start()

    loop(NW - 1, send_first)
    for f in (1, 2):

        def send_field(i, f=f):
            other = wide_peer(w, i)
            assemble(f, other)
            wide_copy(1 + f, msg.at[f, other], msg_rx.at[f, w], other).start()

        loop(NW - 1, send_field)
    number(w)
    ids_rx[w] = ids[w]
    for f in range(3):
        assemble(f, w)
        msg_rx[f, w] = msg[f, w]
    others = pl.ds(0, NW - 1)
    ids_all = wide_copy(0, ids.at[others], ids_rx.at[others], (w + 1) % NW)
    msg_all = [
        wide_copy(1 + f, msg.at[f, others], msg_rx.at[f, others], (w + 1) % NW) for f in range(3)
    ]
    ids_all.wait_recv()
    pair = jnp.broadcast_to(ids_rx[...], (NW, 8, 128)).reshape(NW * 8, 128)
    turned = roll(pair, 64, 1)
    lower = iota((NW * 8, 128), 1) < 64
    ids0, ids1 = jnp.where(lower, pair, turned), jnp.where(lower, turned, pair)
    chosen = jnp.concatenate([one_hot_rows(ids0), one_hot_rows(ids1)], axis=0)
    table_copies[0].wait()
    table_copies[1].wait()
    g_fwd = [dot(chosen, z_fwd[i]).astype(bf16) for i in range(2)]
    g_inv = [dot(chosen, z_inv_t[i]).astype(bf16) for i in range(2)]
    ty0, ty1 = ids0 >> 5, ids1 >> 5

    kz = (iota((NG, 256), 1) & 127).astype(f32)
    for f in range(3):
        msg_all[f].wait_recv()
        field = msg_rx[f].reshape(NW * 8, 128)
        lines = dot3(split(scatter_rows(field, ty0, ty1)), g_fwd, ((0,), (0,)))
        if f == 2:
            lines = lines * kz
        for h in range(2):
            by_x = [
                jnp.concatenate(
                    [
                        lines[ty * 64 + cx * 8 : ty * 64 + cx * 8 + 8, c * 128 : c * 128 + 128]
                        for ty in range(4)
                    ],
                    axis=0,
                )
                for c in range(2)
                for cx in range(4 * h, 4 * h + 4)
            ]
            for i, value in enumerate(exchange(by_x)):
                snd2[f, h, 32 * i : 32 * i + 32, :] = value
            if f == 2:
                pencil_send(2 + h, half(snd2.at[f], h), half(rx2.at[f], h))
        if f < 2:
            pencil_send(f, snd2.at[f], rx2.at[f])

    slope = y_slopes()
    table_copies[2].wait()
    for f in range(2):
        pencil_all(f, snd2.at[f], rx2.at[f]).wait_recv()
        both = jnp.concatenate([rx2[f, 0], rx2[f, 1]], axis=1)
        for h, value in enumerate(combine(dot3((y_fwd[0], y_fwd[1]), split(both)), -1.0)):
            snd3[f, h] = value if f == 0 else slope * value
        if f == 0:
            wide_send(4, snd3.at[0], rx3.at[0])
    for h in range(2):
        pencil_all(2 + h, half(snd2.at[2], h), half(rx2.at[2], h)).wait_recv()
        sums = dot3((y_fwd[0], y_fwd[1]), split(rx2[2, h]))
        snd3[1, h] += combine(sums, -1.0)[0]
        wide_send(5 + h, half(snd3.at[1], h), half(rx3.at[1], h))

    table_copies[3].wait()
    table_copies[4].wait()

    def x_part(i, h):
        parts = exchange([rx3[i, h, pl.ds(j, NW, stride=8), :] for j in range(8)])
        parts = [jnp.concatenate(parts[c : c + 4], axis=0) for c in (0, 4)]
        table = [x_fwd[k, :, h * 128 : h * 128 + 128] for k in range(2)]
        return dot3(table, split(jnp.concatenate(parts, axis=1)))

    wide_all(4, snd3.at[0], rx3.at[0]).wait_recv()
    first = x_part(0, 0) + x_part(0, 1)
    second = []
    for h in range(2):
        wide_all(5 + h, half(snd3.at[1], h), half(rx3.at[1], h)).wait_recv()
        second.append(x_part(1, h))
    spectrum = split(jnp.concatenate(solve_x(first, second[0] + second[1], w, p), axis=0))
    for h in range(2):
        snd4[h] = dot3([x_inv[k, h * NG : h * NG + NG, :] for k in range(2)], spectrum)
        wide_send(7 + h, half(snd4, h), half(rx4, h))

    table_copies[5].wait()
    for h in range(2):
        wide_all(7 + h, half(snd4, h), half(rx4, h)).wait_recv()
        parts = exchange([rx4[h, pl.ds(r, NW, stride=8), :] for r in range(8)])
        sums = dot3((y_inv[0], y_inv[1]), split(jnp.concatenate(parts, axis=0)))
        snd5[h] = combine(sums, 1.0)[0]
        pencil_send(4 + h, half(snd5, h), half(rx5, h))

    table_copies[6].wait()
    lines = []
    for h in range(2):
        pencil_all(4 + h, half(snd5, h), half(rx5, h)).wait_recv()
        lines.append(exchange([rx5[h, 32 * i : 32 * i + 32, :] for i in range(8)]))
    lines = split(
        jnp.concatenate(
            [
                jnp.concatenate(
                    [
                        lines[cx // 4][4 * c + cx % 4][ty * 8 : ty * 8 + 8]
                        for ty in range(4)
                        for cx in range(8)
                    ],
                    axis=0,
                )
                for c in range(2)
            ],
            axis=1,
        )
    )
    values = dot3(g_inv, lines, ((1,), (1,)))
    snd6[...] = pick_rows(values[: NW * 8], values[NW * 8 :], ty0, ty1).reshape(NW, 8, 128)

    def send_back(i):
        other = wide_peer(w, i)
        wide_copy(9, snd6.at[other], rx6.at[w], other).start()

    loop(NW - 1, send_back)
    rx6[w] = snd6[w]
    mesh = dot3(lines, (z_inv[0], z_inv[1]))
    for ty in range(4):
        for cx in range(8):
            mesh_v[cx, ty * 8 : ty * 8 + 8, :] = mesh[ty * 64 + cx * 8 : ty * 64 + cx * 8 + 8]
    mesh_copy = pltpu.make_async_copy(mesh_v, mesh_ref, pick_sem)
    mesh_copy.start()
    ids_all.wait_send()
    for f in range(3):
        msg_all[f].wait_send()
    for f in range(2):
        pencil_all(f, snd2.at[f], rx2.at[f]).wait_send()
    wide_all(4, snd3.at[0], rx3.at[0]).wait_send()
    for h in range(2):
        pencil_all(2 + h, half(snd2.at[2], h), half(rx2.at[2], h)).wait_send()
        wide_all(5 + h, half(snd3.at[1], h), half(rx3.at[1], h)).wait_send()
        wide_all(7 + h, half(snd4, h), half(rx4, h)).wait_send()
        pencil_all(4 + h, half(snd5, h), half(rx5, h)).wait_send()
    wide_copy(9, snd6.at[others], rx6.at[others], (w + 1) % NW).wait()

    def read(b):
        o = owner[0, b]
        pair = rx6[o]
        here = jnp.where(pick[o, 0] == b, pair, roll(pair, 64, 1))
        tile_in = here[:, :64]
        top = tile_in.astype(bf16).astype(f32)
        out = dot(jnp.concatenate([top, tile_in - top], axis=0).astype(bf16), spread[b])
        value = jnp.sum(jnp.where(kept(b), out[:8] + out[8:], 0.0), axis=0, keepdims=True)
        mass_ref[0:1, slots(b)] = value

    loop(NB, read, unroll=4)
    mesh_copy.wait()


def on_device(force_adjoint, paint_index, block_count, block_owner, block_tile):
    tabs = make_tables()
    names = ["z_fwd", "z_inv_t", "z_inv", "y_fwd", "y_inv", "x_fwd", "x_inv"]
    tables = [tabs[n] for n in names]
    vmem = pl.BlockSpec(memory_space=pltpu.VMEM)
    wave = pltpu.VMEM((2, NG, 128), f32)
    dma = pltpu.SemaphoreType.DMA
    mesh_grad, mass_grad = pl.pallas_call(
        step_kernel,
        out_shape=(
            jax.ShapeDtypeStruct((8, 32, NG), f32),
            jax.ShapeDtypeStruct((1, NB * BP), f32),
        ),
        in_specs=[pl.BlockSpec(memory_space=pl.ANY)] * (5 + len(names)),
        out_specs=(pl.BlockSpec(memory_space=pl.ANY), vmem),
        scratch_shapes=[
            pltpu.VMEM((3, 1, NB * BP), f32),
            pltpu.VMEM((1, NB * BP), jnp.int32),
            pltpu.SMEM((1, NB), jnp.int32),
            pltpu.SMEM((1, NB), jnp.int32),
            pltpu.SMEM((1, NB), jnp.int32),
            pltpu.VMEM((1, NB), jnp.int32),
            *[pltpu.VMEM(t.shape, bf16) for t in tables],
            pltpu.VMEM((NB, 64, BP), bf16),
            pltpu.VMEM((NB + 1, 3, 8, 128), f32),
            pltpu.VMEM((NW, 128), jnp.int32),
            pltpu.SMEM((NW, 128), jnp.int32),
            pltpu.VMEM((NW, 1, 128), jnp.int32),
            pltpu.VMEM((3, NW, 8, 128), f32),
            pltpu.VMEM((NW, 1, 128), jnp.int32),
            pltpu.VMEM((3, NW, 8, 128), f32),
            pltpu.VMEM((3, 2, NG, 128), f32),
            pltpu.VMEM((3, 2, NG, 128), f32),
            pltpu.VMEM((2, 2, NG, 128), f32),
            pltpu.VMEM((2, 2, NG, 128), f32),
            wave, wave, wave, wave,
            pltpu.VMEM((NW, 8, 128), f32),
            pltpu.VMEM((NW, 8, 128), f32),
            pltpu.VMEM((8, 32, NG), f32),
            dma((6,)), dma((7,)), dma, dma((10,)), dma((10,)), dma((6,)), dma((6,)),
        ],
        compiler_params=pltpu.CompilerParams(
            collective_id=0, has_side_effects=True, vmem_limit_bytes=60 << 20
        ),
        name="step",
    )(
        force_adjoint, paint_index, block_count, block_owner.reshape(1, NB), block_tile,
        *[jnp.asarray(t) for t in tables],
    )
    return mesh_grad, mass_grad


def solution(mesh):
    return jax.shard_map(
        on_device,
        mesh=mesh,
        in_specs=(
            P(None, "pencil", "wide"),
            P("pencil", "wide"),
            P("pencil", "wide"),
            P("pencil", "wide", None),
            P("pencil", "wide"),
        ),
        out_specs=(P("wide", "pencil", None), P("pencil", "wide")),
        check_vma=False,
    )
```

```python
import math

import jax
import jax.numpy as jnp
import ml_dtypes
import numpy as np
from jax import lax
from jax.experimental import pallas as pl
from jax.experimental.pallas import tpu as pltpu
from jax.sharding import PartitionSpec as P

NG = 256
NW = 32
NP = 8
NB = 32
BP = 512
MESH = pl.DeviceIdType.MESH
f32 = jnp.float32
bf16 = jnp.bfloat16


def roll(x, shift, axis):
    return pltpu.roll(x, shift, axis)


def halves(table):
    table = np.asarray(table, np.float32)
    high = table.astype(ml_dtypes.bfloat16)
    low = (table - high.astype(np.float32)).astype(ml_dtypes.bfloat16)
    return np.stack([high, low])


def waves(first, second):
    phase = (np.asarray(first)[:, None] * np.asarray(second)[None, :]) % NG
    angle = phase * (2.0 * math.pi / NG)
    return np.cos(angle), np.sin(angle)


def ky_of_row():
    out = []
    for w in range(NW):
        for j in range(8):
            base = 4 * w + j % 4
            out.append(base if j < 4 else (128 if base == 0 else NG - base))
    return np.array(out)


def make_tables():
    line = np.arange(NG)
    half = np.arange(NG // 2)
    sign = np.where(line % 2 == 0, 1.0, -1.0)
    c, s = waves(line, half)
    s = -s
    s[:, 0] = sign
    z_fwd = np.concatenate([c, s], axis=1)
    c, s = waves(half, line)
    weight = np.where(half == 0, 1.0, 2.0)[:, None]
    c = c * weight
    s = -2.0 * s
    s[0] = sign
    z_inv = np.concatenate([c, s], axis=0)
    ky = ky_of_row()
    c, s = waves(ky, line)
    y_fwd = np.concatenate([c, s], axis=0)
    kyt = ky.reshape(NW, 8).T.reshape(-1)
    c, s = waves(line, kyt)
    y_inv = np.concatenate([c, s], axis=0)
    xt = line.reshape(NW, 8).T.reshape(-1)
    c, s = waves(line, xt)
    x_fwd = np.concatenate([c, s], axis=0)
    c, s = waves(line, line)
    x_inv = np.concatenate([c, s], axis=0)
    return dict(
        z_fwd=halves(z_fwd),
        z_inv=halves(z_inv),
        z_inv_t=halves(z_inv.T),
        y_fwd=halves(y_fwd),
        y_inv=halves(y_inv),
        x_fwd=halves(x_fwd),
        x_inv=halves(x_inv),
    )


def dot(a, b, dims=((1,), (0,))):
    return lax.dot_general(a, b, (dims, ((), ())), preferred_element_type=f32)


def split(x):
    high = x.astype(bf16)
    return high, (x - high.astype(f32)).astype(bf16)


def dot3(a, b, dims=((1,), (0,))):
    return dot(a[0], b[0], dims) + (dot(a[0], b[1], dims) + dot(a[1], b[0], dims))


def iota(shape, axis):
    return lax.broadcasted_iota(jnp.int32, shape, axis)


def exchange(arrays):
    lane = iota(arrays[0].shape, 1)
    b = 1
    while b < len(arrays):
        bit = (lane // (8 * b)) & 1
        new = []
        for i in range(len(arrays)):
            mine = i // b % 2
            shift = 8 * b if mine == 0 else 128 - 8 * b
            new.append(jnp.where(bit == mine, arrays[i], roll(arrays[i ^ b], shift, 1)))
        arrays = new
        b *= 2
    return arrays


def one_hot_rows(ids):
    spot = (ids & 31) * 8 + (iota((NW * 8, 128), 0) & 7)
    lane = iota((NW * 8, 128), 1)
    both = jnp.concatenate(
        [jnp.where(spot == lane, 1.0, 0.0), jnp.where(spot == lane + 128, 1.0, 0.0)], axis=1
    )
    return both.astype(bf16)


def scatter_rows(field, ty0, ty1):
    upper = (iota((NW * 8, 128), 1) >= 64).astype(jnp.int32)
    turned = roll(field, 64, 1)
    first = jnp.where(upper == 0, field, turned)
    second = jnp.where(upper == 0, turned, field)
    rows = []
    for values, ty in ((first, ty0), (second, ty1)):
        rows.append(
            jnp.concatenate(
                [jnp.where(ty == upper, values, 0.0), jnp.where(ty == upper + 2, values, 0.0)],
                axis=1,
            )
        )
    return jnp.concatenate(rows, axis=0)


def pick_rows(v0, v1, ty0, ty1):
    lower = iota((NW * 8, 128), 1) < 64
    out = []
    for v, ty in ((v0, ty0), (v1, ty1)):
        half = jnp.where(ty >= 2, v[:, 128:], v[:, :128])
        out.append((half, roll(half, 64, 1)))
    first = jnp.where((ty0 & 1) == 1, out[0][1], out[0][0])
    second = jnp.where((ty1 & 1) == 1, out[1][0], out[1][1])
    return jnp.where(lower, first, second)


def y_slopes():
    row = iota((NG, 128), 0)
    base = (row >> 3) * 4 + (row & 3)
    return jnp.where((row & 4) == 0, base, -base).astype(f32)


def combine(sums, sign):
    out = []
    for k in range(0, sums.shape[1], 128):
        turned = roll(sums[NG:, k : k + 128], 64, 1)
        real = iota((NG, 128), 1) < 64
        out.append(sums[:NG, k : k + 128] + jnp.where(real, -sign * turned, sign * turned))
    return out


def solve_x(a, b, w, p, q):
    row = iota((NG, 128), 0)
    lane = iota((NG, 128), 1)
    signed = jnp.where(row < 128, row, row - NG)
    slope = jnp.where(row == 128, 0, signed).astype(f32)
    sign = jnp.where(lane < 64, 1.0, -1.0)
    cos_a, sin_a = sign * a[:NG], roll(a[NG:], 64, 1)
    cos_b, sin_b = sign * b[:NG], roll(b[NG:], 64, 1)
    here = sign * (slope * (cos_a + sin_a) + (cos_b + sin_b))
    j = lane // 8 & 7
    base = 4 * w + (j & 3)
    ny = jnp.where((base == 0) & (j == 4), 128, base)
    nz = 16 * p + 8 * q + (lane & 7)
    flat = signed * signed + ny * ny
    factor = (1.0 / NG**2) / jnp.maximum(flat + nz * nz, 1).astype(f32)
    if q:
        return factor * here
    there = (cos_b - sin_b) - slope * (cos_a - sin_a)
    swapped = jnp.where((lane & 32) == 0, roll(there, 96, 1), roll(there, 32, 1))
    there = jnp.where(base == 0, there, swapped)
    top = (1.0 / NG**2) / (flat + (NG // 2) ** 2).astype(f32)
    shared = nz == 0
    alpha = jnp.where(shared, 0.5 * (factor + top), factor)
    beta = jnp.where(shared, 0.5 * (top - factor), 0.0)
    return alpha * here + beta * there


def times_i(sums):
    turned = roll(sums[:NG], 64, 1)
    return jnp.where(iota((NG, 128), 1) < 64, -turned, turned) - sums[NG:]


def wide_peer(w, i):
    iz, ix = i // 4, i % 4
    dz = 4 + (iz + 1) // 2 * (1 - 2 * ((iz + 1) % 2))
    dx = 2 + (ix + 1) // 2 * (1 - 2 * ((ix + 1) % 2))
    return (w // 8 + dx) % 4 * 8 + (w + dz) % 8


def pencil_peer(p, i):
    dy = 2 + (i // 2 + 1) // 2 * (1 - 2 * ((i // 2 + 1) % 2))
    return (p // 2 + dy) % 4 * 2 + (p + i + i // 6) % 2


def loop(count, step, unroll=1):
    def body(i, carry):
        step(i)
        return carry

    lax.fori_loop(0, count, body, 0, unroll=unroll)


def half(ref, h):
    return ref.at[pl.ds(h, 1)]


def rows(ref, i, size):
    return ref.at[:, pl.ds(pl.multiple_of(i * size, 8), size), :]


def step_kernel(
    force_hbm, cells_hbm, count_hbm, owner_hbm, tile_hbm,
    z_fwd_hbm, z_inv_t_hbm, z_inv_hbm, y_fwd_hbm, y_inv_hbm, x_fwd_hbm, x_inv_hbm,
    mesh_ref, mass_ref,
    force, cells, count, owner, tile, owner_v,
    z_fwd, z_inv_t, z_inv, y_fwd, y_inv, x_fwd, x_inv,
    spread, tiles, pick_v, pick, ids, msg, ids_rx, msg_rx,
    snd2, rx2, snd3, rx3, snd4, rx4, snd5, rx5, snd6, rx6, mesh_v,
    arg_sem, table_sem, pick_sem, wide_out, wide_in, pencil_out, pencil_in,
):
    w = lax.axis_index("wide")
    p = lax.axis_index("pencil")

    arg_copies = [
        pltpu.make_async_copy(src, dst, arg_sem.at[i])
        for i, (src, dst) in enumerate(
            [
                (owner_hbm, owner_v), (owner_hbm, owner), (count_hbm, count), (tile_hbm, tile),
                (cells_hbm, cells), (force_hbm, force),
            ]
        )
    ]
    table_copies = [
        pltpu.make_async_copy(src, dst, table_sem.at[i])
        for i, (src, dst) in enumerate(
            [
                (z_fwd_hbm, z_fwd), (z_inv_t_hbm, z_inv_t), (y_fwd_hbm, y_fwd),
                (x_fwd_hbm, x_fwd), (x_inv_hbm, x_inv), (y_inv_hbm, y_inv), (z_inv_hbm, z_inv),
            ]
        )
    ]
    for copy in arg_copies:
        copy.start()
    barrier = pltpu.get_barrier_semaphore()
    loop(
        NW - 1,
        lambda i: pl.semaphore_signal(
            barrier, inc=1, device_id={"wide": wide_peer(w, i)}, device_id_type=MESH
        ),
    )
    loop(
        NP - 1,
        lambda i: pl.semaphore_signal(
            barrier, inc=1, device_id={"pencil": pencil_peer(p, i)}, device_id_type=MESH
        ),
    )
    for copy in table_copies:
        copy.start()

    def wide_copy(phase, src, dst, other):
        return pltpu.make_async_remote_copy(
            src_ref=src, dst_ref=dst, send_sem=wide_out.at[phase], recv_sem=wide_in.at[phase],
            device_id={"wide": other}, device_id_type=MESH,
        )

    def pencil_copy(phase, src, dst, other):
        return pltpu.make_async_remote_copy(
            src_ref=src, dst_ref=dst, send_sem=pencil_out.at[phase], recv_sem=pencil_in.at[phase],
            device_id={"pencil": other}, device_id_type=MESH,
        )

    def wide_send(phase, src, dst):
        def step(i):
            other = wide_peer(w, i)
            wide_copy(phase, rows(src, other, 8), rows(dst, w, 8), other).start()

        loop(NW - 1, step)
        here = pl.ds(pl.multiple_of(w * 8, 8), 8)
        dst[:, here, :] = src[:, here, :]

    def wide_all(phase, src, dst):
        part = pl.ds(0, (NW - 1) * 8)
        return wide_copy(phase, src.at[:, part, :], dst.at[:, part, :], (w + 1) % NW)

    def pencil_send(phase, src, dst):
        def step(i):
            other = pencil_peer(p, i)
            pencil_copy(phase, rows(src, other, 32), rows(dst, p, 32), other).start()

        loop(NP - 1, step)
        here = pl.ds(pl.multiple_of(p * 32, 32), 32)
        dst[:, here, :] = src[:, here, :]

    def pencil_all(phase, src, dst):
        part = pl.ds(0, (NP - 1) * 32)
        return pencil_copy(phase, src.at[:, part, :], dst.at[:, part, :], (p + 1) % NP)

    arg_copies[0].wait()
    block = iota((NW, NB), 1)
    match = owner_v[...] == iota((NW, NB), 0)
    first = jnp.min(jnp.where(match, block, NB), axis=1, keepdims=True)
    last = jnp.max(jnp.where(match, block, -1), axis=1, keepdims=True)
    second = jnp.where(last > first, last, NB)
    pick_v[...] = jnp.where(iota((NW, 128), 1) == 0, first, second)
    pick_copy = pltpu.make_async_copy(pick_v, pick, pick_sem)
    pick_copy.start()

    for copy in arg_copies[1:]:
        copy.wait()
    tiles[NB] = jnp.zeros((3, 8, 128), f32)

    def slots(b):
        return pl.ds(pl.multiple_of(b * BP, BP), BP)

    def kept(b):
        live = iota((1, BP), 1) < count[0, b]
        return (iota((8, BP), 0) == (cells[0:1, slots(b)] & 7)) & live

    def paint(b):
        key = cells[0:1, slots(b)] >> 3
        hot = jnp.where(iota((64, BP), 0) == key, 1.0, 0.0).astype(bf16)
        spread[b] = hot
        keep = kept(b)
        high, low = [], []
        for f in range(3):
            amount = force[f, 0:1, slots(b)]
            top = amount.astype(bf16).astype(f32)
            high.append(jnp.where(keep, top, 0.0))
            low.append(jnp.where(keep, amount - top, 0.0))
        out = dot(jnp.concatenate(high + low, axis=0).astype(bf16), hot, ((1,), (1,)))
        out = out[:24] + out[24:]
        tiles[b] = jnp.concatenate([out, out], axis=1).reshape(3, 8, 128)

    loop(NB, paint, unroll=4)
    pick_copy.wait()
    pl.semaphore_wait(barrier, NW - 1 + NP - 1)

    left = iota((8, 128), 1) < 64

    def assemble(f, o):
        msg[f, o] = jnp.where(left, tiles[pick[o, 0], f], tiles[pick[o, 1], f])

    def number(o):
        name = []
        for s in range(2):
            b = pick[o, s]
            name.append(jnp.where(b < NB, tile[0, jnp.minimum(b, NB - 1)], -1))
        ids[o] = jnp.where(iota((1, 128), 1) < 64, name[0], name[1])

    def send_first(i):
        other = wide_peer(w, i)
        number(other)
        wide_copy(0, ids.at[other], ids_rx.at[w], other).start()
        assemble(0, other)
        wide_copy(1, msg.at[0, other], msg_rx.at[0, w], other).start()

    loop(NW - 1, send_first)
    for f in (1, 2):

        def send_field(i, f=f):
            other = wide_peer(w, i)
            assemble(f, other)
            wide_copy(1 + f, msg.at[f, other], msg_rx.at[f, w], other).start()

        loop(NW - 1, send_field)
    number(w)
    ids_rx[w] = ids[w]
    for f in range(3):
        assemble(f, w)
        msg_rx[f, w] = msg[f, w]
    others = pl.ds(0, NW - 1)
    ids_all = wide_copy(0, ids.at[others], ids_rx.at[others], (w + 1) % NW)
    msg_all = [
        wide_copy(1 + f, msg.at[f, others], msg_rx.at[f, others], (w + 1) % NW) for f in range(3)
    ]
    ids_all.wait_recv()
    pair = jnp.broadcast_to(ids_rx[...], (NW, 8, 128)).reshape(NW * 8, 128)
    turned = roll(pair, 64, 1)
    lower = iota((NW * 8, 128), 1) < 64
    ids0, ids1 = jnp.where(lower, pair, turned), jnp.where(lower, turned, pair)
    chosen = jnp.concatenate([one_hot_rows(ids0), one_hot_rows(ids1)], axis=0)
    table_copies[0].wait()
    g_fwd = [dot(chosen, z_fwd[i]).astype(bf16) for i in range(2)]
    ty0, ty1 = ids0 >> 5, ids1 >> 5

    kz = (iota((NG, 256), 1) & 127).astype(f32)

    def z_lines(f):
        msg_all[f].wait_recv()
        field = msg_rx[f].reshape(NW * 8, 128)
        lines = dot3(split(scatter_rows(field, ty0, ty1)), g_fwd, ((0,), (0,)))
        if f == 2:
            lines = lines * kz
        by_x = [
            jnp.concatenate(
                [
                    lines[ty * 64 + cx * 8 : ty * 64 + cx * 8 + 8, c * 128 : c * 128 + 128]
                    for ty in range(4)
                ],
                axis=0,
            )
            for c in range(2)
            for cx in range(8)
        ]
        for i, value in enumerate(exchange(by_x)):
            snd2[f, i % 2, i // 2 * 32 : i // 2 * 32 + 32, :] = value
        if f == 1:
            pencil_send(2, snd2.at[f], rx2.at[f])
        else:
            for q in range(2):
                pencil_send(3 * f // 2 + q, half(snd2.at[f], q), half(rx2.at[f], q))

    slope = y_slopes()

    def y_lines(f, q):
        pencil_all(3 * f // 2 + q, half(snd2.at[f], q), half(rx2.at[f], q)).wait_recv()
        return combine(dot3((y_fwd[0], y_fwd[1]), split(rx2[f, q])), -1.0)[0]

    z_lines(0)
    z_lines(1)
    table_copies[2].wait()
    snd3[0, 0] = y_lines(0, 0)
    wide_send(4, half(snd3.at[0], 0), half(rx3.at[0], 0))
    z_lines(2)
    snd3[0, 1] = y_lines(0, 1)
    wide_send(5, half(snd3.at[0], 1), half(rx3.at[0], 1))
    table_copies[1].wait()
    g_inv = [dot(chosen, z_inv_t[i]).astype(bf16) for i in range(2)]
    pencil_all(2, snd2.at[1], rx2.at[1]).wait_recv()
    both = jnp.concatenate([rx2[1, 0], rx2[1, 1]], axis=1)
    for q, value in enumerate(combine(dot3((y_fwd[0], y_fwd[1]), split(both)), -1.0)):
        snd3[1, q] = slope * value
    for q in range(2):
        snd3[1, q] += y_lines(2, q)
        wide_send(6 + q, half(snd3.at[1], q), half(rx3.at[1], q))

    table_copies[3].wait()
    table_copies[4].wait()

    def x_lines(i, q):
        wide_all(4 + 2 * i + q, half(snd3.at[i], q), half(rx3.at[i], q)).wait_recv()
        parts = exchange([rx3[i, q, pl.ds(j, NW, stride=8), :] for j in range(8)])
        return jnp.concatenate(parts, axis=0)

    both = jnp.concatenate([x_lines(0, 0), x_lines(0, 1)], axis=1)
    first = dot3((x_fwd[0], x_fwd[1]), split(both))
    for q in range(2):
        second = dot3((x_fwd[0], x_fwd[1]), split(x_lines(1, q)))
        solved = solve_x(first[:, q * 128 : q * 128 + 128], second, w, p, q)
        snd4[q] = times_i(dot3((x_inv[0], x_inv[1]), split(solved)))
        wide_send(8 + q, half(snd4, q), half(rx4, q))

    table_copies[5].wait()
    for q in range(2):
        wide_all(8 + q, half(snd4, q), half(rx4, q)).wait_recv()
        parts = exchange([rx4[q, pl.ds(cx, NW, stride=8), :] for cx in range(8)])
        sums = dot3((y_inv[0], y_inv[1]), split(jnp.concatenate(parts, axis=0)))
        snd5[q] = combine(sums, 1.0)[0]
        pencil_send(5 + q, half(snd5, q), half(rx5, q))

    table_copies[6].wait()
    for q in range(2):
        pencil_all(5 + q, half(snd5, q), half(rx5, q)).wait_recv()
    by_x = exchange([rx5[i % 2, i // 2 * 32 : i // 2 * 32 + 32, :] for i in range(16)])
    lines = split(
        jnp.concatenate(
            [
                jnp.concatenate(
                    [by_x[8 * c + cx][ty * 8 : ty * 8 + 8] for ty in range(4) for cx in range(8)],
                    axis=0,
                )
                for c in range(2)
            ],
            axis=1,
        )
    )
    values = dot3(g_inv, lines, ((1,), (1,)))
    snd6[...] = pick_rows(values[: NW * 8], values[NW * 8 :], ty0, ty1).reshape(NW, 8, 128)

    def send_back(i):
        other = wide_peer(w, i)
        wide_copy(10, snd6.at[other], rx6.at[w], other).start()

    loop(NW - 1, send_back)
    rx6[w] = snd6[w]
    mesh = dot3(lines, (z_inv[0], z_inv[1]))
    for ty in range(4):
        for cx in range(8):
            mesh_v[cx, ty * 8 : ty * 8 + 8, :] = mesh[ty * 64 + cx * 8 : ty * 64 + cx * 8 + 8]
    mesh_copy = pltpu.make_async_copy(mesh_v, mesh_ref, pick_sem)
    mesh_copy.start()
    ids_all.wait_send()
    for f in range(3):
        msg_all[f].wait_send()
    pencil_all(2, snd2.at[1], rx2.at[1]).wait_send()
    for q in range(2):
        for f in (0, 2):
            pencil_all(3 * f // 2 + q, half(snd2.at[f], q), half(rx2.at[f], q)).wait_send()
        for i in range(2):
            wide_all(4 + 2 * i + q, half(snd3.at[i], q), half(rx3.at[i], q)).wait_send()
        wide_all(8 + q, half(snd4, q), half(rx4, q)).wait_send()
        pencil_all(5 + q, half(snd5, q), half(rx5, q)).wait_send()
    wide_copy(10, snd6.at[others], rx6.at[others], (w + 1) % NW).wait()

    def read(b):
        o = owner[0, b]
        pair = rx6[o]
        here = jnp.where(pick[o, 0] == b, pair, roll(pair, 64, 1))
        tile_in = here[:, :64]
        top = tile_in.astype(bf16).astype(f32)
        out = dot(jnp.concatenate([top, tile_in - top], axis=0).astype(bf16), spread[b])
        value = jnp.sum(jnp.where(kept(b), out[:8] + out[8:], 0.0), axis=0, keepdims=True)
        mass_ref[0:1, slots(b)] = value

    loop(NB, read, unroll=4)
    mesh_copy.wait()


def on_device(force_adjoint, paint_index, block_count, block_owner, block_tile):
    tabs = make_tables()
    names = ["z_fwd", "z_inv_t", "z_inv", "y_fwd", "y_inv", "x_fwd", "x_inv"]
    tables = [tabs[n] for n in names]
    vmem = pl.BlockSpec(memory_space=pltpu.VMEM)
    wave = pltpu.VMEM((2, NG, 128), f32)
    dma = pltpu.SemaphoreType.DMA
    mesh_grad, mass_grad = pl.pallas_call(
        step_kernel,
        out_shape=(
            jax.ShapeDtypeStruct((8, 32, NG), f32),
            jax.ShapeDtypeStruct((1, NB * BP), f32),
        ),
        in_specs=[pl.BlockSpec(memory_space=pl.ANY)] * (5 + len(names)),
        out_specs=(pl.BlockSpec(memory_space=pl.ANY), vmem),
        scratch_shapes=[
            pltpu.VMEM((3, 1, NB * BP), f32),
            pltpu.VMEM((1, NB * BP), jnp.int32),
            pltpu.SMEM((1, NB), jnp.int32),
            pltpu.SMEM((1, NB), jnp.int32),
            pltpu.SMEM((1, NB), jnp.int32),
            pltpu.VMEM((1, NB), jnp.int32),
            *[pltpu.VMEM(t.shape, bf16) for t in tables],
            pltpu.VMEM((NB, 64, BP), bf16),
            pltpu.VMEM((NB + 1, 3, 8, 128), f32),
            pltpu.VMEM((NW, 128), jnp.int32),
            pltpu.SMEM((NW, 128), jnp.int32),
            pltpu.VMEM((NW, 1, 128), jnp.int32),
            pltpu.VMEM((3, NW, 8, 128), f32),
            pltpu.VMEM((NW, 1, 128), jnp.int32),
            pltpu.VMEM((3, NW, 8, 128), f32),
            pltpu.VMEM((3, 2, NG, 128), f32),
            pltpu.VMEM((3, 2, NG, 128), f32),
            pltpu.VMEM((2, 2, NG, 128), f32),
            pltpu.VMEM((2, 2, NG, 128), f32),
            wave, wave, wave, wave,
            pltpu.VMEM((NW, 8, 128), f32),
            pltpu.VMEM((NW, 8, 128), f32),
            pltpu.VMEM((8, 32, NG), f32),
            dma((6,)), dma((7,)), dma, dma((11,)), dma((11,)), dma((7,)), dma((7,)),
        ],
        compiler_params=pltpu.CompilerParams(
            collective_id=0, has_side_effects=True, vmem_limit_bytes=60 << 20
        ),
        name="step",
    )(
        force_adjoint, paint_index, block_count, block_owner.reshape(1, NB), block_tile,
        *[jnp.asarray(t) for t in tables],
    )
    return mesh_grad, mass_grad


def solution(mesh):
    return jax.shard_map(
        on_device,
        mesh=mesh,
        in_specs=(
            P(None, "pencil", "wide"),
            P("pencil", "wide"),
            P("pencil", "wide"),
            P("pencil", "wide", None),
            P("pencil", "wide"),
        ),
        out_specs=(P("wide", "pencil", None), P("pencil", "wide")),
        check_vma=False,
    )
```

```python
import math

import jax
import jax.numpy as jnp
import ml_dtypes
import numpy as np
from jax import lax
from jax.experimental import pallas as pl
from jax.experimental.pallas import tpu as pltpu
from jax.sharding import PartitionSpec as P

NG = 256
NW = 32
NP = 8
NB = 32
BP = 512
MESH = pl.DeviceIdType.MESH
f32 = jnp.float32
bf16 = jnp.bfloat16


def roll(x, shift, axis):
    return pltpu.roll(x, shift, axis)


def halves(table):
    table = np.asarray(table, np.float32)
    high = table.astype(ml_dtypes.bfloat16)
    low = (table - high.astype(np.float32)).astype(ml_dtypes.bfloat16)
    return np.stack([high, low])


def waves(first, second):
    phase = (np.asarray(first)[:, None] * np.asarray(second)[None, :]) % NG
    angle = phase * (2.0 * math.pi / NG)
    return np.cos(angle), np.sin(angle)


def ky_of_row():
    out = []
    for w in range(NW):
        for j in range(8):
            base = 4 * w + j % 4
            out.append(base if j < 4 else (128 if base == 0 else NG - base))
    return np.array(out)


def make_tables():
    line = np.arange(NG)
    half = np.arange(NG // 2)
    sign = np.where(line % 2 == 0, 1.0, -1.0)
    c, s = waves(line, half)
    s = -s
    s[:, 0] = sign
    z_fwd = np.concatenate([c, s], axis=1)
    c, s = waves(half, line)
    weight = np.where(half == 0, 1.0, 2.0)[:, None]
    c = c * weight
    s = -2.0 * s
    s[0] = sign
    z_inv = np.concatenate([c, s], axis=0)
    ky = ky_of_row()
    c, s = waves(ky, line)
    y_fwd = np.concatenate([c, s], axis=0)
    kyt = ky.reshape(NW, 8).T.reshape(-1)
    c, s = waves(line, kyt)
    y_inv = np.concatenate([c, s], axis=0)
    xt = line.reshape(NW, 8).T.reshape(-1)
    c, s = waves(line, xt)
    x_fwd = np.concatenate([c, s], axis=0)
    c, s = waves(line, line)
    x_inv = np.concatenate([c, s], axis=0)
    return dict(
        z_fwd=halves(z_fwd),
        z_inv=halves(z_inv),
        z_inv_t=halves(z_inv.T),
        y_fwd=halves(y_fwd),
        y_inv=halves(y_inv),
        x_fwd=halves(x_fwd),
        x_inv=halves(x_inv),
    )


def dot(a, b, dims=((1,), (0,))):
    return lax.dot_general(a, b, (dims, ((), ())), preferred_element_type=f32)


def split(x):
    high = x.astype(bf16)
    return high, (x - high.astype(f32)).astype(bf16)


def dot3(a, b, dims=((1,), (0,))):
    return dot(a[0], b[0], dims) + (dot(a[0], b[1], dims) + dot(a[1], b[0], dims))


def iota(shape, axis):
    return lax.broadcasted_iota(jnp.int32, shape, axis)


def exchange(arrays):
    lane = iota(arrays[0].shape, 1)
    b = 1
    while b < len(arrays):
        bit = (lane // (8 * b)) & 1
        new = []
        for i in range(len(arrays)):
            mine = i // b % 2
            shift = 8 * b if mine == 0 else 128 - 8 * b
            new.append(jnp.where(bit == mine, arrays[i], roll(arrays[i ^ b], shift, 1)))
        arrays = new
        b *= 2
    return arrays


def one_hot_rows(ids):
    spot = (ids & 31) * 8 + (iota((NW * 8, 128), 0) & 7)
    lane = iota((NW * 8, 128), 1)
    both = jnp.concatenate(
        [jnp.where(spot == lane, 1.0, 0.0), jnp.where(spot == lane + 128, 1.0, 0.0)], axis=1
    )
    return both.astype(bf16)


def scatter_rows(field, ty0, ty1):
    upper = (iota((NW * 8, 128), 1) >= 64).astype(jnp.int32)
    turned = roll(field, 64, 1)
    first = jnp.where(upper == 0, field, turned)
    second = jnp.where(upper == 0, turned, field)
    rows = []
    for values, ty in ((first, ty0), (second, ty1)):
        rows.append(
            jnp.concatenate(
                [jnp.where(ty == upper, values, 0.0), jnp.where(ty == upper + 2, values, 0.0)],
                axis=1,
            )
        )
    return jnp.concatenate(rows, axis=0)


def pick_rows(v0, v1, ty0, ty1):
    lower = iota((NW * 8, 128), 1) < 64
    out = []
    for v, ty in ((v0, ty0), (v1, ty1)):
        half = jnp.where(ty >= 2, v[:, 128:], v[:, :128])
        out.append((half, roll(half, 64, 1)))
    first = jnp.where((ty0 & 1) == 1, out[0][1], out[0][0])
    second = jnp.where((ty1 & 1) == 1, out[1][0], out[1][1])
    return jnp.where(lower, first, second)


def y_slopes():
    row = iota((NG, 128), 0)
    base = (row >> 3) * 4 + (row & 3)
    return jnp.where((row & 4) == 0, base, -base).astype(f32)


def combine(sums, sign):
    out = []
    for k in range(0, sums.shape[1], 128):
        turned = roll(sums[NG:, k : k + 128], 64, 1)
        real = iota((NG, 128), 1) < 64
        out.append(sums[:NG, k : k + 128] + jnp.where(real, -sign * turned, sign * turned))
    return out


def solve_x(a, b, w, p, q):
    row = iota((NG, 128), 0)
    lane = iota((NG, 128), 1)
    signed = jnp.where(row < 128, row, row - NG)
    slope = jnp.where(row == 128, 0, signed).astype(f32)
    sign = jnp.where(lane < 64, 1.0, -1.0)
    cos_a, sin_a = sign * a[:NG], roll(a[NG:], 64, 1)
    cos_b, sin_b = sign * b[:NG], roll(b[NG:], 64, 1)
    here = sign * (slope * (cos_a + sin_a) + (cos_b + sin_b))
    j = lane // 8 & 7
    base = 4 * w + (j & 3)
    ny = jnp.where((base == 0) & (j == 4), 128, base)
    nz = 16 * p + 8 * q + (lane & 7)
    flat = signed * signed + ny * ny
    factor = (1.0 / NG**2) / jnp.maximum(flat + nz * nz, 1).astype(f32)
    if q:
        return factor * here
    there = (cos_b - sin_b) - slope * (cos_a - sin_a)
    swapped = jnp.where((lane & 32) == 0, roll(there, 96, 1), roll(there, 32, 1))
    there = jnp.where(base == 0, there, swapped)
    top = (1.0 / NG**2) / (flat + (NG // 2) ** 2).astype(f32)
    shared = nz == 0
    alpha = jnp.where(shared, 0.5 * (factor + top), factor)
    beta = jnp.where(shared, 0.5 * (top - factor), 0.0)
    return alpha * here + beta * there


def times_i(sums):
    turned = roll(sums[:NG], 64, 1)
    return jnp.where(iota((NG, 128), 1) < 64, -turned, turned) - sums[NG:]


def wide_peer(w, i):
    iz, ix = i // 4, i % 4
    dz = 4 + (iz + 1) // 2 * (1 - 2 * ((iz + 1) % 2))
    dx = 2 + (ix + 1) // 2 * (1 - 2 * ((ix + 1) % 2))
    return (w // 8 + dx) % 4 * 8 + (w + dz) % 8


def pencil_peer(p, i):
    dy = 2 + (i // 2 + 1) // 2 * (1 - 2 * ((i // 2 + 1) % 2))
    return (p // 2 + dy) % 4 * 2 + (p + i + i // 6) % 2


def loop(count, step, unroll=1):
    def body(i, carry):
        step(i)
        return carry

    lax.fori_loop(0, count, body, 0, unroll=unroll)


def half(ref, h):
    return ref.at[pl.ds(h, 1)]


def rows(ref, i, size):
    return ref.at[:, pl.ds(pl.multiple_of(i * size, 8), size), :]


def step_kernel(
    force_hbm, cells_hbm, count_hbm, owner_hbm, tile_hbm,
    z_fwd_hbm, z_inv_t_hbm, z_inv_hbm, y_fwd_hbm, y_inv_hbm, x_fwd_hbm, x_inv_hbm,
    mesh_ref, mass_ref,
    force, cells, count, owner, tile, owner_v,
    z_fwd, z_inv_t, z_inv, y_fwd, y_inv, x_fwd, x_inv,
    spread, tiles, pick_v, pick, ids, msg, ids_rx, msg_rx,
    snd2, rx2, snd3, rx3, snd4, rx4, snd5, rx5, snd6, rx6, mesh_v,
    arg_sem, table_sem, pick_sem, wide_out, wide_in, pencil_out, pencil_in,
):
    w = lax.axis_index("wide")
    p = lax.axis_index("pencil")

    arg_copies = [
        pltpu.make_async_copy(src, dst, arg_sem.at[i])
        for i, (src, dst) in enumerate(
            [
                (owner_hbm, owner_v), (owner_hbm, owner), (count_hbm, count), (tile_hbm, tile),
                (cells_hbm, cells), (force_hbm, force),
            ]
        )
    ]
    table_copies = [
        pltpu.make_async_copy(src, dst, table_sem.at[i])
        for i, (src, dst) in enumerate(
            [
                (z_fwd_hbm, z_fwd), (z_inv_t_hbm, z_inv_t), (y_fwd_hbm, y_fwd),
                (x_fwd_hbm, x_fwd), (x_inv_hbm, x_inv), (y_inv_hbm, y_inv), (z_inv_hbm, z_inv),
            ]
        )
    ]
    for copy in arg_copies:
        copy.start()
    barrier = pltpu.get_barrier_semaphore()
    loop(
        NW - 1,
        lambda i: pl.semaphore_signal(
            barrier, inc=1, device_id={"wide": wide_peer(w, i)}, device_id_type=MESH
        ),
    )
    loop(
        NP - 1,
        lambda i: pl.semaphore_signal(
            barrier, inc=1, device_id={"pencil": pencil_peer(p, i)}, device_id_type=MESH
        ),
    )
    for copy in table_copies:
        copy.start()

    def wide_copy(phase, src, dst, other):
        return pltpu.make_async_remote_copy(
            src_ref=src, dst_ref=dst, send_sem=wide_out.at[phase], recv_sem=wide_in.at[phase],
            device_id={"wide": other}, device_id_type=MESH,
        )

    def pencil_copy(phase, src, dst, other):
        return pltpu.make_async_remote_copy(
            src_ref=src, dst_ref=dst, send_sem=pencil_out.at[phase], recv_sem=pencil_in.at[phase],
            device_id={"pencil": other}, device_id_type=MESH,
        )

    def wide_send(phase, src, dst):
        def step(i):
            other = wide_peer(w, i)
            wide_copy(phase, rows(src, other, 8), rows(dst, w, 8), other).start()

        loop(NW - 1, step)
        here = pl.ds(pl.multiple_of(w * 8, 8), 8)
        dst[:, here, :] = src[:, here, :]

    def wide_all(phase, src, dst):
        part = pl.ds(0, (NW - 1) * 8)
        return wide_copy(phase, src.at[:, part, :], dst.at[:, part, :], (w + 1) % NW)

    def pencil_send(phase, src, dst):
        def step(i):
            other = pencil_peer(p, i)
            pencil_copy(phase, rows(src, other, 32), rows(dst, p, 32), other).start()

        loop(NP - 1, step)
        here = pl.ds(pl.multiple_of(p * 32, 32), 32)
        dst[:, here, :] = src[:, here, :]

    def pencil_all(phase, src, dst):
        part = pl.ds(0, (NP - 1) * 32)
        return pencil_copy(phase, src.at[:, part, :], dst.at[:, part, :], (p + 1) % NP)

    arg_copies[0].wait()
    block = iota((NW, NB), 1)
    match = owner_v[...] == iota((NW, NB), 0)
    first = jnp.min(jnp.where(match, block, NB), axis=1, keepdims=True)
    last = jnp.max(jnp.where(match, block, -1), axis=1, keepdims=True)
    second = jnp.where(last > first, last, NB)
    pick_v[...] = jnp.where(iota((NW, 128), 1) == 0, first, second)
    pick_copy = pltpu.make_async_copy(pick_v, pick, pick_sem)
    pick_copy.start()

    for copy in arg_copies[1:]:
        copy.wait()
    tiles[NB] = jnp.zeros((3, 8, 128), f32)

    def slots(b):
        return pl.ds(pl.multiple_of(b * BP, BP), BP)

    def kept(b):
        live = iota((1, BP), 1) < count[0, b]
        return (iota((8, BP), 0) == (cells[0:1, slots(b)] & 7)) & live

    def paint(b):
        key = cells[0:1, slots(b)] >> 3
        hot = jnp.where(iota((64, BP), 0) == key, 1.0, 0.0).astype(bf16)
        spread[b] = hot
        keep = kept(b)
        high, low = [], []
        for f in range(3):
            amount = force[f, 0:1, slots(b)]
            top = amount.astype(bf16).astype(f32)
            high.append(jnp.where(keep, top, 0.0))
            low.append(jnp.where(keep, amount - top, 0.0))
        out = dot(jnp.concatenate(high + low, axis=0).astype(bf16), hot, ((1,), (1,)))
        out = out[:24] + out[24:]
        tiles[b] = jnp.concatenate([out, out], axis=1).reshape(3, 8, 128)

    loop(NB, paint, unroll=16)
    pick_copy.wait()
    pl.semaphore_wait(barrier, NW - 1 + NP - 1)

    left = iota((8, 128), 1) < 64

    def assemble(f, o):
        msg[f, o] = jnp.where(left, tiles[pick[o, 0], f], tiles[pick[o, 1], f])

    def number(o):
        name = []
        for s in range(2):
            b = pick[o, s]
            name.append(jnp.where(b < NB, tile[0, jnp.minimum(b, NB - 1)], -1))
        ids[o] = jnp.where(iota((1, 128), 1) < 64, name[0], name[1])

    def send_first(i):
        other = wide_peer(w, i)
        number(other)
        wide_copy(0, ids.at[other], ids_rx.at[w], other).start()
        assemble(0, other)
        wide_copy(1, msg.at[0, other], msg_rx.at[0, w], other).start()

    loop(NW - 1, send_first)
    for f in (1, 2):

        def send_field(i, f=f):
            other = wide_peer(w, i)
            assemble(f, other)
            wide_copy(1 + f, msg.at[f, other], msg_rx.at[f, w], other).start()

        loop(NW - 1, send_field)
    number(w)
    ids_rx[w] = ids[w]
    for f in range(3):
        assemble(f, w)
        msg_rx[f, w] = msg[f, w]
    others = pl.ds(0, NW - 1)
    ids_all = wide_copy(0, ids.at[others], ids_rx.at[others], (w + 1) % NW)
    msg_all = [
        wide_copy(1 + f, msg.at[f, others], msg_rx.at[f, others], (w + 1) % NW) for f in range(3)
    ]
    ids_all.wait_recv()
    pair = jnp.broadcast_to(ids_rx[...], (NW, 8, 128)).reshape(NW * 8, 128)
    turned = roll(pair, 64, 1)
    lower = iota((NW * 8, 128), 1) < 64
    ids0, ids1 = jnp.where(lower, pair, turned), jnp.where(lower, turned, pair)
    chosen = jnp.concatenate([one_hot_rows(ids0), one_hot_rows(ids1)], axis=0)
    table_copies[0].wait()
    g_fwd = [dot(chosen, z_fwd[i]).astype(bf16) for i in range(2)]
    ty0, ty1 = ids0 >> 5, ids1 >> 5

    kz = (iota((NG, 256), 1) & 127).astype(f32)

    def z_lines(f):
        msg_all[f].wait_recv()
        field = msg_rx[f].reshape(NW * 8, 128)
        lines = dot3(split(scatter_rows(field, ty0, ty1).T), g_fwd)
        if f == 2:
            lines = lines * kz
        by_x = [
            jnp.concatenate(
                [
                    lines[ty * 64 + cx * 8 : ty * 64 + cx * 8 + 8, c * 128 : c * 128 + 128]
                    for ty in range(4)
                ],
                axis=0,
            )
            for c in range(2)
            for cx in range(8)
        ]
        for i, value in enumerate(exchange(by_x)):
            snd2[f, i % 2, i // 2 * 32 : i // 2 * 32 + 32, :] = value
        if f == 1:
            pencil_send(2, snd2.at[f], rx2.at[f])
        else:
            for q in range(2):
                pencil_send(3 * f // 2 + q, half(snd2.at[f], q), half(rx2.at[f], q))

    slope = y_slopes()

    def y_lines(f, q):
        pencil_all(3 * f // 2 + q, half(snd2.at[f], q), half(rx2.at[f], q)).wait_recv()
        return combine(dot3((y_fwd[0], y_fwd[1]), split(rx2[f, q])), -1.0)[0]

    z_lines(0)
    z_lines(1)
    z_lines(2)
    table_copies[2].wait()
    for q in range(2):
        snd3[0, q] = y_lines(0, q)
        wide_send(4 + q, half(snd3.at[0], q), half(rx3.at[0], q))
    table_copies[1].wait()
    g_inv = [dot(chosen, z_inv_t[i]).astype(bf16) for i in range(2)]
    pencil_all(2, snd2.at[1], rx2.at[1]).wait_recv()
    both = jnp.concatenate([rx2[1, 0], rx2[1, 1]], axis=1)
    for q, value in enumerate(combine(dot3((y_fwd[0], y_fwd[1]), split(both)), -1.0)):
        snd3[1, q] = slope * value
    for q in range(2):
        snd3[1, q] += y_lines(2, q)
        wide_send(6 + q, half(snd3.at[1], q), half(rx3.at[1], q))

    table_copies[3].wait()
    table_copies[4].wait()

    def x_lines(i, q):
        wide_all(4 + 2 * i + q, half(snd3.at[i], q), half(rx3.at[i], q)).wait_recv()
        parts = exchange([rx3[i, q, pl.ds(j, NW, stride=8), :] for j in range(8)])
        return jnp.concatenate(parts, axis=0)

    both = jnp.concatenate([x_lines(0, 0), x_lines(0, 1)], axis=1)
    first = dot3((x_fwd[0], x_fwd[1]), split(both))
    for q in range(2):
        second = dot3((x_fwd[0], x_fwd[1]), split(x_lines(1, q)))
        solved = solve_x(first[:, q * 128 : q * 128 + 128], second, w, p, q)
        snd4[q] = times_i(dot3((x_inv[0], x_inv[1]), split(solved)))
        wide_send(8 + q, half(snd4, q), half(rx4, q))

    table_copies[5].wait()
    for q in range(2):
        wide_all(8 + q, half(snd4, q), half(rx4, q)).wait_recv()
        parts = exchange([rx4[q, pl.ds(cx, NW, stride=8), :] for cx in range(8)])
        sums = dot3((y_inv[0], y_inv[1]), split(jnp.concatenate(parts, axis=0)))
        snd5[q] = combine(sums, 1.0)[0]
        pencil_send(5 + q, half(snd5, q), half(rx5, q))

    table_copies[6].wait()
    for q in range(2):
        pencil_all(5 + q, half(snd5, q), half(rx5, q)).wait_recv()
    by_x = exchange([rx5[i % 2, i // 2 * 32 : i // 2 * 32 + 32, :] for i in range(16)])
    lines = split(
        jnp.concatenate(
            [
                jnp.concatenate(
                    [by_x[8 * c + cx][ty * 8 : ty * 8 + 8] for ty in range(4) for cx in range(8)],
                    axis=0,
                )
                for c in range(2)
            ],
            axis=1,
        )
    )
    values = dot3(g_inv, lines, ((1,), (1,)))
    snd6[...] = pick_rows(values[: NW * 8], values[NW * 8 :], ty0, ty1).reshape(NW, 8, 128)

    def send_back(i):
        other = wide_peer(w, i)
        wide_copy(10, snd6.at[other], rx6.at[w], other).start()

    loop(NW - 1, send_back)
    rx6[w] = snd6[w]
    mesh = dot3(lines, (z_inv[0], z_inv[1]))
    for ty in range(4):
        for cx in range(8):
            mesh_v[cx, ty * 8 : ty * 8 + 8, :] = mesh[ty * 64 + cx * 8 : ty * 64 + cx * 8 + 8]
    mesh_copy = pltpu.make_async_copy(mesh_v, mesh_ref, pick_sem)
    mesh_copy.start()
    ids_all.wait_send()
    for f in range(3):
        msg_all[f].wait_send()
    pencil_all(2, snd2.at[1], rx2.at[1]).wait_send()
    for q in range(2):
        for f in (0, 2):
            pencil_all(3 * f // 2 + q, half(snd2.at[f], q), half(rx2.at[f], q)).wait_send()
        for i in range(2):
            wide_all(4 + 2 * i + q, half(snd3.at[i], q), half(rx3.at[i], q)).wait_send()
        wide_all(8 + q, half(snd4, q), half(rx4, q)).wait_send()
        pencil_all(5 + q, half(snd5, q), half(rx5, q)).wait_send()
    wide_copy(10, snd6.at[others], rx6.at[others], (w + 1) % NW).wait()

    def read(b):
        o = owner[0, b]
        pair = rx6[o]
        here = jnp.where(pick[o, 0] == b, pair, roll(pair, 64, 1))
        tile_in = here[:, :64]
        top = tile_in.astype(bf16).astype(f32)
        out = dot(jnp.concatenate([top, tile_in - top], axis=0).astype(bf16), spread[b])
        value = jnp.sum(jnp.where(kept(b), out[:8] + out[8:], 0.0), axis=0, keepdims=True)
        mass_ref[0:1, slots(b)] = value

    loop(NB, read, unroll=16)
    mesh_copy.wait()


def on_device(force_adjoint, paint_index, block_count, block_owner, block_tile):
    tabs = make_tables()
    names = ["z_fwd", "z_inv_t", "z_inv", "y_fwd", "y_inv", "x_fwd", "x_inv"]
    tables = [tabs[n] for n in names]
    vmem = pl.BlockSpec(memory_space=pltpu.VMEM)
    wave = pltpu.VMEM((2, NG, 128), f32)
    dma = pltpu.SemaphoreType.DMA
    mesh_grad, mass_grad = pl.pallas_call(
        step_kernel,
        out_shape=(
            jax.ShapeDtypeStruct((8, 32, NG), f32),
            jax.ShapeDtypeStruct((1, NB * BP), f32),
        ),
        in_specs=[pl.BlockSpec(memory_space=pl.ANY)] * (5 + len(names)),
        out_specs=(pl.BlockSpec(memory_space=pl.ANY), vmem),
        scratch_shapes=[
            pltpu.VMEM((3, 1, NB * BP), f32),
            pltpu.VMEM((1, NB * BP), jnp.int32),
            pltpu.SMEM((1, NB), jnp.int32),
            pltpu.SMEM((1, NB), jnp.int32),
            pltpu.SMEM((1, NB), jnp.int32),
            pltpu.VMEM((1, NB), jnp.int32),
            *[pltpu.VMEM(t.shape, bf16) for t in tables],
            pltpu.VMEM((NB, 64, BP), bf16),
            pltpu.VMEM((NB + 1, 3, 8, 128), f32),
            pltpu.VMEM((NW, 128), jnp.int32),
            pltpu.SMEM((NW, 128), jnp.int32),
            pltpu.VMEM((NW, 1, 128), jnp.int32),
            pltpu.VMEM((3, NW, 8, 128), f32),
            pltpu.VMEM((NW, 1, 128), jnp.int32),
            pltpu.VMEM((3, NW, 8, 128), f32),
            pltpu.VMEM((3, 2, NG, 128), f32),
            pltpu.VMEM((3, 2, NG, 128), f32),
            pltpu.VMEM((2, 2, NG, 128), f32),
            pltpu.VMEM((2, 2, NG, 128), f32),
            wave, wave, wave, wave,
            pltpu.VMEM((NW, 8, 128), f32),
            pltpu.VMEM((NW, 8, 128), f32),
            pltpu.VMEM((8, 32, NG), f32),
            dma((6,)), dma((7,)), dma, dma((11,)), dma((11,)), dma((7,)), dma((7,)),
        ],
        compiler_params=pltpu.CompilerParams(
            collective_id=0, has_side_effects=True, vmem_limit_bytes=60 << 20
        ),
        name="step",
    )(
        force_adjoint, paint_index, block_count, block_owner.reshape(1, NB), block_tile,
        *[jnp.asarray(t) for t in tables],
    )
    return mesh_grad, mass_grad


def solution(mesh):
    return jax.shard_map(
        on_device,
        mesh=mesh,
        in_specs=(
            P(None, "pencil", "wide"),
            P("pencil", "wide"),
            P("pencil", "wide"),
            P("pencil", "wide", None),
            P("pencil", "wide"),
        ),
        out_specs=(P("wide", "pencil", None), P("pencil", "wide")),
        check_vma=False,
    )
```

```python
import math

import jax
import jax.numpy as jnp
import ml_dtypes
import numpy as np
from jax import lax
from jax.experimental import pallas as pl
from jax.experimental.pallas import tpu as pltpu
from jax.sharding import PartitionSpec as P

NG = 256
NW = 32
NP = 8
NB = 32
BP = 512
MESH = pl.DeviceIdType.MESH
f32 = jnp.float32
bf16 = jnp.bfloat16


def roll(x, shift, axis):
    return pltpu.roll(x, shift, axis)


def halves(table):
    table = np.asarray(table, np.float32)
    high = table.astype(ml_dtypes.bfloat16)
    low = (table - high.astype(np.float32)).astype(ml_dtypes.bfloat16)
    return np.stack([high, low])


def waves(first, second):
    phase = (np.asarray(first)[:, None] * np.asarray(second)[None, :]) % NG
    angle = phase * (2.0 * math.pi / NG)
    return np.cos(angle), np.sin(angle)


def ky_of_row():
    out = []
    for w in range(NW):
        for j in range(8):
            base = 4 * w + j % 4
            out.append(base if j < 4 else (128 if base == 0 else NG - base))
    return np.array(out)


def make_tables():
    line = np.arange(NG)
    half = np.arange(NG // 2)
    sign = np.where(line % 2 == 0, 1.0, -1.0)
    by_half = line.reshape(2, NP, 2, 8).transpose(2, 0, 1, 3).reshape(-1)
    c, s = waves(line, half)
    s = -s
    s[:, 0] = sign
    z_fwd = np.concatenate([c, s], axis=1)[:, by_half]
    c, s = waves(half, line)
    weight = np.where(half == 0, 1.0, 2.0)[:, None]
    c = c * weight
    s = -2.0 * s
    s[0] = sign
    z_inv = np.concatenate([c, s], axis=0)[by_half]
    ky = ky_of_row()
    c, s = waves(ky, line)
    y_fwd = np.concatenate([c, s], axis=0)
    kyt = ky.reshape(NW, 8).T.reshape(-1)
    c, s = waves(line, kyt)
    y_inv = np.concatenate([c, s], axis=0)
    xt = line.reshape(NW, 8).T.reshape(-1)
    c, s = waves(line, xt)
    x_fwd = np.concatenate([c, s], axis=0)
    c, s = waves(line, line)
    x_inv = np.concatenate([c, s], axis=0)
    return dict(
        z_fwd=halves(z_fwd),
        z_inv=halves(z_inv),
        z_inv_t=halves(z_inv.T),
        y_fwd=halves(y_fwd),
        y_inv=halves(y_inv),
        x_fwd=halves(x_fwd),
        x_inv=halves(x_inv),
    )


def dot(a, b, dims=((1,), (0,))):
    return lax.dot_general(a, b, (dims, ((), ())), preferred_element_type=f32)


def split(x):
    high = x.astype(bf16)
    return high, (x - high.astype(f32)).astype(bf16)


def dot3(a, b, dims=((1,), (0,))):
    if b[0].shape[1] == 128:
        high = dot(a[0], jnp.concatenate(b, axis=1))
        return high[:, :128] + (high[:, 128:] + dot(a[1], b[0]))
    return dot(a[0], b[0], dims) + (dot(a[0], b[1], dims) + dot(a[1], b[0], dims))


def iota(shape, axis):
    return lax.broadcasted_iota(jnp.int32, shape, axis)


def exchange(arrays):
    lane = iota(arrays[0].shape, 1)
    b = 1
    while b < len(arrays):
        bit = (lane // (8 * b)) & 1
        new = []
        for i in range(len(arrays)):
            mine = i // b % 2
            shift = 8 * b if mine == 0 else 128 - 8 * b
            new.append(jnp.where(bit == mine, arrays[i], roll(arrays[i ^ b], shift, 1)))
        arrays = new
        b *= 2
    return arrays


def one_hot_rows(ids):
    spot = (ids & 31) * 8 + (iota((NW * 8, 128), 0) & 7)
    lane = iota((NW * 8, 128), 1)
    both = jnp.concatenate(
        [jnp.where(spot == lane, 1.0, 0.0), jnp.where(spot == lane + 128, 1.0, 0.0)], axis=1
    )
    return both.astype(bf16)


def scatter_rows(field, ty0, ty1):
    upper = (iota((NW * 8, 128), 1) >= 64).astype(jnp.int32)
    turned = roll(field, 64, 1)
    first = jnp.where(upper == 0, field, turned)
    second = jnp.where(upper == 0, turned, field)
    rows = []
    for values, ty in ((first, ty0), (second, ty1)):
        rows.append(
            jnp.concatenate(
                [jnp.where(ty == upper, values, 0.0), jnp.where(ty == upper + 2, values, 0.0)],
                axis=1,
            )
        )
    return jnp.concatenate(rows, axis=0)


def pick_rows(v0, v1, ty0, ty1):
    lower = iota((NW * 8, 128), 1) < 64
    out = []
    for v, ty in ((v0, ty0), (v1, ty1)):
        half = jnp.where(ty >= 2, v[:, 128:], v[:, :128])
        out.append((half, roll(half, 64, 1)))
    first = jnp.where((ty0 & 1) == 1, out[0][1], out[0][0])
    second = jnp.where((ty1 & 1) == 1, out[1][0], out[1][1])
    return jnp.where(lower, first, second)


def y_slopes():
    row = iota((NG, 128), 0)
    base = (row >> 3) * 4 + (row & 3)
    return jnp.where((row & 4) == 0, base, -base).astype(f32)


def combine(sums, sign):
    out = []
    for k in range(0, sums.shape[1], 128):
        turned = roll(sums[NG:, k : k + 128], 64, 1)
        real = iota((NG, 128), 1) < 64
        out.append(sums[:NG, k : k + 128] + jnp.where(real, -sign * turned, sign * turned))
    return out


def solve_x(a, b, w, p, q):
    row = iota((NG, 128), 0)
    lane = iota((NG, 128), 1)
    signed = jnp.where(row < 128, row, row - NG)
    slope = jnp.where(row == 128, 0, signed).astype(f32)
    sign = jnp.where(lane < 64, 1.0, -1.0)
    cos_a, sin_a = sign * a[:NG], roll(a[NG:], 64, 1)
    cos_b, sin_b = sign * b[:NG], roll(b[NG:], 64, 1)
    here = sign * (slope * (cos_a + sin_a) + (cos_b + sin_b))
    j = lane // 8 & 7
    base = 4 * w + (j & 3)
    ny = jnp.where((base == 0) & (j == 4), 128, base)
    nz = 16 * p + 8 * q + (lane & 7)
    flat = signed * signed + ny * ny
    factor = (1.0 / NG**2) / jnp.maximum(flat + nz * nz, 1).astype(f32)
    if q:
        return factor * here
    there = (cos_b - sin_b) - slope * (cos_a - sin_a)
    swapped = jnp.where((lane & 32) == 0, roll(there, 96, 1), roll(there, 32, 1))
    there = jnp.where(base == 0, there, swapped)
    top = (1.0 / NG**2) / (flat + (NG // 2) ** 2).astype(f32)
    shared = nz == 0
    alpha = jnp.where(shared, 0.5 * (factor + top), factor)
    beta = jnp.where(shared, 0.5 * (top - factor), 0.0)
    return alpha * here + beta * there


def times_i(sums):
    turned = roll(sums[:NG], 64, 1)
    return jnp.where(iota((NG, 128), 1) < 64, -turned, turned) - sums[NG:]


def wide_peer(w, i):
    iz, ix = i // 4, i % 4
    dz = 4 + (iz + 1) // 2 * (1 - 2 * ((iz + 1) % 2))
    dx = 2 + (ix + 1) // 2 * (1 - 2 * ((ix + 1) % 2))
    return (w // 8 + dx) % 4 * 8 + (w + dz) % 8


def pencil_peer(p, i):
    dy = 2 + (i // 2 + 1) // 2 * (1 - 2 * ((i // 2 + 1) % 2))
    return (p // 2 + dy) % 4 * 2 + (p + i + i // 6) % 2


def loop(count, step, unroll=1):
    def body(i, carry):
        step(i)
        return carry

    lax.fori_loop(0, count, body, 0, unroll=unroll)


def half(ref, h):
    return ref.at[pl.ds(h, 1)]


def rows(ref, i, size):
    return ref.at[:, pl.ds(pl.multiple_of(i * size, 8), size), :]


def step_kernel(
    force_hbm, cells_hbm, count_hbm, owner_hbm, tile_hbm,
    z_fwd_hbm, z_inv_t_hbm, z_inv_hbm, y_fwd_hbm, y_inv_hbm, x_fwd_hbm, x_inv_hbm,
    mesh_ref, mass_ref,
    force, cells, count, owner, tile, owner_v,
    z_fwd, z_inv_t, z_inv, y_fwd, y_inv, x_fwd, x_inv,
    spread, tiles, pick_v, pick, ids, msg, ids_rx, msg_rx,
    snd2, rx2, snd3, rx3, snd4, rx4, snd5, rx5, snd6, rx6, mesh_v,
    arg_sem, table_sem, pick_sem, wide_out, wide_in, pencil_out, pencil_in,
):
    w = lax.axis_index("wide")
    p = lax.axis_index("pencil")

    arg_copies = [
        pltpu.make_async_copy(src, dst, arg_sem.at[i])
        for i, (src, dst) in enumerate(
            [
                (owner_hbm, owner_v), (owner_hbm, owner), (count_hbm, count), (tile_hbm, tile),
                (cells_hbm, cells), (force_hbm, force),
            ]
        )
    ]
    table_copies = [
        pltpu.make_async_copy(src, dst, table_sem.at[i])
        for i, (src, dst) in enumerate(
            [
                (z_fwd_hbm, z_fwd), (z_inv_t_hbm, z_inv_t), (y_fwd_hbm, y_fwd),
                (x_fwd_hbm, x_fwd), (x_inv_hbm, x_inv), (y_inv_hbm, y_inv), (z_inv_hbm, z_inv),
            ]
        )
    ]
    for copy in arg_copies:
        copy.start()
    barrier = pltpu.get_barrier_semaphore()
    loop(
        NW - 1,
        lambda i: pl.semaphore_signal(
            barrier, inc=1, device_id={"wide": wide_peer(w, i)}, device_id_type=MESH
        ),
    )
    loop(
        NP - 1,
        lambda i: pl.semaphore_signal(
            barrier, inc=1, device_id={"pencil": pencil_peer(p, i)}, device_id_type=MESH
        ),
    )
    for copy in table_copies:
        copy.start()

    def wide_copy(phase, src, dst, other):
        return pltpu.make_async_remote_copy(
            src_ref=src, dst_ref=dst, send_sem=wide_out.at[phase], recv_sem=wide_in.at[phase],
            device_id={"wide": other}, device_id_type=MESH,
        )

    def pencil_copy(phase, src, dst, other):
        return pltpu.make_async_remote_copy(
            src_ref=src, dst_ref=dst, send_sem=pencil_out.at[phase], recv_sem=pencil_in.at[phase],
            device_id={"pencil": other}, device_id_type=MESH,
        )

    def wide_send(phase, src, dst):
        def step(i):
            other = wide_peer(w, i)
            wide_copy(phase, rows(src, other, 8), rows(dst, w, 8), other).start()

        loop(NW - 1, step)
        here = pl.ds(pl.multiple_of(w * 8, 8), 8)
        dst[:, here, :] = src[:, here, :]

    def wide_all(phase, src, dst):
        part = pl.ds(0, (NW - 1) * 8)
        return wide_copy(phase, src.at[:, part, :], dst.at[:, part, :], (w + 1) % NW)

    def pencil_send(phase, src, dst):
        def step(i):
            other = pencil_peer(p, i)
            pencil_copy(phase, rows(src, other, 32), rows(dst, p, 32), other).start()

        loop(NP - 1, step)
        here = pl.ds(pl.multiple_of(p * 32, 32), 32)
        dst[:, here, :] = src[:, here, :]

    def pencil_all(phase, src, dst):
        part = pl.ds(0, (NP - 1) * 32)
        return pencil_copy(phase, src.at[:, part, :], dst.at[:, part, :], (p + 1) % NP)

    arg_copies[0].wait()
    block = iota((NW, NB), 1)
    match = owner_v[...] == iota((NW, NB), 0)
    first = jnp.min(jnp.where(match, block, NB), axis=1, keepdims=True)
    last = jnp.max(jnp.where(match, block, -1), axis=1, keepdims=True)
    second = jnp.where(last > first, last, NB)
    pick_v[...] = jnp.where(iota((NW, 128), 1) == 0, first, second)
    pick_copy = pltpu.make_async_copy(pick_v, pick, pick_sem)
    pick_copy.start()

    for copy in arg_copies[1:]:
        copy.wait()
    tiles[NB] = jnp.zeros((3, 8, 128), f32)

    def slots(b):
        return pl.ds(pl.multiple_of(b * BP, BP), BP)

    def kept(b):
        live = iota((1, BP), 1) < count[0, b]
        return (iota((8, BP), 0) == (cells[0:1, slots(b)] & 7)) & live

    def paint(b):
        key = cells[0:1, slots(b)] >> 3
        hot = jnp.where(iota((64, BP), 0) == key, 1.0, 0.0).astype(bf16)
        spread[b] = hot
        keep = kept(b)
        high, low = [], []
        for f in range(3):
            amount = force[f, 0:1, slots(b)]
            top = amount.astype(bf16).astype(f32)
            high.append(jnp.where(keep, top, 0.0))
            low.append(jnp.where(keep, amount - top, 0.0))
        out = dot(jnp.concatenate(high + low, axis=0).astype(bf16), hot, ((1,), (1,)))
        out = out[:24] + out[24:]
        tiles[b] = jnp.concatenate([out, out], axis=1).reshape(3, 8, 128)

    loop(NB, paint, unroll=16)
    pick_copy.wait()
    pl.semaphore_wait(barrier, NW - 1 + NP - 1)

    left = iota((8, 128), 1) < 64

    def assemble(f, o):
        msg[f, o] = jnp.where(left, tiles[pick[o, 0], f], tiles[pick[o, 1], f])

    def number(o):
        name = []
        for s in range(2):
            b = pick[o, s]
            name.append(jnp.where(b < NB, tile[0, jnp.minimum(b, NB - 1)], -1))
        ids[o] = jnp.where(iota((1, 128), 1) < 64, name[0], name[1])

    def send_first(i):
        other = wide_peer(w, i)
        number(other)
        wide_copy(0, ids.at[other], ids_rx.at[w], other).start()
        assemble(0, other)
        wide_copy(1, msg.at[0, other], msg_rx.at[0, w], other).start()

    loop(NW - 1, send_first)
    for f in (1, 2):

        def send_field(i, f=f):
            other = wide_peer(w, i)
            assemble(f, other)
            wide_copy(1 + f, msg.at[f, other], msg_rx.at[f, w], other).start()

        loop(NW - 1, send_field)
    number(w)
    ids_rx[w] = ids[w]
    for f in range(3):
        assemble(f, w)
        msg_rx[f, w] = msg[f, w]
    others = pl.ds(0, NW - 1)
    ids_all = wide_copy(0, ids.at[others], ids_rx.at[others], (w + 1) % NW)
    msg_all = [
        wide_copy(1 + f, msg.at[f, others], msg_rx.at[f, others], (w + 1) % NW) for f in range(3)
    ]
    ids_all.wait_recv()
    pair = jnp.broadcast_to(ids_rx[...], (NW, 8, 128)).reshape(NW * 8, 128)
    turned = roll(pair, 64, 1)
    lower = iota((NW * 8, 128), 1) < 64
    ids0, ids1 = jnp.where(lower, pair, turned), jnp.where(lower, turned, pair)
    chosen = jnp.concatenate([one_hot_rows(ids0), one_hot_rows(ids1)], axis=0)
    table_copies[0].wait()
    g_fwd = [dot(chosen, z_fwd[i]).astype(bf16) for i in range(2)]
    ty0, ty1 = ids0 >> 5, ids1 >> 5

    lane = iota((NG, 256), 1)
    kz = ((lane // 8 & 7) * 16 + lane // 128 * 8 + (lane & 7)).astype(f32)

    def z_lines(f):
        msg_all[f].wait_recv()
        field = msg_rx[f].reshape(NW * 8, 128)
        lines = dot3(split(scatter_rows(field, ty0, ty1).T), g_fwd)
        if f == 2:
            lines = lines * kz
        for q in range(2):
            by_x = [
                jnp.concatenate(
                    [
                        lines[ty * 64 + cx * 8 : ty * 64 + cx * 8 + 8, q * 128 : q * 128 + 128]
                        for ty in range(4)
                    ],
                    axis=0,
                )
                for cx in range(8)
            ]
            for i, value in enumerate(exchange(by_x)):
                snd2[f, q, 32 * i : 32 * i + 32, :] = value
            if f != 1:
                pencil_send(3 * f // 2 + q, half(snd2.at[f], q), half(rx2.at[f], q))
        if f == 1:
            pencil_send(2, snd2.at[f], rx2.at[f])

    slope = y_slopes()

    def y_lines(f, q):
        pencil_all(3 * f // 2 + q, half(snd2.at[f], q), half(rx2.at[f], q)).wait_recv()
        return combine(dot3((y_fwd[0], y_fwd[1]), split(rx2[f, q])), -1.0)[0]

    z_lines(0)
    z_lines(1)
    z_lines(2)
    table_copies[2].wait()
    for q in range(2):
        snd3[0, q] = y_lines(0, q)
        wide_send(4 + q, half(snd3.at[0], q), half(rx3.at[0], q))
    table_copies[1].wait()
    g_inv = [dot(chosen, z_inv_t[i]).astype(bf16) for i in range(2)]
    pencil_all(2, snd2.at[1], rx2.at[1]).wait_recv()
    both = jnp.concatenate([rx2[1, 0], rx2[1, 1]], axis=1)
    for q, value in enumerate(combine(dot3((y_fwd[0], y_fwd[1]), split(both)), -1.0)):
        snd3[1, q] = slope * value
    for q in range(2):
        snd3[1, q] += y_lines(2, q)
        wide_send(6 + q, half(snd3.at[1], q), half(rx3.at[1], q))

    table_copies[3].wait()
    table_copies[4].wait()

    def x_lines(i, q):
        wide_all(4 + 2 * i + q, half(snd3.at[i], q), half(rx3.at[i], q)).wait_recv()
        parts = exchange([rx3[i, q, pl.ds(j, NW, stride=8), :] for j in range(8)])
        return jnp.concatenate(parts, axis=0)

    both = jnp.concatenate([x_lines(0, 0), x_lines(0, 1)], axis=1)
    first = dot3((x_fwd[0], x_fwd[1]), split(both))
    for q in range(2):
        second = dot3((x_fwd[0], x_fwd[1]), split(x_lines(1, q)))
        solved = solve_x(first[:, q * 128 : q * 128 + 128], second, w, p, q)
        snd4[q] = times_i(dot3((x_inv[0], x_inv[1]), split(solved)))
        wide_send(8 + q, half(snd4, q), half(rx4, q))

    table_copies[5].wait()
    for q in range(2):
        wide_all(8 + q, half(snd4, q), half(rx4, q)).wait_recv()
        parts = exchange([rx4[q, pl.ds(cx, NW, stride=8), :] for cx in range(8)])
        sums = dot3((y_inv[0], y_inv[1]), split(jnp.concatenate(parts, axis=0)))
        snd5[q] = combine(sums, 1.0)[0]
        pencil_send(5 + q, half(snd5, q), half(rx5, q))

    table_copies[6].wait()
    lines = []
    for q in range(2):
        pencil_all(5 + q, half(snd5, q), half(rx5, q)).wait_recv()
        by_x = exchange([rx5[q, 32 * i : 32 * i + 32, :] for i in range(8)])
        lines.append(
            split(
                jnp.concatenate(
                    [by_x[cx][ty * 8 : ty * 8 + 8] for ty in range(4) for cx in range(8)], axis=0
                )
            )
        )
    lines = [jnp.concatenate([lines[0][i], lines[1][i]], axis=1) for i in range(2)]
    values = dot3(g_inv, lines, ((1,), (1,)))
    snd6[...] = pick_rows(values[: NW * 8], values[NW * 8 :], ty0, ty1).reshape(NW, 8, 128)

    def send_back(i):
        other = wide_peer(w, i)
        wide_copy(10, snd6.at[other], rx6.at[w], other).start()

    loop(NW - 1, send_back)
    rx6[w] = snd6[w]
    mesh = dot3(lines, (z_inv[0], z_inv[1]))
    for ty in range(4):
        for cx in range(8):
            mesh_v[cx, ty * 8 : ty * 8 + 8, :] = mesh[ty * 64 + cx * 8 : ty * 64 + cx * 8 + 8]
    mesh_copy = pltpu.make_async_copy(mesh_v, mesh_ref, pick_sem)
    mesh_copy.start()
    ids_all.wait_send()
    for f in range(3):
        msg_all[f].wait_send()
    pencil_all(2, snd2.at[1], rx2.at[1]).wait_send()
    for q in range(2):
        for f in (0, 2):
            pencil_all(3 * f // 2 + q, half(snd2.at[f], q), half(rx2.at[f], q)).wait_send()
        for i in range(2):
            wide_all(4 + 2 * i + q, half(snd3.at[i], q), half(rx3.at[i], q)).wait_send()
        wide_all(8 + q, half(snd4, q), half(rx4, q)).wait_send()
        pencil_all(5 + q, half(snd5, q), half(rx5, q)).wait_send()
    wide_copy(10, snd6.at[others], rx6.at[others], (w + 1) % NW).wait()

    def read(b):
        o = owner[0, b]
        pair = rx6[o]
        here = jnp.where(pick[o, 0] == b, pair, roll(pair, 64, 1))
        tile_in = here[:, :64]
        top = tile_in.astype(bf16).astype(f32)
        out = dot(jnp.concatenate([top, tile_in - top], axis=0).astype(bf16), spread[b])
        value = jnp.sum(jnp.where(kept(b), out[:8] + out[8:], 0.0), axis=0, keepdims=True)
        mass_ref[0:1, slots(b)] = value

    loop(NB, read, unroll=16)
    mesh_copy.wait()


def hand_over(mesh_in, mass_in, mesh_out, mass_out, mesh_v, mass_v, in_sem, out_sem):
    reads = [pltpu.make_async_copy(mass_in, mass_v, in_sem.at[4])]
    writes = [pltpu.make_async_copy(mass_v, mass_out, out_sem.at[4])]
    for i in range(4):
        part = pl.ds(2 * i, 2)
        reads.append(pltpu.make_async_copy(mesh_in.at[part], mesh_v.at[part], in_sem.at[i]))
        writes.append(pltpu.make_async_copy(mesh_v.at[part], mesh_out.at[part], out_sem.at[i]))
    for copy in reads:
        copy.start()
    for read, write in zip(reads, writes):
        read.wait()
        write.start()
    for copy in writes:
        copy.wait()


def on_device(force_adjoint, paint_index, block_count, block_owner, block_tile):
    tabs = make_tables()
    names = ["z_fwd", "z_inv_t", "z_inv", "y_fwd", "y_inv", "x_fwd", "x_inv"]
    tables = [tabs[n] for n in names]
    vmem = pl.BlockSpec(memory_space=pltpu.VMEM)
    wave = pltpu.VMEM((2, NG, 128), f32)
    dma = pltpu.SemaphoreType.DMA
    mesh_grad, mass_grad = pl.pallas_call(
        step_kernel,
        out_shape=(
            jax.ShapeDtypeStruct((8, 32, NG), f32),
            jax.ShapeDtypeStruct((1, NB * BP), f32),
        ),
        in_specs=[pl.BlockSpec(memory_space=pl.ANY)] * (5 + len(names)),
        out_specs=(pl.BlockSpec(memory_space=pl.ANY), vmem),
        scratch_shapes=[
            pltpu.VMEM((3, 1, NB * BP), f32),
            pltpu.VMEM((1, NB * BP), jnp.int32),
            pltpu.SMEM((1, NB), jnp.int32),
            pltpu.SMEM((1, NB), jnp.int32),
            pltpu.SMEM((1, NB), jnp.int32),
            pltpu.VMEM((1, NB), jnp.int32),
            *[pltpu.VMEM(t.shape, bf16) for t in tables],
            pltpu.VMEM((NB, 64, BP), bf16),
            pltpu.VMEM((NB + 1, 3, 8, 128), f32),
            pltpu.VMEM((NW, 128), jnp.int32),
            pltpu.SMEM((NW, 128), jnp.int32),
            pltpu.VMEM((NW, 1, 128), jnp.int32),
            pltpu.VMEM((3, NW, 8, 128), f32),
            pltpu.VMEM((NW, 1, 128), jnp.int32),
            pltpu.VMEM((3, NW, 8, 128), f32),
            pltpu.VMEM((3, 2, NG, 128), f32),
            pltpu.VMEM((3, 2, NG, 128), f32),
            pltpu.VMEM((2, 2, NG, 128), f32),
            pltpu.VMEM((2, 2, NG, 128), f32),
            wave, wave, wave, wave,
            pltpu.VMEM((NW, 8, 128), f32),
            pltpu.VMEM((NW, 8, 128), f32),
            pltpu.VMEM((8, 32, NG), f32),
            dma((6,)), dma((7,)), dma, dma((11,)), dma((11,)), dma((7,)), dma((7,)),
        ],
        compiler_params=pltpu.CompilerParams(
            collective_id=0, has_side_effects=True, vmem_limit_bytes=60 << 20
        ),
        name="step",
    )(
        force_adjoint, paint_index, block_count, block_owner.reshape(1, NB), block_tile,
        *[jnp.asarray(t) for t in tables],
    )
    anywhere = pl.BlockSpec(memory_space=pl.ANY)
    return pl.pallas_call(
        hand_over,
        out_shape=(
            jax.ShapeDtypeStruct((8, 32, NG), f32),
            jax.ShapeDtypeStruct((1, NB * BP), f32),
        ),
        in_specs=[anywhere, anywhere],
        out_specs=(anywhere, anywhere),
        scratch_shapes=[
            pltpu.VMEM((8, 32, NG), f32), pltpu.VMEM((1, NB * BP), f32), dma((5,)), dma((5,)),
        ],
        compiler_params=pltpu.CompilerParams(vmem_limit_bytes=60 << 20),
        name="hand_over",
    )(mesh_grad, mass_grad)


def solution(mesh):
    return jax.shard_map(
        on_device,
        mesh=mesh,
        in_specs=(
            P(None, "pencil", "wide"),
            P("pencil", "wide"),
            P("pencil", "wide"),
            P("pencil", "wide", None),
            P("pencil", "wide"),
        ),
        out_specs=(P("wide", "pencil", None), P("pencil", "wide")),
        check_vma=False,
    )
```

```python
import math

import jax
import jax.numpy as jnp
import ml_dtypes
import numpy as np
from jax import lax
from jax.experimental import pallas as pl
from jax.experimental.pallas import tpu as pltpu
from jax.sharding import PartitionSpec as P

NG = 256
NW = 32
NP = 8
NB = 32
BP = 512
MESH = pl.DeviceIdType.MESH
f32 = jnp.float32
bf16 = jnp.bfloat16


def roll(x, shift, axis):
    return pltpu.roll(x, shift, axis)


def halves(table):
    table = np.asarray(table, np.float32)
    high = table.astype(ml_dtypes.bfloat16)
    low = (table - high.astype(np.float32)).astype(ml_dtypes.bfloat16)
    return np.stack([high, low])


def waves(first, second):
    phase = (np.asarray(first)[:, None] * np.asarray(second)[None, :]) % NG
    angle = phase * (2.0 * math.pi / NG)
    return np.cos(angle), np.sin(angle)


def ky_of_row():
    out = []
    for w in range(NW):
        for j in range(8):
            base = 4 * w + j % 4
            out.append(base if j < 4 else (128 if base == 0 else NG - base))
    return np.array(out)


def make_tables():
    line = np.arange(NG)
    half = np.arange(NG // 2)
    sign = np.where(line % 2 == 0, 1.0, -1.0)
    by_half = line.reshape(2, NP, 2, 8).transpose(2, 0, 1, 3).reshape(-1)
    c, s = waves(line, half)
    s = -s
    s[:, 0] = sign
    z_fwd = np.concatenate([c, s], axis=1)[:, by_half]
    c, s = waves(half, line)
    weight = np.where(half == 0, 1.0, 2.0)[:, None]
    c = c * weight
    s = -2.0 * s
    s[0] = sign
    z_inv = np.concatenate([c, s], axis=0)[by_half]
    ky = ky_of_row()
    c, s = waves(ky, line)
    y_fwd = np.concatenate([c, s], axis=0)
    kyt = ky.reshape(NW, 8).T.reshape(-1)
    c, s = waves(line, kyt)
    y_inv = np.concatenate([c, s], axis=0)
    xt = line.reshape(NW, 8).T.reshape(-1)
    c, s = waves(line, xt)
    x_fwd = np.concatenate([c, s], axis=0)
    c, s = waves(line, line)
    x_inv = np.concatenate([c, s], axis=0)
    return dict(
        z_fwd=halves(z_fwd),
        z_inv=halves(z_inv),
        z_inv_t=halves(z_inv.T),
        y_fwd=halves(y_fwd),
        y_inv=halves(y_inv),
        x_fwd=halves(x_fwd),
        x_inv=halves(x_inv),
    )


def dot(a, b, dims=((1,), (0,))):
    return lax.dot_general(a, b, (dims, ((), ())), preferred_element_type=f32)


def split(x):
    high = x.astype(bf16)
    return high, (x - high.astype(f32)).astype(bf16)


def dot3(a, b, dims=((1,), (0,))):
    if b[0].shape[1] == 128:
        high = dot(a[0], jnp.concatenate(b, axis=1))
        return high[:, :128] + (high[:, 128:] + dot(a[1], b[0]))
    return dot(a[0], b[0], dims) + (dot(a[0], b[1], dims) + dot(a[1], b[0], dims))


def iota(shape, axis):
    return lax.broadcasted_iota(jnp.int32, shape, axis)


def exchange(arrays):
    lane = iota(arrays[0].shape, 1)
    b = 1
    while b < len(arrays):
        bit = (lane // (8 * b)) & 1
        new = []
        for i in range(len(arrays)):
            mine = i // b % 2
            shift = 8 * b if mine == 0 else 128 - 8 * b
            new.append(jnp.where(bit == mine, arrays[i], roll(arrays[i ^ b], shift, 1)))
        arrays = new
        b *= 2
    return arrays


def one_hot_rows(ids):
    spot = (ids & 31) * 8 + (iota((NW * 8, 128), 0) & 7)
    lane = iota((NW * 8, 128), 1)
    both = jnp.concatenate(
        [jnp.where(spot == lane, 1.0, 0.0), jnp.where(spot == lane + 128, 1.0, 0.0)], axis=1
    )
    return both.astype(bf16)


def scatter_rows(field, ty0, ty1):
    upper = (iota((NW * 8, 128), 1) >= 64).astype(jnp.int32)
    turned = roll(field, 64, 1)
    first = jnp.where(upper == 0, field, turned)
    second = jnp.where(upper == 0, turned, field)
    rows = []
    for values, ty in ((first, ty0), (second, ty1)):
        rows.append(
            jnp.concatenate(
                [jnp.where(ty == upper, values, 0.0), jnp.where(ty == upper + 2, values, 0.0)],
                axis=1,
            )
        )
    return jnp.concatenate(rows, axis=0)


def pick_rows(v0, v1, ty0, ty1):
    lower = iota((NW * 8, 128), 1) < 64
    out = []
    for v, ty in ((v0, ty0), (v1, ty1)):
        half = jnp.where(ty >= 2, v[:, 128:], v[:, :128])
        out.append((half, roll(half, 64, 1)))
    first = jnp.where((ty0 & 1) == 1, out[0][1], out[0][0])
    second = jnp.where((ty1 & 1) == 1, out[1][0], out[1][1])
    return jnp.where(lower, first, second)


def y_slopes():
    row = iota((NG, 128), 0)
    base = (row >> 3) * 4 + (row & 3)
    return jnp.where((row & 4) == 0, base, -base).astype(f32)


def combine(sums, sign):
    out = []
    for k in range(0, sums.shape[1], 128):
        turned = roll(sums[NG:, k : k + 128], 64, 1)
        real = iota((NG, 128), 1) < 64
        out.append(sums[:NG, k : k + 128] + jnp.where(real, -sign * turned, sign * turned))
    return out


def solve_x(a, b, w, p, q):
    row = iota((NG, 128), 0)
    lane = iota((NG, 128), 1)
    signed = jnp.where(row < 128, row, row - NG)
    slope = jnp.where(row == 128, 0, signed).astype(f32)
    sign = jnp.where(lane < 64, 1.0, -1.0)
    cos_a, sin_a = sign * a[:NG], roll(a[NG:], 64, 1)
    cos_b, sin_b = sign * b[:NG], roll(b[NG:], 64, 1)
    here = sign * (slope * (cos_a + sin_a) + (cos_b + sin_b))
    j = lane // 8 & 7
    base = 4 * w + (j & 3)
    ny = jnp.where((base == 0) & (j == 4), 128, base)
    nz = 16 * p + 8 * q + (lane & 7)
    flat = signed * signed + ny * ny
    factor = (1.0 / NG**2) / jnp.maximum(flat + nz * nz, 1).astype(f32)
    if q:
        return factor * here
    there = (cos_b - sin_b) - slope * (cos_a - sin_a)
    swapped = jnp.where((lane & 32) == 0, roll(there, 96, 1), roll(there, 32, 1))
    there = jnp.where(base == 0, there, swapped)
    top = (1.0 / NG**2) / (flat + (NG // 2) ** 2).astype(f32)
    shared = nz == 0
    alpha = jnp.where(shared, 0.5 * (factor + top), factor)
    beta = jnp.where(shared, 0.5 * (top - factor), 0.0)
    return alpha * here + beta * there


def times_i(sums):
    turned = roll(sums[:NG], 64, 1)
    return jnp.where(iota((NG, 128), 1) < 64, -turned, turned) - sums[NG:]


def wide_peer(w, i):
    iz, ix = i // 4, i % 4
    dz = 4 + (iz + 1) // 2 * (1 - 2 * ((iz + 1) % 2))
    dx = 2 + (ix + 1) // 2 * (1 - 2 * ((ix + 1) % 2))
    return (w // 8 + dx) % 4 * 8 + (w + dz) % 8


def pencil_peer(p, i):
    dy = 2 + (i // 2 + 1) // 2 * (1 - 2 * ((i // 2 + 1) % 2))
    return (p // 2 + dy) % 4 * 2 + (p + i + i // 6) % 2


def loop(count, step, unroll=1):
    def body(i, carry):
        step(i)
        return carry

    lax.fori_loop(0, count, body, 0, unroll=unroll)


def half(ref, h):
    return ref.at[pl.ds(h, 1)]


def rows(ref, i, size):
    return ref.at[:, pl.ds(pl.multiple_of(i * size, 8), size), :]


def step_kernel(
    force_hbm, cells_hbm, count_hbm, owner_hbm, tile_hbm,
    z_fwd_hbm, z_inv_t_hbm, z_inv_hbm, y_fwd_hbm, y_inv_hbm, x_fwd_hbm, x_inv_hbm,
    mesh_ref, mass_ref,
    force, cells, count, owner, tile, owner_v,
    z_fwd, z_inv_t, z_inv, y_fwd, y_inv, x_fwd, x_inv,
    spread, tiles, pick_v, pick, ids, msg, ids_rx, msg_rx,
    snd2, rx2, snd3, rx3, snd4, rx4, snd5, rx5, snd6, rx6, mesh_v,
    arg_sem, table_sem, pick_sem, wide_out, wide_in, pencil_out, pencil_in,
):
    w = lax.axis_index("wide")
    p = lax.axis_index("pencil")

    arg_copies = [
        pltpu.make_async_copy(src, dst, arg_sem.at[i])
        for i, (src, dst) in enumerate(
            [
                (owner_hbm, owner_v), (owner_hbm, owner), (count_hbm, count), (tile_hbm, tile),
                (cells_hbm, cells), (force_hbm, force),
            ]
        )
    ]
    table_copies = [
        pltpu.make_async_copy(src, dst, table_sem.at[i])
        for i, (src, dst) in enumerate(
            [
                (z_fwd_hbm, z_fwd), (z_inv_t_hbm, z_inv_t), (y_fwd_hbm, y_fwd),
                (x_fwd_hbm, x_fwd), (x_inv_hbm, x_inv), (y_inv_hbm, y_inv), (z_inv_hbm, z_inv),
            ]
        )
    ]
    for copy in arg_copies:
        copy.start()
    barrier = pltpu.get_barrier_semaphore()
    loop(
        NW - 1,
        lambda i: pl.semaphore_signal(
            barrier, inc=1, device_id={"wide": wide_peer(w, i)}, device_id_type=MESH
        ),
    )
    loop(
        NP - 1,
        lambda i: pl.semaphore_signal(
            barrier, inc=1, device_id={"pencil": pencil_peer(p, i)}, device_id_type=MESH
        ),
    )
    for copy in table_copies:
        copy.start()

    def wide_copy(phase, src, dst, other):
        return pltpu.make_async_remote_copy(
            src_ref=src, dst_ref=dst, send_sem=wide_out.at[phase], recv_sem=wide_in.at[phase],
            device_id={"wide": other}, device_id_type=MESH,
        )

    def pencil_copy(phase, src, dst, other):
        return pltpu.make_async_remote_copy(
            src_ref=src, dst_ref=dst, send_sem=pencil_out.at[phase], recv_sem=pencil_in.at[phase],
            device_id={"pencil": other}, device_id_type=MESH,
        )

    def wide_send(phase, src, dst):
        def step(i):
            other = wide_peer(w, i)
            wide_copy(phase, rows(src, other, 8), rows(dst, w, 8), other).start()

        loop(NW - 1, step, unroll=NW - 1)
        here = pl.ds(pl.multiple_of(w * 8, 8), 8)
        dst[:, here, :] = src[:, here, :]

    def wide_all(phase, src, dst):
        part = pl.ds(0, (NW - 1) * 8)
        return wide_copy(phase, src.at[:, part, :], dst.at[:, part, :], (w + 1) % NW)

    def pencil_send(phase, src, dst):
        def step(i):
            other = pencil_peer(p, i)
            pencil_copy(phase, rows(src, other, 32), rows(dst, p, 32), other).start()

        loop(NP - 1, step, unroll=NP - 1)
        here = pl.ds(pl.multiple_of(p * 32, 32), 32)
        dst[:, here, :] = src[:, here, :]

    def pencil_all(phase, src, dst):
        part = pl.ds(0, (NP - 1) * 32)
        return pencil_copy(phase, src.at[:, part, :], dst.at[:, part, :], (p + 1) % NP)

    arg_copies[0].wait()
    block = iota((NW, NB), 1)
    match = owner_v[...] == iota((NW, NB), 0)
    first = jnp.min(jnp.where(match, block, NB), axis=1, keepdims=True)
    last = jnp.max(jnp.where(match, block, -1), axis=1, keepdims=True)
    second = jnp.where(last > first, last, NB)
    pick_v[...] = jnp.where(iota((NW, 128), 1) == 0, first, second)
    pick_copy = pltpu.make_async_copy(pick_v, pick, pick_sem)
    pick_copy.start()

    for copy in arg_copies[1:]:
        copy.wait()
    tiles[NB] = jnp.zeros((3, 8, 128), f32)

    def slots(b):
        return pl.ds(pl.multiple_of(b * BP, BP), BP)

    def kept(b):
        live = iota((1, BP), 1) < count[0, b]
        return (iota((8, BP), 0) == (cells[0:1, slots(b)] & 7)) & live

    def paint(b):
        key = cells[0:1, slots(b)] >> 3
        hot = jnp.where(iota((64, BP), 0) == key, 1.0, 0.0).astype(bf16)
        spread[b] = hot
        keep = kept(b)
        high, low = [], []
        for f in range(3):
            amount = force[f, 0:1, slots(b)]
            top = amount.astype(bf16).astype(f32)
            high.append(jnp.where(keep, top, 0.0))
            low.append(jnp.where(keep, amount - top, 0.0))
        out = dot(jnp.concatenate(high + low, axis=0).astype(bf16), hot, ((1,), (1,)))
        out = out[:24] + out[24:]
        tiles[b] = jnp.concatenate([out, out], axis=1).reshape(3, 8, 128)

    loop(NB, paint, unroll=16)
    pick_copy.wait()
    pl.semaphore_wait(barrier, NW - 1 + NP - 1)

    left = iota((8, 128), 1) < 64

    def assemble(f, o):
        msg[f, o] = jnp.where(left, tiles[pick[o, 0], f], tiles[pick[o, 1], f])

    def number(o):
        name = []
        for s in range(2):
            b = pick[o, s]
            name.append(jnp.where(b < NB, tile[0, jnp.minimum(b, NB - 1)], -1))
        ids[o] = jnp.where(iota((1, 128), 1) < 64, name[0], name[1])

    def send_first(i):
        other = wide_peer(w, i)
        number(other)
        wide_copy(0, ids.at[other], ids_rx.at[w], other).start()
        assemble(0, other)
        wide_copy(1, msg.at[0, other], msg_rx.at[0, w], other).start()

    loop(NW - 1, send_first, unroll=NW - 1)
    for f in (1, 2):

        def send_field(i, f=f):
            other = wide_peer(w, i)
            assemble(f, other)
            wide_copy(1 + f, msg.at[f, other], msg_rx.at[f, w], other).start()

        loop(NW - 1, send_field, unroll=NW - 1)
    number(w)
    ids_rx[w] = ids[w]
    for f in range(3):
        assemble(f, w)
        msg_rx[f, w] = msg[f, w]
    others = pl.ds(0, NW - 1)
    ids_all = wide_copy(0, ids.at[others], ids_rx.at[others], (w + 1) % NW)
    msg_all = [
        wide_copy(1 + f, msg.at[f, others], msg_rx.at[f, others], (w + 1) % NW) for f in range(3)
    ]
    ids_all.wait_recv()
    pair = jnp.broadcast_to(ids_rx[...], (NW, 8, 128)).reshape(NW * 8, 128)
    turned = roll(pair, 64, 1)
    lower = iota((NW * 8, 128), 1) < 64
    ids0, ids1 = jnp.where(lower, pair, turned), jnp.where(lower, turned, pair)
    chosen = jnp.concatenate([one_hot_rows(ids0), one_hot_rows(ids1)], axis=0)
    table_copies[0].wait()
    g_fwd = [dot(chosen, z_fwd[i]).astype(bf16) for i in range(2)]
    ty0, ty1 = ids0 >> 5, ids1 >> 5

    lane = iota((NG, 256), 1)
    kz = ((lane // 8 & 7) * 16 + lane // 128 * 8 + (lane & 7)).astype(f32)

    def z_lines(f):
        msg_all[f].wait_recv()
        field = msg_rx[f].reshape(NW * 8, 128)
        lines = dot3(split(scatter_rows(field, ty0, ty1).T), g_fwd)
        if f == 2:
            lines = lines * kz
        for q in range(2):
            by_x = [
                jnp.concatenate(
                    [
                        lines[ty * 64 + cx * 8 : ty * 64 + cx * 8 + 8, q * 128 : q * 128 + 128]
                        for ty in range(4)
                    ],
                    axis=0,
                )
                for cx in range(8)
            ]
            for i, value in enumerate(exchange(by_x)):
                snd2[f, q, 32 * i : 32 * i + 32, :] = value
            if f != 1:
                pencil_send(3 * f // 2 + q, half(snd2.at[f], q), half(rx2.at[f], q))
        if f == 1:
            pencil_send(2, snd2.at[f], rx2.at[f])

    slope = y_slopes()

    def y_lines(f, q):
        pencil_all(3 * f // 2 + q, half(snd2.at[f], q), half(rx2.at[f], q)).wait_recv()
        return combine(dot3((y_fwd[0], y_fwd[1]), split(rx2[f, q])), -1.0)[0]

    z_lines(0)
    z_lines(1)
    z_lines(2)
    table_copies[2].wait()
    for q in range(2):
        snd3[0, q] = y_lines(0, q)
        wide_send(4 + q, half(snd3.at[0], q), half(rx3.at[0], q))
    table_copies[1].wait()
    g_inv = [dot(chosen, z_inv_t[i]).astype(bf16) for i in range(2)]
    pencil_all(2, snd2.at[1], rx2.at[1]).wait_recv()
    both = jnp.concatenate([rx2[1, 0], rx2[1, 1]], axis=1)
    for q, value in enumerate(combine(dot3((y_fwd[0], y_fwd[1]), split(both)), -1.0)):
        snd3[1, q] = slope * value
    for q in range(2):
        snd3[1, q] += y_lines(2, q)
        wide_send(6 + q, half(snd3.at[1], q), half(rx3.at[1], q))

    table_copies[3].wait()
    table_copies[4].wait()

    def x_lines(i, q):
        wide_all(4 + 2 * i + q, half(snd3.at[i], q), half(rx3.at[i], q)).wait_recv()
        parts = exchange([rx3[i, q, pl.ds(j, NW, stride=8), :] for j in range(8)])
        return jnp.concatenate(parts, axis=0)

    both = jnp.concatenate([x_lines(0, 0), x_lines(0, 1)], axis=1)
    first = dot3((x_fwd[0], x_fwd[1]), split(both))
    for q in range(2):
        second = dot3((x_fwd[0], x_fwd[1]), split(x_lines(1, q)))
        solved = solve_x(first[:, q * 128 : q * 128 + 128], second, w, p, q)
        snd4[q] = times_i(dot3((x_inv[0], x_inv[1]), split(solved)))
        wide_send(8 + q, half(snd4, q), half(rx4, q))

    table_copies[5].wait()
    for q in range(2):
        wide_all(8 + q, half(snd4, q), half(rx4, q)).wait_recv()
        parts = exchange([rx4[q, pl.ds(cx, NW, stride=8), :] for cx in range(8)])
        sums = dot3((y_inv[0], y_inv[1]), split(jnp.concatenate(parts, axis=0)))
        snd5[q] = combine(sums, 1.0)[0]
        pencil_send(5 + q, half(snd5, q), half(rx5, q))

    table_copies[6].wait()
    lines = []
    for q in range(2):
        pencil_all(5 + q, half(snd5, q), half(rx5, q)).wait_recv()
        by_x = exchange([rx5[q, 32 * i : 32 * i + 32, :] for i in range(8)])
        lines.append(
            split(
                jnp.concatenate(
                    [by_x[cx][ty * 8 : ty * 8 + 8] for ty in range(4) for cx in range(8)], axis=0
                )
            )
        )
    lines = [jnp.concatenate([lines[0][i], lines[1][i]], axis=1) for i in range(2)]
    values = dot3(g_inv, lines, ((1,), (1,)))
    snd6[...] = pick_rows(values[: NW * 8], values[NW * 8 :], ty0, ty1).reshape(NW, 8, 128)

    def send_back(i):
        other = wide_peer(w, i)
        wide_copy(10, snd6.at[other], rx6.at[w], other).start()

    loop(NW - 1, send_back, unroll=NW - 1)
    rx6[w] = snd6[w]
    mesh = dot3(lines, (z_inv[0], z_inv[1]))
    for ty in range(4):
        for cx in range(8):
            mesh_v[cx, ty * 8 : ty * 8 + 8, :] = mesh[ty * 64 + cx * 8 : ty * 64 + cx * 8 + 8]
    mesh_copy = pltpu.make_async_copy(mesh_v, mesh_ref, pick_sem)
    mesh_copy.start()
    ids_all.wait_send()
    for f in range(3):
        msg_all[f].wait_send()
    pencil_all(2, snd2.at[1], rx2.at[1]).wait_send()
    for q in range(2):
        for f in (0, 2):
            pencil_all(3 * f // 2 + q, half(snd2.at[f], q), half(rx2.at[f], q)).wait_send()
        for i in range(2):
            wide_all(4 + 2 * i + q, half(snd3.at[i], q), half(rx3.at[i], q)).wait_send()
        wide_all(8 + q, half(snd4, q), half(rx4, q)).wait_send()
        pencil_all(5 + q, half(snd5, q), half(rx5, q)).wait_send()
    wide_copy(10, snd6.at[others], rx6.at[others], (w + 1) % NW).wait()

    def read(b):
        o = owner[0, b]
        pair = rx6[o]
        here = jnp.where(pick[o, 0] == b, pair, roll(pair, 64, 1))
        tile_in = here[:, :64]
        top = tile_in.astype(bf16).astype(f32)
        out = dot(jnp.concatenate([top, tile_in - top], axis=0).astype(bf16), spread[b])
        value = jnp.sum(jnp.where(kept(b), out[:8] + out[8:], 0.0), axis=0, keepdims=True)
        mass_ref[0:1, slots(b)] = value

    loop(NB, read, unroll=16)
    mesh_copy.wait()


def hand_over(mesh_in, mass_in, mesh_out, mass_out, mesh_v, mass_v, in_sem, out_sem):
    reads = [pltpu.make_async_copy(mass_in, mass_v, in_sem.at[4])]
    writes = [pltpu.make_async_copy(mass_v, mass_out, out_sem.at[4])]
    for i in range(4):
        part = pl.ds(2 * i, 2)
        reads.append(pltpu.make_async_copy(mesh_in.at[part], mesh_v.at[part], in_sem.at[i]))
        writes.append(pltpu.make_async_copy(mesh_v.at[part], mesh_out.at[part], out_sem.at[i]))
    for copy in reads:
        copy.start()
    for read, write in zip(reads, writes):
        read.wait()
        write.start()
    for copy in writes:
        copy.wait()


def on_device(force_adjoint, paint_index, block_count, block_owner, block_tile):
    tabs = make_tables()
    names = ["z_fwd", "z_inv_t", "z_inv", "y_fwd", "y_inv", "x_fwd", "x_inv"]
    tables = [tabs[n] for n in names]
    vmem = pl.BlockSpec(memory_space=pltpu.VMEM)
    wave = pltpu.VMEM((2, NG, 128), f32)
    dma = pltpu.SemaphoreType.DMA
    mesh_grad, mass_grad = pl.pallas_call(
        step_kernel,
        out_shape=(
            jax.ShapeDtypeStruct((8, 32, NG), f32),
            jax.ShapeDtypeStruct((1, NB * BP), f32),
        ),
        in_specs=[pl.BlockSpec(memory_space=pl.ANY)] * (5 + len(names)),
        out_specs=(pl.BlockSpec(memory_space=pl.ANY), vmem),
        scratch_shapes=[
            pltpu.VMEM((3, 1, NB * BP), f32),
            pltpu.VMEM((1, NB * BP), jnp.int32),
            pltpu.SMEM((1, NB), jnp.int32),
            pltpu.SMEM((1, NB), jnp.int32),
            pltpu.SMEM((1, NB), jnp.int32),
            pltpu.VMEM((1, NB), jnp.int32),
            *[pltpu.VMEM(t.shape, bf16) for t in tables],
            pltpu.VMEM((NB, 64, BP), bf16),
            pltpu.VMEM((NB + 1, 3, 8, 128), f32),
            pltpu.VMEM((NW, 128), jnp.int32),
            pltpu.SMEM((NW, 128), jnp.int32),
            pltpu.VMEM((NW, 1, 128), jnp.int32),
            pltpu.VMEM((3, NW, 8, 128), f32),
            pltpu.VMEM((NW, 1, 128), jnp.int32),
            pltpu.VMEM((3, NW, 8, 128), f32),
            pltpu.VMEM((3, 2, NG, 128), f32),
            pltpu.VMEM((3, 2, NG, 128), f32),
            pltpu.VMEM((2, 2, NG, 128), f32),
            pltpu.VMEM((2, 2, NG, 128), f32),
            wave, wave, wave, wave,
            pltpu.VMEM((NW, 8, 128), f32),
            pltpu.VMEM((NW, 8, 128), f32),
            pltpu.VMEM((8, 32, NG), f32),
            dma((6,)), dma((7,)), dma, dma((11,)), dma((11,)), dma((7,)), dma((7,)),
        ],
        compiler_params=pltpu.CompilerParams(
            collective_id=0, has_side_effects=True, vmem_limit_bytes=60 << 20
        ),
        name="step",
    )(
        force_adjoint, paint_index, block_count, block_owner.reshape(1, NB), block_tile,
        *[jnp.asarray(t) for t in tables],
    )
    anywhere = pl.BlockSpec(memory_space=pl.ANY)
    return pl.pallas_call(
        hand_over,
        out_shape=(
            jax.ShapeDtypeStruct((8, 32, NG), f32),
            jax.ShapeDtypeStruct((1, NB * BP), f32),
        ),
        in_specs=[anywhere, anywhere],
        out_specs=(anywhere, anywhere),
        scratch_shapes=[
            pltpu.VMEM((8, 32, NG), f32), pltpu.VMEM((1, NB * BP), f32), dma((5,)), dma((5,)),
        ],
        compiler_params=pltpu.CompilerParams(vmem_limit_bytes=60 << 20),
        name="hand_over",
    )(mesh_grad, mass_grad)


def solution(mesh):
    return jax.shard_map(
        on_device,
        mesh=mesh,
        in_specs=(
            P(None, "pencil", "wide"),
            P("pencil", "wide"),
            P("pencil", "wide"),
            P("pencil", "wide", None),
            P("pencil", "wide"),
        ),
        out_specs=(P("wide", "pencil", None), P("pencil", "wide")),
        check_vma=False,
    )
```

```python
import math

import jax
import jax.numpy as jnp
import ml_dtypes
import numpy as np
from jax import lax
from jax.experimental import pallas as pl
from jax.experimental.pallas import tpu as pltpu
from jax.sharding import PartitionSpec as P

NG = 256
NW = 32
NP = 8
NB = 32
BP = 512
MESH = pl.DeviceIdType.MESH
f32 = jnp.float32
bf16 = jnp.bfloat16


def roll(x, shift, axis):
    return pltpu.roll(x, shift, axis)


def halves(table):
    table = np.asarray(table, np.float32)
    high = table.astype(ml_dtypes.bfloat16)
    low = (table - high.astype(np.float32)).astype(ml_dtypes.bfloat16)
    return np.stack([high, low])


def waves(first, second):
    phase = (np.asarray(first)[:, None] * np.asarray(second)[None, :]) % NG
    angle = phase * (2.0 * math.pi / NG)
    return np.cos(angle), np.sin(angle)


def ky_of_row():
    out = []
    for w in range(NW):
        for j in range(8):
            base = 4 * w + j % 4
            out.append(base if j < 4 else (128 if base == 0 else NG - base))
    return np.array(out)


def make_tables():
    line = np.arange(NG)
    half = np.arange(NG // 2)
    sign = np.where(line % 2 == 0, 1.0, -1.0)
    by_half = line.reshape(2, NP, 2, 8).transpose(2, 0, 1, 3).reshape(-1)
    c, s = waves(line, half)
    s = -s
    s[:, 0] = sign
    z_fwd = np.concatenate([c, s], axis=1)[:, by_half]
    c, s = waves(half, line)
    weight = np.where(half == 0, 1.0, 2.0)[:, None]
    c = c * weight
    s = -2.0 * s
    s[0] = sign
    z_inv = np.concatenate([c, s], axis=0)[by_half]
    ky = ky_of_row()
    c, s = waves(ky, line)
    y_fwd = np.concatenate([c, s], axis=0)
    kyt = ky.reshape(NW, 8).T.reshape(-1)
    c, s = waves(line, kyt)
    y_inv = np.concatenate([c, s], axis=0)
    xt = line.reshape(NW, 8).T.reshape(-1)
    c, s = waves(line, xt)
    x_fwd = np.concatenate([c, s], axis=0)
    c, s = waves(line, line)
    x_inv = np.concatenate([c, s], axis=0)
    return dict(
        z_fwd=halves(z_fwd),
        z_inv=halves(z_inv),
        z_inv_t=halves(z_inv.T),
        y_fwd=halves(y_fwd),
        y_inv=halves(y_inv),
        x_fwd=halves(x_fwd),
        x_inv=halves(x_inv),
    )


def dot(a, b, dims=((1,), (0,))):
    return lax.dot_general(a, b, (dims, ((), ())), preferred_element_type=f32)


def split(x):
    high = x.astype(bf16)
    return high, (x - high.astype(f32)).astype(bf16)


def dot3(a, b, dims=((1,), (0,))):
    if b[0].shape[1] == 128:
        high = dot(a[0], jnp.concatenate(b, axis=1))
        return high[:, :128] + (high[:, 128:] + dot(a[1], b[0]))
    return dot(a[0], b[0], dims) + (dot(a[0], b[1], dims) + dot(a[1], b[0], dims))


def iota(shape, axis):
    return lax.broadcasted_iota(jnp.int32, shape, axis)


def exchange(arrays):
    lane = iota(arrays[0].shape, 1)
    b = 1
    while b < len(arrays):
        bit = (lane // (8 * b)) & 1
        new = []
        for i in range(len(arrays)):
            mine = i // b % 2
            shift = 8 * b if mine == 0 else 128 - 8 * b
            new.append(jnp.where(bit == mine, arrays[i], roll(arrays[i ^ b], shift, 1)))
        arrays = new
        b *= 2
    return arrays


def one_hot_rows(ids):
    spot = (ids & 31) * 8 + (iota((NW * 8, 128), 0) & 7)
    lane = iota((NW * 8, 128), 1)
    both = jnp.concatenate(
        [jnp.where(spot == lane, 1.0, 0.0), jnp.where(spot == lane + 128, 1.0, 0.0)], axis=1
    )
    return both.astype(bf16)


def scatter_rows(field, ty0, ty1):
    upper = (iota((NW * 8, 128), 1) >= 64).astype(jnp.int32)
    turned = roll(field, 64, 1)
    first = jnp.where(upper == 0, field, turned)
    second = jnp.where(upper == 0, turned, field)
    rows = []
    for values, ty in ((first, ty0), (second, ty1)):
        rows.append(
            jnp.concatenate(
                [jnp.where(ty == upper, values, 0.0), jnp.where(ty == upper + 2, values, 0.0)],
                axis=1,
            )
        )
    return jnp.concatenate(rows, axis=0)


def pick_rows(v0, v1, ty0, ty1):
    lower = iota((NW * 8, 128), 1) < 64
    out = []
    for v, ty in ((v0, ty0), (v1, ty1)):
        half = jnp.where(ty >= 2, v[:, 128:], v[:, :128])
        out.append((half, roll(half, 64, 1)))
    first = jnp.where((ty0 & 1) == 1, out[0][1], out[0][0])
    second = jnp.where((ty1 & 1) == 1, out[1][0], out[1][1])
    return jnp.where(lower, first, second)


def y_slopes():
    row = iota((NG, 128), 0)
    base = (row >> 3) * 4 + (row & 3)
    return jnp.where((row & 4) == 0, base, -base).astype(f32)


def combine(sums, sign):
    out = []
    for k in range(0, sums.shape[1], 128):
        turned = roll(sums[NG:, k : k + 128], 64, 1)
        real = iota((NG, 128), 1) < 64
        out.append(sums[:NG, k : k + 128] + jnp.where(real, -sign * turned, sign * turned))
    return out


def solve_x(a, b, w, p, q):
    row = iota((NG, 128), 0)
    lane = iota((NG, 128), 1)
    signed = jnp.where(row < 128, row, row - NG)
    slope = jnp.where(row == 128, 0, signed).astype(f32)
    sign = jnp.where(lane < 64, 1.0, -1.0)
    cos_a, sin_a = sign * a[:NG], roll(a[NG:], 64, 1)
    cos_b, sin_b = sign * b[:NG], roll(b[NG:], 64, 1)
    here = sign * (slope * (cos_a + sin_a) + (cos_b + sin_b))
    j = lane // 8 & 7
    base = 4 * w + (j & 3)
    ny = jnp.where((base == 0) & (j == 4), 128, base)
    nz = 16 * p + 8 * q + (lane & 7)
    flat = signed * signed + ny * ny
    factor = (1.0 / NG**2) / jnp.maximum(flat + nz * nz, 1).astype(f32)
    if q:
        return factor * here
    there = (cos_b - sin_b) - slope * (cos_a - sin_a)
    swapped = jnp.where((lane & 32) == 0, roll(there, 96, 1), roll(there, 32, 1))
    there = jnp.where(base == 0, there, swapped)
    top = (1.0 / NG**2) / (flat + (NG // 2) ** 2).astype(f32)
    shared = nz == 0
    alpha = jnp.where(shared, 0.5 * (factor + top), factor)
    beta = jnp.where(shared, 0.5 * (top - factor), 0.0)
    return alpha * here + beta * there


def times_i(sums):
    turned = roll(sums[:NG], 64, 1)
    return jnp.where(iota((NG, 128), 1) < 64, -turned, turned) - sums[NG:]


def wide_peer(w, i):
    iz, ix = i // 4, i % 4
    dz = 4 + (iz + 1) // 2 * (1 - 2 * ((iz + 1) % 2))
    dx = 2 + (ix + 1) // 2 * (1 - 2 * ((ix + 1) % 2))
    return (w // 8 + dx) % 4 * 8 + (w + dz) % 8


def pencil_peer(p, i):
    dy = 2 + (i // 2 + 1) // 2 * (1 - 2 * ((i // 2 + 1) % 2))
    return (p // 2 + dy) % 4 * 2 + (p + i + i // 6) % 2


def loop(count, step, unroll=1):
    def body(i, carry):
        step(i)
        return carry

    lax.fori_loop(0, count, body, 0, unroll=unroll)


def half(ref, h):
    return ref.at[pl.ds(h, 1)]


def rows(ref, i, size):
    return ref.at[:, pl.ds(pl.multiple_of(i * size, 8), size), :]


def step_kernel(
    force_hbm, cells_hbm, count_hbm, owner_hbm, tile_hbm,
    z_fwd_hbm, z_inv_t_hbm, z_inv_hbm, y_fwd_hbm, y_inv_hbm, x_fwd_hbm, x_inv_hbm,
    mesh_ref, mass_ref,
    force, cells, count, owner, tile, owner_v,
    z_fwd, z_inv_t, z_inv, y_fwd, y_inv, x_fwd, x_inv,
    spread, tiles, pick_v, pick, ids, msg, ids_rx, msg_rx,
    snd2, rx2, snd3, rx3, snd4, rx4, snd5, rx5, snd6, rx6, mesh_v,
    arg_sem, table_sem, pick_sem, wide_out, wide_in, pencil_out, pencil_in,
):
    w = lax.axis_index("wide")
    p = lax.axis_index("pencil")

    arg_copies = [
        pltpu.make_async_copy(src, dst, arg_sem.at[i])
        for i, (src, dst) in enumerate(
            [
                (owner_hbm, owner_v), (owner_hbm, owner), (count_hbm, count), (tile_hbm, tile),
                (cells_hbm, cells), (force_hbm, force),
            ]
        )
    ]
    table_copies = [
        pltpu.make_async_copy(src, dst, table_sem.at[i])
        for i, (src, dst) in enumerate(
            [
                (z_fwd_hbm, z_fwd), (z_inv_t_hbm, z_inv_t), (y_fwd_hbm, y_fwd),
                (x_fwd_hbm, x_fwd), (x_inv_hbm, x_inv), (y_inv_hbm, y_inv), (z_inv_hbm, z_inv),
            ]
        )
    ]
    for copy in arg_copies:
        copy.start()
    barrier = pltpu.get_barrier_semaphore()
    loop(
        NW - 1,
        lambda i: pl.semaphore_signal(
            barrier, inc=1, device_id={"wide": wide_peer(w, i)}, device_id_type=MESH
        ),
    )
    loop(
        NP - 1,
        lambda i: pl.semaphore_signal(
            barrier, inc=1, device_id={"pencil": pencil_peer(p, i)}, device_id_type=MESH
        ),
    )
    for copy in table_copies:
        copy.start()

    def wide_copy(phase, src, dst, other):
        return pltpu.make_async_remote_copy(
            src_ref=src, dst_ref=dst, send_sem=wide_out.at[phase], recv_sem=wide_in.at[phase],
            device_id={"wide": other}, device_id_type=MESH,
        )

    def pencil_copy(phase, src, dst, other):
        return pltpu.make_async_remote_copy(
            src_ref=src, dst_ref=dst, send_sem=pencil_out.at[phase], recv_sem=pencil_in.at[phase],
            device_id={"pencil": other}, device_id_type=MESH,
        )

    def wide_send(phase, src, dst):
        def step(i):
            other = wide_peer(w, i)
            wide_copy(phase, rows(src, other, 8), rows(dst, w, 8), other).start()

        loop(NW - 1, step, unroll=NW - 1)
        here = pl.ds(pl.multiple_of(w * 8, 8), 8)
        dst[:, here, :] = src[:, here, :]

    def wide_all(phase, src, dst):
        part = pl.ds(0, (NW - 1) * 8)
        return wide_copy(phase, src.at[:, part, :], dst.at[:, part, :], (w + 1) % NW)

    def pencil_send(phase, src, dst):
        def step(i):
            other = pencil_peer(p, i)
            pencil_copy(phase, rows(src, other, 32), rows(dst, p, 32), other).start()

        loop(NP - 1, step, unroll=NP - 1)
        here = pl.ds(pl.multiple_of(p * 32, 32), 32)
        dst[:, here, :] = src[:, here, :]

    def pencil_all(phase, src, dst):
        part = pl.ds(0, (NP - 1) * 32)
        return pencil_copy(phase, src.at[:, part, :], dst.at[:, part, :], (p + 1) % NP)

    arg_copies[0].wait()
    block = iota((NW, NB), 1)
    match = owner_v[...] == iota((NW, NB), 0)
    first = jnp.min(jnp.where(match, block, NB), axis=1, keepdims=True)
    last = jnp.max(jnp.where(match, block, -1), axis=1, keepdims=True)
    second = jnp.where(last > first, last, NB)
    pick_v[...] = jnp.where(iota((NW, 128), 1) == 0, first, second)
    pick_copy = pltpu.make_async_copy(pick_v, pick, pick_sem)
    pick_copy.start()

    for copy in arg_copies[1:]:
        copy.wait()
    tiles[NB] = jnp.zeros((3, 8, 128), f32)

    def slots(b):
        return pl.ds(pl.multiple_of(b * BP, BP), BP)

    def kept(b):
        live = iota((1, BP), 1) < count[0, b]
        return (iota((8, BP), 0) == (cells[0:1, slots(b)] & 7)) & live

    def paint(b):
        key = cells[0:1, slots(b)] >> 3
        hot = jnp.where(iota((64, BP), 0) == key, 1.0, 0.0).astype(bf16)
        spread[b] = hot
        keep = kept(b)
        high, low = [], []
        for f in range(3):
            amount = force[f, 0:1, slots(b)]
            top = amount.astype(bf16).astype(f32)
            high.append(jnp.where(keep, top, 0.0))
            low.append(jnp.where(keep, amount - top, 0.0))
        out = dot(jnp.concatenate(high + low, axis=0).astype(bf16), hot, ((1,), (1,)))
        out = out[:24] + out[24:]
        tiles[b] = jnp.concatenate([out, out], axis=1).reshape(3, 8, 128)

    loop(NB, paint, unroll=16)
    pick_copy.wait()

    left = iota((8, 128), 1) < 64

    def assemble(f, o):
        msg[f, o] = jnp.where(left, tiles[pick[o, 0], f], tiles[pick[o, 1], f])

    def number(o):
        name = []
        for s in range(2):
            b = pick[o, s]
            name.append(jnp.where(b < NB, tile[0, jnp.minimum(b, NB - 1)], -1))
        ids[o] = jnp.where(iota((1, 128), 1) < 64, name[0], name[1])

    def ready(o):
        number(o)
        for f in range(3):
            assemble(f, o)

    loop(NW, ready, unroll=NW)
    pl.semaphore_wait(barrier, NW - 1 + NP - 1)

    def send_first(i):
        other = wide_peer(w, i)
        wide_copy(0, ids.at[other], ids_rx.at[w], other).start()
        wide_copy(1, msg.at[0, other], msg_rx.at[0, w], other).start()

    loop(NW - 1, send_first, unroll=NW - 1)
    for f in (1, 2):

        def send_field(i, f=f):
            other = wide_peer(w, i)
            wide_copy(1 + f, msg.at[f, other], msg_rx.at[f, w], other).start()

        loop(NW - 1, send_field, unroll=NW - 1)
    ids_rx[w] = ids[w]
    for f in range(3):
        msg_rx[f, w] = msg[f, w]
    others = pl.ds(0, NW - 1)
    ids_all = wide_copy(0, ids.at[others], ids_rx.at[others], (w + 1) % NW)
    msg_all = [
        wide_copy(1 + f, msg.at[f, others], msg_rx.at[f, others], (w + 1) % NW) for f in range(3)
    ]
    ids_all.wait_recv()
    pair = jnp.broadcast_to(ids_rx[...], (NW, 8, 128)).reshape(NW * 8, 128)
    turned = roll(pair, 64, 1)
    lower = iota((NW * 8, 128), 1) < 64
    ids0, ids1 = jnp.where(lower, pair, turned), jnp.where(lower, turned, pair)
    chosen = jnp.concatenate([one_hot_rows(ids0), one_hot_rows(ids1)], axis=0)
    table_copies[0].wait()
    g_fwd = [dot(chosen, z_fwd[i]).astype(bf16) for i in range(2)]
    ty0, ty1 = ids0 >> 5, ids1 >> 5

    lane = iota((NG, 256), 1)
    kz = ((lane // 8 & 7) * 16 + lane // 128 * 8 + (lane & 7)).astype(f32)

    def z_lines(f):
        msg_all[f].wait_recv()
        field = msg_rx[f].reshape(NW * 8, 128)
        lines = dot3(split(scatter_rows(field, ty0, ty1).T), g_fwd)
        if f == 2:
            lines = lines * kz
        for q in range(2):
            by_x = [
                jnp.concatenate(
                    [
                        lines[ty * 64 + cx * 8 : ty * 64 + cx * 8 + 8, q * 128 : q * 128 + 128]
                        for ty in range(4)
                    ],
                    axis=0,
                )
                for cx in range(8)
            ]
            for i, value in enumerate(exchange(by_x)):
                snd2[f, q, 32 * i : 32 * i + 32, :] = value
            if f != 1:
                pencil_send(3 * f // 2 + q, half(snd2.at[f], q), half(rx2.at[f], q))
        if f == 1:
            pencil_send(2, snd2.at[f], rx2.at[f])

    slope = y_slopes()

    def y_lines(f, q):
        pencil_all(3 * f // 2 + q, half(snd2.at[f], q), half(rx2.at[f], q)).wait_recv()
        return combine(dot3((y_fwd[0], y_fwd[1]), split(rx2[f, q])), -1.0)[0]

    z_lines(0)
    z_lines(1)
    z_lines(2)
    table_copies[2].wait()
    for q in range(2):
        snd3[0, q] = y_lines(0, q)
        wide_send(4 + q, half(snd3.at[0], q), half(rx3.at[0], q))
    table_copies[1].wait()
    g_inv = [dot(chosen, z_inv_t[i]).astype(bf16) for i in range(2)]
    pencil_all(2, snd2.at[1], rx2.at[1]).wait_recv()
    both = jnp.concatenate([rx2[1, 0], rx2[1, 1]], axis=1)
    for q, value in enumerate(combine(dot3((y_fwd[0], y_fwd[1]), split(both)), -1.0)):
        snd3[1, q] = slope * value
    for q in range(2):
        snd3[1, q] += y_lines(2, q)
        wide_send(6 + q, half(snd3.at[1], q), half(rx3.at[1], q))

    table_copies[3].wait()
    table_copies[4].wait()

    def x_lines(i, q):
        wide_all(4 + 2 * i + q, half(snd3.at[i], q), half(rx3.at[i], q)).wait_recv()
        parts = exchange([rx3[i, q, pl.ds(j, NW, stride=8), :] for j in range(8)])
        return jnp.concatenate(parts, axis=0)

    both = jnp.concatenate([x_lines(0, 0), x_lines(0, 1)], axis=1)
    first = dot3((x_fwd[0], x_fwd[1]), split(both))
    for q in range(2):
        second = dot3((x_fwd[0], x_fwd[1]), split(x_lines(1, q)))
        solved = solve_x(first[:, q * 128 : q * 128 + 128], second, w, p, q)
        snd4[q] = times_i(dot3((x_inv[0], x_inv[1]), split(solved)))
        wide_send(8 + q, half(snd4, q), half(rx4, q))

    table_copies[5].wait()
    for q in range(2):
        wide_all(8 + q, half(snd4, q), half(rx4, q)).wait_recv()
        parts = exchange([rx4[q, pl.ds(cx, NW, stride=8), :] for cx in range(8)])
        sums = dot3((y_inv[0], y_inv[1]), split(jnp.concatenate(parts, axis=0)))
        snd5[q] = combine(sums, 1.0)[0]
        pencil_send(5 + q, half(snd5, q), half(rx5, q))

    table_copies[6].wait()
    lines = []
    for q in range(2):
        pencil_all(5 + q, half(snd5, q), half(rx5, q)).wait_recv()
        by_x = exchange([rx5[q, 32 * i : 32 * i + 32, :] for i in range(8)])
        lines.append(
            split(
                jnp.concatenate(
                    [by_x[cx][ty * 8 : ty * 8 + 8] for ty in range(4) for cx in range(8)], axis=0
                )
            )
        )
    lines = [jnp.concatenate([lines[0][i], lines[1][i]], axis=1) for i in range(2)]
    values = dot3(g_inv, lines, ((1,), (1,)))
    snd6[...] = pick_rows(values[: NW * 8], values[NW * 8 :], ty0, ty1).reshape(NW, 8, 128)

    def send_back(i):
        other = wide_peer(w, i)
        wide_copy(10, snd6.at[other], rx6.at[w], other).start()

    loop(NW - 1, send_back, unroll=NW - 1)
    rx6[w] = snd6[w]
    mesh = dot3(lines, (z_inv[0], z_inv[1]))
    for ty in range(4):
        for cx in range(8):
            mesh_v[cx, ty * 8 : ty * 8 + 8, :] = mesh[ty * 64 + cx * 8 : ty * 64 + cx * 8 + 8]
    mesh_copy = pltpu.make_async_copy(mesh_v, mesh_ref, pick_sem)
    mesh_copy.start()
    ids_all.wait_send()
    for f in range(3):
        msg_all[f].wait_send()
    pencil_all(2, snd2.at[1], rx2.at[1]).wait_send()
    for q in range(2):
        for f in (0, 2):
            pencil_all(3 * f // 2 + q, half(snd2.at[f], q), half(rx2.at[f], q)).wait_send()
        for i in range(2):
            wide_all(4 + 2 * i + q, half(snd3.at[i], q), half(rx3.at[i], q)).wait_send()
        wide_all(8 + q, half(snd4, q), half(rx4, q)).wait_send()
        pencil_all(5 + q, half(snd5, q), half(rx5, q)).wait_send()
    wide_copy(10, snd6.at[others], rx6.at[others], (w + 1) % NW).wait()

    def read(b):
        o = owner[0, b]
        pair = rx6[o]
        here = jnp.where(pick[o, 0] == b, pair, roll(pair, 64, 1))
        tile_in = here[:, :64]
        top = tile_in.astype(bf16).astype(f32)
        out = dot(jnp.concatenate([top, tile_in - top], axis=0).astype(bf16), spread[b])
        value = jnp.sum(jnp.where(kept(b), out[:8] + out[8:], 0.0), axis=0, keepdims=True)
        mass_ref[0:1, slots(b)] = value

    loop(NB, read, unroll=16)
    mesh_copy.wait()


def hand_over(mesh_in, mass_in, mesh_out, mass_out, mesh_v, mass_v, in_sem, out_sem):
    reads = [pltpu.make_async_copy(mass_in, mass_v, in_sem.at[4])]
    writes = [pltpu.make_async_copy(mass_v, mass_out, out_sem.at[4])]
    for i in range(4):
        part = pl.ds(2 * i, 2)
        reads.append(pltpu.make_async_copy(mesh_in.at[part], mesh_v.at[part], in_sem.at[i]))
        writes.append(pltpu.make_async_copy(mesh_v.at[part], mesh_out.at[part], out_sem.at[i]))
    for copy in reads:
        copy.start()
    for read, write in zip(reads, writes):
        read.wait()
        write.start()
    for copy in writes:
        copy.wait()


def on_device(force_adjoint, paint_index, block_count, block_owner, block_tile):
    tabs = make_tables()
    names = ["z_fwd", "z_inv_t", "z_inv", "y_fwd", "y_inv", "x_fwd", "x_inv"]
    tables = [tabs[n] for n in names]
    vmem = pl.BlockSpec(memory_space=pltpu.VMEM)
    wave = pltpu.VMEM((2, NG, 128), f32)
    dma = pltpu.SemaphoreType.DMA
    mesh_grad, mass_grad = pl.pallas_call(
        step_kernel,
        out_shape=(
            jax.ShapeDtypeStruct((8, 32, NG), f32),
            jax.ShapeDtypeStruct((1, NB * BP), f32),
        ),
        in_specs=[pl.BlockSpec(memory_space=pl.ANY)] * (5 + len(names)),
        out_specs=(pl.BlockSpec(memory_space=pl.ANY), vmem),
        scratch_shapes=[
            pltpu.VMEM((3, 1, NB * BP), f32),
            pltpu.VMEM((1, NB * BP), jnp.int32),
            pltpu.SMEM((1, NB), jnp.int32),
            pltpu.SMEM((1, NB), jnp.int32),
            pltpu.SMEM((1, NB), jnp.int32),
            pltpu.VMEM((1, NB), jnp.int32),
            *[pltpu.VMEM(t.shape, bf16) for t in tables],
            pltpu.VMEM((NB, 64, BP), bf16),
            pltpu.VMEM((NB + 1, 3, 8, 128), f32),
            pltpu.VMEM((NW, 128), jnp.int32),
            pltpu.SMEM((NW, 128), jnp.int32),
            pltpu.VMEM((NW, 1, 128), jnp.int32),
            pltpu.VMEM((3, NW, 8, 128), f32),
            pltpu.VMEM((NW, 1, 128), jnp.int32),
            pltpu.VMEM((3, NW, 8, 128), f32),
            pltpu.VMEM((3, 2, NG, 128), f32),
            pltpu.VMEM((3, 2, NG, 128), f32),
            pltpu.VMEM((2, 2, NG, 128), f32),
            pltpu.VMEM((2, 2, NG, 128), f32),
            wave, wave, wave, wave,
            pltpu.VMEM((NW, 8, 128), f32),
            pltpu.VMEM((NW, 8, 128), f32),
            pltpu.VMEM((8, 32, NG), f32),
            dma((6,)), dma((7,)), dma, dma((11,)), dma((11,)), dma((7,)), dma((7,)),
        ],
        compiler_params=pltpu.CompilerParams(
            collective_id=0, has_side_effects=True, vmem_limit_bytes=60 << 20
        ),
        name="step",
    )(
        force_adjoint, paint_index, block_count, block_owner.reshape(1, NB), block_tile,
        *[jnp.asarray(t) for t in tables],
    )
    anywhere = pl.BlockSpec(memory_space=pl.ANY)
    return pl.pallas_call(
        hand_over,
        out_shape=(
            jax.ShapeDtypeStruct((8, 32, NG), f32),
            jax.ShapeDtypeStruct((1, NB * BP), f32),
        ),
        in_specs=[anywhere, anywhere],
        out_specs=(anywhere, anywhere),
        scratch_shapes=[
            pltpu.VMEM((8, 32, NG), f32), pltpu.VMEM((1, NB * BP), f32), dma((5,)), dma((5,)),
        ],
        compiler_params=pltpu.CompilerParams(vmem_limit_bytes=60 << 20),
        name="hand_over",
    )(mesh_grad, mass_grad)


def solution(mesh):
    return jax.shard_map(
        on_device,
        mesh=mesh,
        in_specs=(
            P(None, "pencil", "wide"),
            P("pencil", "wide"),
            P("pencil", "wide"),
            P("pencil", "wide", None),
            P("pencil", "wide"),
        ),
        out_specs=(P("wide", "pencil", None), P("pencil", "wide")),
        check_vma=False,
    )
```

```python
import math

import jax
import jax.numpy as jnp
import ml_dtypes
import numpy as np
from jax import lax
from jax.experimental import pallas as pl
from jax.experimental.pallas import tpu as pltpu
from jax.sharding import PartitionSpec as P

NG = 256
NW = 32
NP = 8
NB = 32
BP = 512
MESH = pl.DeviceIdType.MESH
f32 = jnp.float32
bf16 = jnp.bfloat16


def roll(x, shift, axis):
    return pltpu.roll(x, shift, axis)


def halves(table):
    table = np.asarray(table, np.float32)
    high = table.astype(ml_dtypes.bfloat16)
    low = (table - high.astype(np.float32)).astype(ml_dtypes.bfloat16)
    return np.stack([high, low])


def waves(first, second):
    phase = (np.asarray(first)[:, None] * np.asarray(second)[None, :]) % NG
    angle = phase * (2.0 * math.pi / NG)
    return np.cos(angle), np.sin(angle)


def ky_of_row():
    out = []
    for w in range(NW):
        for j in range(8):
            base = 4 * w + j % 4
            out.append(base if j < 4 else (128 if base == 0 else NG - base))
    return np.array(out)


def make_tables():
    line = np.arange(NG)
    half = np.arange(NG // 2)
    sign = np.where(line % 2 == 0, 1.0, -1.0)
    by_half = line.reshape(2, NP, 2, 8).transpose(2, 0, 1, 3).reshape(-1)
    c, s = waves(line, half)
    s = -s
    s[:, 0] = sign
    z_fwd = np.concatenate([c, s], axis=1)[:, by_half]
    c, s = waves(half, line)
    weight = np.where(half == 0, 1.0, 2.0)[:, None]
    c = c * weight
    s = -2.0 * s
    s[0] = sign
    z_inv = np.concatenate([c, s], axis=0)[by_half]
    ky = ky_of_row()
    c, s = waves(ky, line)
    y_fwd = np.concatenate([c, s], axis=0)
    kyt = ky.reshape(NW, 8).T.reshape(-1)
    c, s = waves(line, kyt)
    y_inv = np.concatenate([c, s], axis=0)
    xt = line.reshape(NW, 8).T.reshape(-1)
    c, s = waves(line, xt)
    x_fwd = np.concatenate([c, s], axis=0)
    c, s = waves(line, line)
    x_inv = np.concatenate([c, s], axis=0)
    return dict(
        z_fwd=halves(z_fwd),
        z_inv=halves(z_inv),
        z_inv_t=halves(z_inv.T),
        y_fwd=halves(y_fwd),
        y_inv=halves(y_inv),
        x_fwd=halves(x_fwd),
        x_inv=halves(x_inv),
    )


def dot(a, b, dims=((1,), (0,))):
    return lax.dot_general(a, b, (dims, ((), ())), preferred_element_type=f32)


def split(x):
    high = x.astype(bf16)
    return high, (x - high.astype(f32)).astype(bf16)


def dot3(a, b, dims=((1,), (0,))):
    if b[0].shape[1] == 128:
        high = dot(a[0], jnp.concatenate(b, axis=1))
        return high[:, :128] + (high[:, 128:] + dot(a[1], b[0]))
    return dot(a[0], b[0], dims) + (dot(a[0], b[1], dims) + dot(a[1], b[0], dims))


def iota(shape, axis):
    return lax.broadcasted_iota(jnp.int32, shape, axis)


def exchange(arrays):
    lane = iota(arrays[0].shape, 1)
    b = 1
    while b < len(arrays):
        bit = (lane // (8 * b)) & 1
        new = []
        for i in range(len(arrays)):
            mine = i // b % 2
            shift = 8 * b if mine == 0 else 128 - 8 * b
            new.append(jnp.where(bit == mine, arrays[i], roll(arrays[i ^ b], shift, 1)))
        arrays = new
        b *= 2
    return arrays


def one_hot_rows(ids):
    spot = (ids & 31) * 8 + (iota((NW * 8, 128), 0) & 7)
    lane = iota((NW * 8, 128), 1)
    both = jnp.concatenate(
        [jnp.where(spot == lane, 1.0, 0.0), jnp.where(spot == lane + 128, 1.0, 0.0)], axis=1
    )
    return both.astype(bf16)


def scatter_rows(field, ty0, ty1):
    upper = (iota((NW * 8, 128), 1) >= 64).astype(jnp.int32)
    turned = roll(field, 64, 1)
    first = jnp.where(upper == 0, field, turned)
    second = jnp.where(upper == 0, turned, field)
    rows = []
    for values, ty in ((first, ty0), (second, ty1)):
        rows.append(
            jnp.concatenate(
                [jnp.where(ty == upper, values, 0.0), jnp.where(ty == upper + 2, values, 0.0)],
                axis=1,
            )
        )
    return jnp.concatenate(rows, axis=0)


def pick_rows(v0, v1, ty0, ty1):
    lower = iota((NW * 8, 128), 1) < 64
    out = []
    for v, ty in ((v0, ty0), (v1, ty1)):
        half = jnp.where(ty >= 2, v[:, 128:], v[:, :128])
        out.append((half, roll(half, 64, 1)))
    first = jnp.where((ty0 & 1) == 1, out[0][1], out[0][0])
    second = jnp.where((ty1 & 1) == 1, out[1][0], out[1][1])
    return jnp.where(lower, first, second)


def y_slopes():
    row = iota((NG, 128), 0)
    base = (row >> 3) * 4 + (row & 3)
    return jnp.where((row & 4) == 0, base, -base).astype(f32)


def combine(sums, sign):
    out = []
    for k in range(0, sums.shape[1], 128):
        turned = roll(sums[NG:, k : k + 128], 64, 1)
        real = iota((NG, 128), 1) < 64
        out.append(sums[:NG, k : k + 128] + jnp.where(real, -sign * turned, sign * turned))
    return out


def solve_x(a, b, w, p, q):
    row = iota((NG, 128), 0)
    lane = iota((NG, 128), 1)
    signed = jnp.where(row < 128, row, row - NG)
    slope = jnp.where(row == 128, 0, signed).astype(f32)
    sign = jnp.where(lane < 64, 1.0, -1.0)
    cos_a, sin_a = sign * a[:NG], roll(a[NG:], 64, 1)
    cos_b, sin_b = sign * b[:NG], roll(b[NG:], 64, 1)
    here = sign * (slope * (cos_a + sin_a) + (cos_b + sin_b))
    j = lane // 8 & 7
    base = 4 * w + (j & 3)
    ny = jnp.where((base == 0) & (j == 4), 128, base)
    nz = 16 * p + 8 * q + (lane & 7)
    flat = signed * signed + ny * ny
    factor = (1.0 / NG**2) / jnp.maximum(flat + nz * nz, 1).astype(f32)
    if q:
        return factor * here
    there = (cos_b - sin_b) - slope * (cos_a - sin_a)
    swapped = jnp.where((lane & 32) == 0, roll(there, 96, 1), roll(there, 32, 1))
    there = jnp.where(base == 0, there, swapped)
    top = (1.0 / NG**2) / (flat + (NG // 2) ** 2).astype(f32)
    shared = nz == 0
    alpha = jnp.where(shared, 0.5 * (factor + top), factor)
    beta = jnp.where(shared, 0.5 * (top - factor), 0.0)
    return alpha * here + beta * there


def times_i(sums):
    turned = roll(sums[:NG], 64, 1)
    return jnp.where(iota((NG, 128), 1) < 64, -turned, turned) - sums[NG:]


def wide_peer(w, i):
    iz, ix = i // 4, i % 4
    dz = 4 + (iz + 1) // 2 * (1 - 2 * ((iz + 1) % 2))
    dx = 2 + (ix + 1) // 2 * (1 - 2 * ((ix + 1) % 2))
    return (w // 8 + dx) % 4 * 8 + (w + dz) % 8


def pencil_peer(p, i):
    dy = 2 + (i // 2 + 1) // 2 * (1 - 2 * ((i // 2 + 1) % 2))
    return (p // 2 + dy) % 4 * 2 + (p + i + i // 6) % 2


def loop(count, step, unroll=1):
    def body(i, carry):
        step(i)
        return carry

    lax.fori_loop(0, count, body, 0, unroll=unroll)


def half(ref, h):
    return ref.at[pl.ds(h, 1)]


def rows(ref, i, size):
    return ref.at[:, pl.ds(pl.multiple_of(i * size, 8), size), :]


def step_kernel(
    force_hbm, cells_hbm, count_hbm, owner_hbm, tile_hbm,
    z_fwd_hbm, z_inv_t_hbm, z_inv_hbm, y_fwd_hbm, y_inv_hbm, x_fwd_hbm, x_inv_hbm,
    mesh_ref, mass_ref,
    force, cells, count, owner, tile, owner_v,
    z_fwd, z_inv_t, z_inv, y_fwd, y_inv, x_fwd, x_inv,
    spread, tiles, pick_v, pick, ids, msg, ids_rx, msg_rx,
    snd2, rx2, snd3, rx3, snd4, rx4, snd5, rx5, snd6, rx6, mesh_v,
    arg_sem, table_sem, pick_sem, wide_out, wide_in, pencil_out, pencil_in,
):
    w = lax.axis_index("wide")
    p = lax.axis_index("pencil")

    arg_copies = [
        pltpu.make_async_copy(src, dst, arg_sem.at[i])
        for i, (src, dst) in enumerate(
            [
                (owner_hbm, owner_v), (owner_hbm, owner), (count_hbm, count), (tile_hbm, tile),
                (cells_hbm, cells), (force_hbm, force),
            ]
        )
    ]
    table_copies = [
        pltpu.make_async_copy(src, dst, table_sem.at[i])
        for i, (src, dst) in enumerate(
            [
                (z_fwd_hbm, z_fwd), (z_inv_t_hbm, z_inv_t), (y_fwd_hbm, y_fwd),
                (x_fwd_hbm, x_fwd), (x_inv_hbm, x_inv), (y_inv_hbm, y_inv), (z_inv_hbm, z_inv),
            ]
        )
    ]
    for copy in arg_copies:
        copy.start()
    barrier = pltpu.get_barrier_semaphore()
    loop(
        NW - 1,
        lambda i: pl.semaphore_signal(
            barrier, inc=1, device_id={"wide": wide_peer(w, i)}, device_id_type=MESH
        ),
        unroll=NW - 1,
    )
    loop(
        NP - 1,
        lambda i: pl.semaphore_signal(
            barrier, inc=1, device_id={"pencil": pencil_peer(p, i)}, device_id_type=MESH
        ),
        unroll=NP - 1,
    )
    for copy in table_copies:
        copy.start()

    def wide_copy(phase, src, dst, other):
        return pltpu.make_async_remote_copy(
            src_ref=src, dst_ref=dst, send_sem=wide_out.at[phase], recv_sem=wide_in.at[phase],
            device_id={"wide": other}, device_id_type=MESH,
        )

    def pencil_copy(phase, src, dst, other):
        return pltpu.make_async_remote_copy(
            src_ref=src, dst_ref=dst, send_sem=pencil_out.at[phase], recv_sem=pencil_in.at[phase],
            device_id={"pencil": other}, device_id_type=MESH,
        )

    def wide_send(phase, src, dst):
        def step(i):
            other = wide_peer(w, i)
            wide_copy(phase, rows(src, other, 8), rows(dst, w, 8), other).start()

        loop(NW - 1, step, unroll=NW - 1)
        here = pl.ds(pl.multiple_of(w * 8, 8), 8)
        dst[:, here, :] = src[:, here, :]

    def wide_all(phase, src, dst):
        part = pl.ds(0, (NW - 1) * 8)
        return wide_copy(phase, src.at[:, part, :], dst.at[:, part, :], (w + 1) % NW)

    def pencil_send(phase, src, dst):
        def step(i):
            other = pencil_peer(p, i)
            pencil_copy(phase, rows(src, other, 32), rows(dst, p, 32), other).start()

        loop(NP - 1, step, unroll=NP - 1)
        here = pl.ds(pl.multiple_of(p * 32, 32), 32)
        dst[:, here, :] = src[:, here, :]

    def pencil_all(phase, src, dst):
        part = pl.ds(0, (NP - 1) * 32)
        return pencil_copy(phase, src.at[:, part, :], dst.at[:, part, :], (p + 1) % NP)

    arg_copies[0].wait()
    block = iota((NW, NB), 1)
    match = owner_v[...] == iota((NW, NB), 0)
    first = jnp.min(jnp.where(match, block, NB), axis=1, keepdims=True)
    last = jnp.max(jnp.where(match, block, -1), axis=1, keepdims=True)
    second = jnp.where(last > first, last, NB)
    pick_v[...] = jnp.where(iota((NW, 128), 1) == 0, first, second)
    pick_copy = pltpu.make_async_copy(pick_v, pick, pick_sem)
    pick_copy.start()

    for copy in arg_copies[1:]:
        copy.wait()
    tiles[NB] = jnp.zeros((3, 8, 128), f32)

    def slots(b):
        return pl.ds(pl.multiple_of(b * BP, BP), BP)

    def kept(b):
        live = iota((1, BP), 1) < count[0, b]
        return (iota((8, BP), 0) == (cells[0:1, slots(b)] & 7)) & live

    def paint(b):
        key = cells[0:1, slots(b)] >> 3
        hot = jnp.where(iota((64, BP), 0) == key, 1.0, 0.0).astype(bf16)
        spread[b] = hot
        keep = kept(b)
        high, low = [], []
        for f in range(3):
            amount = force[f, 0:1, slots(b)]
            top = amount.astype(bf16).astype(f32)
            high.append(jnp.where(keep, top, 0.0))
            low.append(jnp.where(keep, amount - top, 0.0))
        out = dot(jnp.concatenate(high + low, axis=0).astype(bf16), hot, ((1,), (1,)))
        out = out[:24] + out[24:]
        tiles[b] = jnp.concatenate([out, out], axis=1).reshape(3, 8, 128)

    loop(NB, paint, unroll=16)
    pick_copy.wait()

    left = iota((8, 128), 1) < 64

    def assemble(f, o):
        msg[f, o] = jnp.where(left, tiles[pick[o, 0], f], tiles[pick[o, 1], f])

    def number(o):
        name = []
        for s in range(2):
            b = pick[o, s]
            name.append(jnp.where(b < NB, tile[0, jnp.minimum(b, NB - 1)], -1))
        ids[o] = jnp.where(iota((1, 128), 1) < 64, name[0], name[1])

    def ready(o):
        number(o)
        for f in range(3):
            assemble(f, o)

    loop(NW, ready, unroll=NW)
    pl.semaphore_wait(barrier, NW - 1 + NP - 1)

    def send_first(i):
        other = wide_peer(w, i)
        wide_copy(0, ids.at[other], ids_rx.at[w], other).start()
        wide_copy(1, msg.at[0, other], msg_rx.at[0, w], other).start()

    loop(NW - 1, send_first, unroll=NW - 1)
    for f in (1, 2):

        def send_field(i, f=f):
            other = wide_peer(w, i)
            wide_copy(1 + f, msg.at[f, other], msg_rx.at[f, w], other).start()

        loop(NW - 1, send_field, unroll=NW - 1)
    ids_rx[w] = ids[w]
    for f in range(3):
        msg_rx[f, w] = msg[f, w]
    others = pl.ds(0, NW - 1)
    ids_all = wide_copy(0, ids.at[others], ids_rx.at[others], (w + 1) % NW)
    msg_all = [
        wide_copy(1 + f, msg.at[f, others], msg_rx.at[f, others], (w + 1) % NW) for f in range(3)
    ]
    ids_all.wait_recv()
    pair = jnp.broadcast_to(ids_rx[...], (NW, 8, 128)).reshape(NW * 8, 128)
    turned = roll(pair, 64, 1)
    lower = iota((NW * 8, 128), 1) < 64
    ids0, ids1 = jnp.where(lower, pair, turned), jnp.where(lower, turned, pair)
    chosen = jnp.concatenate([one_hot_rows(ids0), one_hot_rows(ids1)], axis=0)
    table_copies[0].wait()
    g_fwd = [dot(chosen, z_fwd[i]).astype(bf16) for i in range(2)]
    ty0, ty1 = ids0 >> 5, ids1 >> 5

    lane = iota((NG, 256), 1)
    kz = ((lane // 8 & 7) * 16 + lane // 128 * 8 + (lane & 7)).astype(f32)

    def z_lines(f):
        msg_all[f].wait_recv()
        field = msg_rx[f].reshape(NW * 8, 128)
        lines = dot3(split(scatter_rows(field, ty0, ty1).T), g_fwd)
        if f == 2:
            lines = lines * kz
        for q in range(2):
            by_x = [
                jnp.concatenate(
                    [
                        lines[ty * 64 + cx * 8 : ty * 64 + cx * 8 + 8, q * 128 : q * 128 + 128]
                        for ty in range(4)
                    ],
                    axis=0,
                )
                for cx in range(8)
            ]
            for i, value in enumerate(exchange(by_x)):
                snd2[f, q, 32 * i : 32 * i + 32, :] = value
            if f != 1:
                pencil_send(3 * f // 2 + q, half(snd2.at[f], q), half(rx2.at[f], q))
        if f == 1:
            pencil_send(2, snd2.at[f], rx2.at[f])

    slope = y_slopes()

    def y_lines(f, q):
        pencil_all(3 * f // 2 + q, half(snd2.at[f], q), half(rx2.at[f], q)).wait_recv()
        return combine(dot3((y_fwd[0], y_fwd[1]), split(rx2[f, q])), -1.0)[0]

    z_lines(0)
    z_lines(1)
    z_lines(2)
    table_copies[2].wait()
    for q in range(2):
        snd3[0, q] = y_lines(0, q)
        wide_send(4 + q, half(snd3.at[0], q), half(rx3.at[0], q))
    pencil_all(2, snd2.at[1], rx2.at[1]).wait_recv()
    both = jnp.concatenate([rx2[1, 0], rx2[1, 1]], axis=1)
    for q, value in enumerate(combine(dot3((y_fwd[0], y_fwd[1]), split(both)), -1.0)):
        snd3[1, q] = slope * value
    for q in range(2):
        snd3[1, q] += y_lines(2, q)
        wide_send(6 + q, half(snd3.at[1], q), half(rx3.at[1], q))

    table_copies[3].wait()
    table_copies[4].wait()

    def x_lines(i, q):
        wide_all(4 + 2 * i + q, half(snd3.at[i], q), half(rx3.at[i], q)).wait_recv()
        parts = exchange([rx3[i, q, pl.ds(j, NW, stride=8), :] for j in range(8)])
        return jnp.concatenate(parts, axis=0)

    table_copies[1].wait()
    g_inv = [dot(chosen, z_inv_t[i]).astype(bf16) for i in range(2)]
    both = jnp.concatenate([x_lines(0, 0), x_lines(0, 1)], axis=1)
    first = dot3((x_fwd[0], x_fwd[1]), split(both))
    for q in range(2):
        second = dot3((x_fwd[0], x_fwd[1]), split(x_lines(1, q)))
        solved = solve_x(first[:, q * 128 : q * 128 + 128], second, w, p, q)
        snd4[q] = times_i(dot3((x_inv[0], x_inv[1]), split(solved)))
        wide_send(8 + q, half(snd4, q), half(rx4, q))

    table_copies[5].wait()
    for q in range(2):
        wide_all(8 + q, half(snd4, q), half(rx4, q)).wait_recv()
        parts = exchange([rx4[q, pl.ds(cx, NW, stride=8), :] for cx in range(8)])
        sums = dot3((y_inv[0], y_inv[1]), split(jnp.concatenate(parts, axis=0)))
        snd5[q] = combine(sums, 1.0)[0]
        pencil_send(5 + q, half(snd5, q), half(rx5, q))

    table_copies[6].wait()
    lines = []
    for q in range(2):
        pencil_all(5 + q, half(snd5, q), half(rx5, q)).wait_recv()
        by_x = exchange([rx5[q, 32 * i : 32 * i + 32, :] for i in range(8)])
        lines.append(
            split(
                jnp.concatenate(
                    [by_x[cx][ty * 8 : ty * 8 + 8] for ty in range(4) for cx in range(8)], axis=0
                )
            )
        )
    lines = [jnp.concatenate([lines[0][i], lines[1][i]], axis=1) for i in range(2)]
    values = dot3(g_inv, lines, ((1,), (1,)))
    snd6[...] = pick_rows(values[: NW * 8], values[NW * 8 :], ty0, ty1).reshape(NW, 8, 128)

    def send_back(i):
        other = wide_peer(w, i)
        wide_copy(10, snd6.at[other], rx6.at[w], other).start()

    loop(NW - 1, send_back, unroll=NW - 1)
    rx6[w] = snd6[w]
    mesh = dot3(lines, (z_inv[0], z_inv[1]))
    for ty in range(4):
        for cx in range(8):
            mesh_v[cx, ty * 8 : ty * 8 + 8, :] = mesh[ty * 64 + cx * 8 : ty * 64 + cx * 8 + 8]
    mesh_copy = pltpu.make_async_copy(mesh_v, mesh_ref, pick_sem)
    mesh_copy.start()
    ids_all.wait_send()
    for f in range(3):
        msg_all[f].wait_send()
    pencil_all(2, snd2.at[1], rx2.at[1]).wait_send()
    for q in range(2):
        for f in (0, 2):
            pencil_all(3 * f // 2 + q, half(snd2.at[f], q), half(rx2.at[f], q)).wait_send()
        for i in range(2):
            wide_all(4 + 2 * i + q, half(snd3.at[i], q), half(rx3.at[i], q)).wait_send()
        wide_all(8 + q, half(snd4, q), half(rx4, q)).wait_send()
        pencil_all(5 + q, half(snd5, q), half(rx5, q)).wait_send()
    wide_copy(10, snd6.at[others], rx6.at[others], (w + 1) % NW).wait()

    def read(b):
        o = owner[0, b]
        pair = rx6[o]
        here = jnp.where(pick[o, 0] == b, pair, roll(pair, 64, 1))
        tile_in = here[:, :64]
        top = tile_in.astype(bf16).astype(f32)
        out = dot(jnp.concatenate([top, tile_in - top], axis=0).astype(bf16), spread[b])
        value = jnp.sum(jnp.where(kept(b), out[:8] + out[8:], 0.0), axis=0, keepdims=True)
        mass_ref[0:1, slots(b)] = value

    loop(NB, read, unroll=16)
    mesh_copy.wait()


def hand_over(mesh_in, mass_in, mesh_out, mass_out, mesh_v, mass_v, in_sem, out_sem):
    reads = [pltpu.make_async_copy(mass_in, mass_v, in_sem.at[4])]
    writes = [pltpu.make_async_copy(mass_v, mass_out, out_sem.at[4])]
    for i in range(4):
        part = pl.ds(2 * i, 2)
        reads.append(pltpu.make_async_copy(mesh_in.at[part], mesh_v.at[part], in_sem.at[i]))
        writes.append(pltpu.make_async_copy(mesh_v.at[part], mesh_out.at[part], out_sem.at[i]))
    for copy in reads:
        copy.start()
    for read, write in zip(reads, writes):
        read.wait()
        write.start()
    for copy in writes:
        copy.wait()


def on_device(force_adjoint, paint_index, block_count, block_owner, block_tile):
    tabs = make_tables()
    names = ["z_fwd", "z_inv_t", "z_inv", "y_fwd", "y_inv", "x_fwd", "x_inv"]
    tables = [tabs[n] for n in names]
    vmem = pl.BlockSpec(memory_space=pltpu.VMEM)
    wave = pltpu.VMEM((2, NG, 128), f32)
    dma = pltpu.SemaphoreType.DMA
    mesh_grad, mass_grad = pl.pallas_call(
        step_kernel,
        out_shape=(
            jax.ShapeDtypeStruct((8, 32, NG), f32),
            jax.ShapeDtypeStruct((1, NB * BP), f32),
        ),
        in_specs=[pl.BlockSpec(memory_space=pl.ANY)] * (5 + len(names)),
        out_specs=(pl.BlockSpec(memory_space=pl.ANY), vmem),
        scratch_shapes=[
            pltpu.VMEM((3, 1, NB * BP), f32),
            pltpu.VMEM((1, NB * BP), jnp.int32),
            pltpu.SMEM((1, NB), jnp.int32),
            pltpu.SMEM((1, NB), jnp.int32),
            pltpu.SMEM((1, NB), jnp.int32),
            pltpu.VMEM((1, NB), jnp.int32),
            *[pltpu.VMEM(t.shape, bf16) for t in tables],
            pltpu.VMEM((NB, 64, BP), bf16),
            pltpu.VMEM((NB + 1, 3, 8, 128), f32),
            pltpu.VMEM((NW, 128), jnp.int32),
            pltpu.SMEM((NW, 128), jnp.int32),
            pltpu.VMEM((NW, 1, 128), jnp.int32),
            pltpu.VMEM((3, NW, 8, 128), f32),
            pltpu.VMEM((NW, 1, 128), jnp.int32),
            pltpu.VMEM((3, NW, 8, 128), f32),
            pltpu.VMEM((3, 2, NG, 128), f32),
            pltpu.VMEM((3, 2, NG, 128), f32),
            pltpu.VMEM((2, 2, NG, 128), f32),
            pltpu.VMEM((2, 2, NG, 128), f32),
            wave, wave, wave, wave,
            pltpu.VMEM((NW, 8, 128), f32),
            pltpu.VMEM((NW, 8, 128), f32),
            pltpu.VMEM((8, 32, NG), f32),
            dma((6,)), dma((7,)), dma, dma((11,)), dma((11,)), dma((7,)), dma((7,)),
        ],
        compiler_params=pltpu.CompilerParams(
            collective_id=0, has_side_effects=True, vmem_limit_bytes=60 << 20
        ),
        name="step",
    )(
        force_adjoint, paint_index, block_count, block_owner.reshape(1, NB), block_tile,
        *[jnp.asarray(t) for t in tables],
    )
    anywhere = pl.BlockSpec(memory_space=pl.ANY)
    return pl.pallas_call(
        hand_over,
        out_shape=(
            jax.ShapeDtypeStruct((8, 32, NG), f32),
            jax.ShapeDtypeStruct((1, NB * BP), f32),
        ),
        in_specs=[anywhere, anywhere],
        out_specs=(anywhere, anywhere),
        scratch_shapes=[
            pltpu.VMEM((8, 32, NG), f32), pltpu.VMEM((1, NB * BP), f32), dma((5,)), dma((5,)),
        ],
        compiler_params=pltpu.CompilerParams(vmem_limit_bytes=60 << 20),
        name="hand_over",
    )(mesh_grad, mass_grad)


def solution(mesh):
    return jax.shard_map(
        on_device,
        mesh=mesh,
        in_specs=(
            P(None, "pencil", "wide"),
            P("pencil", "wide"),
            P("pencil", "wide"),
            P("pencil", "wide", None),
            P("pencil", "wide"),
        ),
        out_specs=(P("wide", "pencil", None), P("pencil", "wide")),
        check_vma=False,
    )
```
